32 devices in a mesh: dom: 16 (over z, y, x), tp: 2 (over core).
Axes of the slice: x: 2, y: 2, z: 4, core: 2. Of those that a mesh axis runs over, the one named last changes fastest.
Arguments:
- queries: bfloat16 [2, 256, 8192], P(None, 'dom', 'tp'), may hold values from -400 to 400
- new_kv: bfloat16 [2, 256, 2048], P(None, 'dom', 'tp'), may hold values from -5 to 5
- gen_cache: bfloat16 [256, 128, 2048], P('dom', None, 'tp'), may hold values from -5 to 5
- prompt_kv: bfloat16 [4096, 2048], P(None, 'tp'), may hold values from -5 to 5
- lengths: int32 [256], replicated, may hold values from 1 to 126
- ancestors: int32 [256], replicated, may hold values from 0 to 255, as said below
- tokens: int32 [2, 256], P(None, 'dom'), may hold values from 0 to 128255
- twist_vector: float32 [8192], P('tp'), may hold values from -31 to 31
- twist_bias: float32 [128256], replicated, may hold values from -5 to 5
- prior_weights: float32 [256], P('dom'), may hold values from -252 to 4
Outputs:
- twist: float32 [2, 256], P(None, 'dom')
- normalized: float32 [256], P('dom')
- resampled_cache: bfloat16 [256, 128, 2048], P('dom', None, 'tp')
- new_lengths: int32 [256], P('dom')
The draws below stay inside these ranges and needn't reach their ends.
Inputs may be any that keep to these rules, and one draw needn't show every extreme that they name: Particle p's ancestor lies on the index of dom that holds p or at most 2 indices from it; the particles of one index of dom name at most 2 distinct ancestors on any other index, and exactly 2 for some pair of indices.
All inputs are finite; a program needn't handle non-finite values.
Results may differ from the reference program's by a relative error of at most 0.0018.
Values may be sent and summed in bfloat16 or wider, within the bound.
No kernel may reach another device: no remote copies, remote signals or barrier semaphores. Data moves between devices by JAX's collectives and lax.ppermute only.
A program may use at most 128 MiB of HBM per device.

```python
import math
import jax
import jax.numpy as jnp
import numpy as np
from jax import lax

HEADS = 64
KV_HEADS = 8
HEAD_DIM = 128
VOCAB = 128256
PROMPT = 4096
GEN = 128
PART_DEV = 16
SPAN = 2
PARTICLES = 256


def drawn_pair(key):
    base_key = jax.random.fold_in(key, 7)
    key_query, key_prompt = jax.random.split(base_key)
    prompt = jnp.clip(jax.random.normal(key_prompt, (PROMPT, KV_HEADS, 2, HEAD_DIM), jnp.float32), -5.0, 5.0)
    query_draw = jnp.clip(jax.random.normal(key_query, (2, PARTICLES, HEADS, HEAD_DIM), jnp.float32), -5.0, 5.0)
    return (query_draw.reshape(2, PARTICLES, HEADS * HEAD_DIM), prompt.reshape(PROMPT, KV_HEADS * 2 * HEAD_DIM))


def draw_queries(key, part):
    return drawn_pair(key)[0].astype(jnp.bfloat16)


def draw_prompt_kv(key, part):
    return drawn_pair(key)[1].astype(jnp.bfloat16)


def draw_ancestors(key, part):
    base_key = jax.random.fold_in(key, 11)
    key_offset, key_stay, key_heavy, key_pick, key_local = jax.random.split(base_key, 5)
    dom_count = PARTICLES // PART_DEV
    positions = jnp.arange(PARTICLES, dtype=jnp.int32)
    home_dev = positions // PART_DEV
    offsets = jax.random.randint(key_offset, (PARTICLES,), -SPAN, SPAN + 1)
    stay_home = jax.random.randint(key_stay, (PARTICLES,), 0, 3) == 0
    offsets = jnp.where(stay_home, 0, offsets)
    last_first = (dom_count - 1) * PART_DEV
    offsets = offsets.at[0].set(SPAN).at[1].set(SPAN).at[last_first].set(-SPAN).at[last_first + 1].set(-SPAN)
    source_dev = jnp.clip(home_dev + offsets, 0, dom_count - 1)
    heavy_scores = jax.random.randint(key_heavy, (dom_count, PART_DEV), 0, 1 << 20) * PART_DEV + jnp.arange(PART_DEV, dtype=jnp.int32)[None, :]
    heavy_slots = jnp.argsort(heavy_scores, axis=1)[:, :2].astype(jnp.int32)
    heavy_pick = jax.random.randint(key_pick, (PARTICLES,), 0, 2)
    heavy_pick = heavy_pick.at[0].set(0).at[1].set(1).at[last_first].set(0).at[last_first + 1].set(1)
    local_draw = jax.random.randint(key_local, (PARTICLES,), 0, PART_DEV)
    remote_local = heavy_slots[source_dev, heavy_pick]
    local_index = jnp.where(source_dev == home_dev, local_draw, remote_local)
    return (source_dev * PART_DEV + local_index).astype(jnp.int32)


def draw_twist_vector(key, part):
    head_ids = (jnp.arange(HEADS * HEAD_DIM) // HEAD_DIM).astype(jnp.float32)
    base_draw = jnp.clip(jax.random.normal(jax.random.fold_in(key, 17), (HEADS * HEAD_DIM,), jnp.float32), -4.0, 4.0)
    head_ramp = 1.0 + 2.0 * head_ids / (HEADS - 1)
    return base_draw * head_ramp


def draw_prior_weights(key, part):
    positions = jnp.arange(PARTICLES).astype(jnp.float32)
    noise = jax.random.uniform(jax.random.fold_in(key, 23), (PARTICLES,), jnp.float32, -1.0, 1.0)
    return jnp.log(1.0 + 2.0 * positions / (PARTICLES - 1)) + noise


def set_ends(array, key, least, top_value):
    extent = array.shape
    place = [jax.random.randint(jax.random.fold_in(key, axis), (), 0, extent[axis]) for axis in range(len(extent))]
    array = array.at[tuple(place)].set(least)
    longest = extent.index(max(extent))
    place[longest] = (place[longest] + 1) % extent[longest]
    return array.at[tuple(place)].set(top_value)


def levels(rng, extent, cuts, low, high):
    loudness, own = 1.0, jax.random.fold_in(rng, 6)
    for position, blocks in cuts:
        steps = jnp.exp(jax.random.uniform(jax.random.fold_in(own, position), (blocks,), jnp.float32, low / len(cuts), high / len(cuts)))
        loudness = loudness * jnp.repeat(steps, extent[position] // blocks).reshape([-1 if axis == position else 1 for axis in range(len(extent))])
    return loudness


def wide_ids(own_key, extent, amount, skew):
    loads = [min(1 << octave, amount + 1 - (1 << octave)) * (1 << 20) // math.isqrt((1 << octave) ** skew) + 1 for octave in range((amount + 1).bit_length()) if 1 << octave <= amount]
    deviation = 1 + sum(loads) // (1 << 30)
    grid = np.cumsum(np.array([max(1, weight // deviation) for weight in loads]))
    pick = jax.random.randint(jax.random.fold_in(own_key, 1), extent, 0, int(grid[len(loads) - 1]))
    start = jnp.left_shift(1, jnp.searchsorted(jnp.asarray(grid, jnp.int32), pick, side="right").astype(jnp.int32))
    standing = start - 1 + jax.random.randint(jax.random.fold_in(own_key, 4), extent, 0, 1 << 30) % jnp.minimum(start, amount + 1 - start)
    return jax.random.permutation(jax.random.fold_in(own_key, 2), amount)[standing].astype(jnp.int32)


def scatter_about(key, extent, deviation, limit, cuts=(), held_as=jnp.bfloat16):
    drawn = deviation * jax.random.normal(key, extent, jnp.float32)
    if cuts:
        drawn = drawn * levels(key, extent, cuts, -0.22, 0.18)
    return jnp.clip(drawn, -limit, limit).astype(held_as)


def setup_inputs(seed: int = 0) -> dict:
    key_list = jax.random.split(jax.random.key(seed), 11)
    return {
        "queries": draw_queries(jax.random.fold_in(key_list[10], 71), 0),
        "new_kv": scatter_about(key_list[1], (2, PARTICLES, KV_HEADS * 2 * HEAD_DIM), 1.0, 5.0, ((1, 16), (2, 2))),
        "gen_cache": scatter_about(key_list[2], (PARTICLES, GEN, KV_HEADS * 2 * HEAD_DIM), 1.0, 5.0, ((0, 16), (2, 2))),
        "prompt_kv": draw_prompt_kv(jax.random.fold_in(key_list[10], 71), 0),
        "lengths": set_ends(jax.random.randint(key_list[4], (PARTICLES,), 1, GEN - 1), jax.random.fold_in(key_list[4], 1), 1, (GEN - 1) - 1).astype(jnp.int32),
        "ancestors": draw_ancestors(jax.random.fold_in(key_list[10], 71), 0),
        "tokens": set_ends(wide_ids(key_list[6], (2, PARTICLES), VOCAB, 2), jax.random.fold_in(key_list[6], 3), 0, VOCAB - 1).astype(jnp.int32),
        "twist_vector": draw_twist_vector(jax.random.fold_in(key_list[10], 71), 0),
        "twist_bias": scatter_about(key_list[8], (VOCAB,), 1.0, 5.0, (), jnp.float32),
        "prior_weights": draw_prior_weights(jax.random.fold_in(key_list[10], 71), 0),
    }


NEG_FILL = -1e+30

def grow_cache(gen_cache, new_kv, own_lengths):
    slot_ids = lax.broadcasted_iota(jnp.int32, (1, gen_cache.shape[1], 1), 1)
    start_row = own_lengths[:, None, None]
    first_row = new_kv[0][:, None, :]
    second = new_kv[1][:, None, :]
    empty_rows = jnp.zeros_like(gen_cache)
    later_rows = jnp.where(slot_ids == start_row + 1, second, empty_rows)
    return jnp.where(slot_ids < start_row, gen_cache, jnp.where(slot_ids == start_row, first_row, later_rows))

def attend_block(block_queries, prompt_kv, grown, own_lengths):
    step_count, per_block, width = block_queries.shape
    kv_count = prompt_kv.shape[1] // (2 * HEAD_DIM)
    group_size = width // (kv_count * HEAD_DIM)
    query_heads = block_queries.reshape(step_count, per_block, kv_count, group_size, HEAD_DIM).astype(jnp.float32)
    prompt = prompt_kv.reshape(prompt_kv.shape[0], kv_count, 2, HEAD_DIM).astype(jnp.float32)
    cached = grown.reshape(per_block, grown.shape[1], kv_count, 2, HEAD_DIM).astype(jnp.float32)
    score_scale = 1.0 / math.sqrt(HEAD_DIM)
    prompt_scores = jnp.einsum('tpcgd,scd->tpcgs', query_heads, prompt[:, :, 0]) * score_scale
    cache_scores = jnp.einsum('tpcgd,pscd->tpcgs', query_heads, cached[:, :, :, 0]) * score_scale
    slot_ids = lax.broadcasted_iota(jnp.int32, (step_count, 1, 1, 1, grown.shape[1]), 4)
    step_ids = lax.broadcasted_iota(jnp.int32, (step_count, 1, 1, 1, 1), 0)
    visible = slot_ids <= own_lengths[None, :, None, None, None] + step_ids
    cache_scores = jnp.where(visible, cache_scores, NEG_FILL)
    row_max = jnp.maximum(lax.optimization_barrier(jnp.max(prompt_scores, axis=-1, keepdims=True)), lax.optimization_barrier(jnp.max(cache_scores, axis=-1, keepdims=True)))
    prompt_exp = jnp.exp(prompt_scores - row_max)
    cache_exp = jnp.where(visible, jnp.exp(cache_scores - row_max), 0.0)
    row_sum = lax.optimization_barrier(jnp.sum(prompt_exp, axis=-1)) + lax.optimization_barrier(jnp.sum(cache_exp, axis=-1))
    prompt_probs = prompt_exp.astype(jnp.bfloat16).astype(jnp.float32)
    cache_probs = cache_exp.astype(jnp.bfloat16).astype(jnp.float32)
    mixed = jnp.einsum('tpcgs,scd->tpcgd', prompt_probs, prompt[:, :, 1]) + jnp.einsum('tpcgs,pscd->tpcgd', cache_probs, cached[:, :, :, 1])
    return mixed / row_sum[..., None]

def reference(queries, new_kv, gen_cache, prompt_kv, lengths, ancestors, tokens, twist_vector, twist_bias, prior_weights):
    grown = grow_cache(gen_cache, new_kv, lengths)
    block_count = PARTICLES // 8
    query_blocks = jnp.transpose(queries.reshape(2, block_count, 8, queries.shape[2]), (1, 0, 2, 3))
    grown_blocks = grown.reshape(block_count, 8, GEN, grown.shape[2])
    length_blocks = lengths.reshape(block_count, 8)

    def block_twist(block_item):
        block_queries, block_grown, block_lengths = block_item
        mixed = attend_block(block_queries, prompt_kv, block_grown, block_lengths)
        head_weights = twist_vector.reshape(mixed.shape[2:])
        return lax.optimization_barrier(jnp.sum(mixed * head_weights, axis=(2, 3, 4)))
    partial_twist = lax.map(block_twist, (query_blocks, grown_blocks, length_blocks))
    twist = jnp.transpose(partial_twist, (1, 0, 2)).reshape(2, PARTICLES) + twist_bias[tokens]
    log_weight = prior_weights + twist[1] - twist[0]
    largest = jnp.max(log_weight)
    normalized = log_weight - (largest + jnp.log(jnp.sum(jnp.exp(log_weight - largest))))
    resampled_cache = grown[ancestors]
    new_lengths = lengths[ancestors] + 2
    return (twist, normalized, resampled_cache, new_lengths)
```

```python
import functools
import math

import jax
import jax.numpy as jnp
from jax import lax
from jax.experimental import pallas as pl
from jax.experimental.pallas import tpu as pltpu
from jax.sharding import PartitionSpec as P

HEAD_DIM = 128
SPAN = 2
PICKS = 2
NEG_FILL = -1e30
KEY_CHUNK = 512
VMEM_BYTES = 50 * 1024 * 1024

ORDERS = ((1, -2, 2, -1), (2, -1, 1, -2))


def with_new_rows(cache, new_rows, length, slot, per_dev):
    rows = cache.shape[0]
    row_ids = lax.broadcasted_iota(jnp.int32, (rows, 2 * per_dev), 0)
    col_ids = lax.broadcasted_iota(jnp.int32, (rows, 2 * per_dev), 1)
    step_ids = col_ids // per_dev
    hit = jnp.logical_and(col_ids - step_ids * per_dev == slot, row_ids == length + step_ids)
    placed = jnp.dot(
        hit.astype(jnp.bfloat16), new_rows, preferred_element_type=jnp.float32
    )
    old = lax.broadcasted_iota(jnp.int32, cache.shape, 0) < length
    return jnp.where(old, cache.astype(jnp.float32), placed).astype(jnp.bfloat16)


def named_range(anc_ref, reader, owner, per_dev, doms):
    safe = jnp.clip(reader, 0, doms - 1) * per_dev
    low, high = jnp.int32(per_dev), jnp.int32(-1)
    for j in range(per_dev):
        local = anc_ref[safe + j] - owner * per_dev
        named = jnp.logical_and(local >= 0, local < per_dev)
        low = jnp.minimum(low, jnp.where(named, local, per_dev))
        high = jnp.maximum(high, jnp.where(named, local, -1))
    return low, high


def pack_kernel(
    per_dev, doms, place_ref, len_ref, anc_ref, new_ref, gen_ref, *refs
):
    sends = refs[: len(ORDERS[0])]
    new_len_ref, own_len_ref, held, in_sem, out_sem = refs[len(ORDERS[0]) :]
    me, odd = place_ref[0], place_ref[1]
    picks = []
    for even_step, odd_step in zip(*ORDERS):
        reader = me + jnp.where(odd == 1, odd_step, even_step)
        low, high = named_range(anc_ref, reader, me, per_dev, doms)
        picks += [jnp.minimum(low, per_dev - 1), jnp.maximum(high, 0)]
    loads = []
    for k, pick in enumerate(picks):
        loads.append(pltpu.make_async_copy(gen_ref.at[pick], held.at[k], in_sem.at[k]))
        loads[-1].start()
    for j in range(per_dev):
        new_len_ref[j] = len_ref[anc_ref[me * per_dev + j]] + 2
        own_len_ref[j] = len_ref[me * per_dev + j]
    new_rows = new_ref[...].reshape(2 * per_dev, new_ref.shape[-1])
    stores = []
    for k, pick in enumerate(picks):
        loads[k].wait()
        held[k] = with_new_rows(
            held[k], new_rows, len_ref[me * per_dev + pick], pick, per_dev
        )
        stores.append(
            pltpu.make_async_copy(
                held.at[k], sends[k // PICKS].at[k % PICKS], out_sem.at[k]
            )
        )
        stores[-1].start()
    for store in stores:
        store.wait()


def pack(place, lengths, ancestors, new_kv, gen_cache, doms):
    per_dev, rows, width = gen_cache.shape
    count = len(ORDERS[0])
    smem = pl.BlockSpec(memory_space=pltpu.SMEM)
    vmem = pl.BlockSpec(memory_space=pltpu.VMEM)
    hbm = pl.BlockSpec(memory_space=pl.ANY)
    block_bytes = PICKS * rows * width * 2
    return pl.pallas_call(
        functools.partial(pack_kernel, per_dev, doms),
        out_shape=[jax.ShapeDtypeStruct((PICKS, rows, width), jnp.bfloat16)] * count
        + [jax.ShapeDtypeStruct((per_dev,), jnp.int32)] * 2,
        in_specs=[smem, smem, smem, vmem, hbm],
        out_specs=[hbm] * count + [smem] * 2,
        scratch_shapes=[
            pltpu.VMEM((count * PICKS, rows, width), jnp.bfloat16),
            pltpu.SemaphoreType.DMA((count * PICKS,)),
            pltpu.SemaphoreType.DMA((count * PICKS,)),
        ],
        compiler_params=pltpu.CompilerParams(vmem_limit_bytes=VMEM_BYTES),
        cost_estimate=pl.CostEstimate(
            flops=0, bytes_accessed=2 * count * block_bytes, transcendentals=0
        ),
        name="pack_sends",
    )(place, lengths, ancestors, new_kv, gen_cache)


def tile_rows(block, count):
    return jnp.concatenate([block] * count, axis=0)


def attend_kernel(
    per_dev,
    group,
    place_ref,
    len_ref,
    anc_ref,
    q_ref,
    prompt_ref,
    gen_ref,
    new_ref,
    head_ref,
    acc_ref,
    out_ref,
    scores,
    grown,
):
    head = pl.program_id(0)
    me = place_ref[0]
    steps = q_ref.shape[0]
    rows = gen_ref.shape[1]
    keys = prompt_ref.shape[0]
    scale = 1.0 / math.sqrt(HEAD_DIM)
    base_rows = steps * per_dev
    all_rows = group * base_rows

    new_rows = new_ref[...].reshape(steps * per_dev, new_ref.shape[-1])
    for p in range(per_dev):
        grown[p] = with_new_rows(gen_ref[p], new_rows, len_ref[p], p, per_dev)
    for p in range(per_dev):
        local = jnp.clip(anc_ref[me * per_dev + p] - me * per_dev, 0, per_dev - 1)
        out_ref[p] = grown[local]

    q2 = q_ref[...].reshape(base_rows, group * HEAD_DIM)
    queries = jnp.concatenate(
        [q2[:, h * HEAD_DIM : (h + 1) * HEAD_DIM] for h in range(group)], axis=0
    )

    row_ids = lax.broadcasted_iota(jnp.int32, (base_rows, HEAD_DIM), 0)
    step_ids = row_ids // per_dev
    owner = row_ids - step_ids * per_dev
    last = step_ids
    for p in range(per_dev):
        last = last + jnp.where(owner == p, len_ref[p], 0)
    owner = tile_rows(owner, group)
    visible = tile_rows(lax.broadcasted_iota(jnp.int32, (base_rows, rows), 1) <= last, group)

    contract_last = (((1,), (1,)), ((), ()))
    own_scores = jnp.full((all_rows, rows), NEG_FILL, jnp.float32)
    for p in range(0, per_dev, 2):
        pair_keys = jnp.concatenate(
            [grown[p, :, :HEAD_DIM], grown[p + 1, :, :HEAD_DIM]], axis=0
        )
        pair = lax.dot_general(
            queries, pair_keys, contract_last, preferred_element_type=jnp.float32
        )
        own_scores = jnp.where(owner == p, pair[:, :rows], own_scores)
        own_scores = jnp.where(owner == p + 1, pair[:, rows:], own_scores)
    own_scores = jnp.where(visible, own_scores * scale, NEG_FILL)
    top = own_scores

    for first in range(0, keys, KEY_CHUNK):
        part = lax.dot_general(
            queries,
            prompt_ref[first : first + KEY_CHUNK, :HEAD_DIM],
            contract_last,
            preferred_element_type=jnp.float32,
        )
        part = part * scale
        scores[:, first : first + KEY_CHUNK] = part
        for k in range(0, KEY_CHUNK, HEAD_DIM):
            top = jnp.maximum(top, part[:, k : k + HEAD_DIM])
    row_max = jnp.broadcast_to(
        jnp.max(top, axis=1, keepdims=True), (all_rows, HEAD_DIM)
    )

    own_exp = jnp.where(visible, jnp.exp(own_scores - row_max), 0.0)
    total = own_exp
    mixed = jnp.zeros((all_rows, HEAD_DIM), jnp.float32)
    for p in range(0, per_dev, 2):
        pair_probs = jnp.concatenate(
            [jnp.where(owner == p + i, own_exp, 0.0).astype(jnp.bfloat16) for i in range(2)],
            axis=1,
        )
        pair_values = jnp.concatenate(
            [grown[p, :, HEAD_DIM:], grown[p + 1, :, HEAD_DIM:]], axis=0
        )
        mixed = mixed + jnp.dot(pair_probs, pair_values, preferred_element_type=jnp.float32)
    wide_max = jnp.concatenate([row_max] * (KEY_CHUNK // HEAD_DIM), axis=1)
    for first in range(0, keys, KEY_CHUNK):
        exps = jnp.exp(scores[:, first : first + KEY_CHUNK] - wide_max)
        for k in range(0, KEY_CHUNK, HEAD_DIM):
            total = total + exps[:, k : k + HEAD_DIM]
        mixed = mixed + jnp.dot(
            exps.astype(jnp.bfloat16),
            prompt_ref[first : first + KEY_CHUNK, HEAD_DIM:],
            preferred_element_type=jnp.float32,
        )
    mixed = mixed / jnp.sum(total, axis=1, keepdims=True)
    weighted = jnp.zeros((base_rows, HEAD_DIM), jnp.float32)
    for h in range(group):
        weighted = weighted + mixed[h * base_rows : (h + 1) * base_rows] * head_ref[0, h : h + 1, :]

    @pl.when(head == 0)
    def _():
        acc_ref[...] = weighted

    @pl.when(head > 0)
    def _():
        acc_ref[...] += weighted


def attend(place, own_lengths, ancestors, queries, prompt_kv, gen_cache, new_kv, twist_vector):
    steps, per_dev, width = queries.shape
    keys, kv_width = prompt_kv.shape
    rows = gen_cache.shape[1]
    kv_local = kv_width // (2 * HEAD_DIM)
    group = width // (kv_local * HEAD_DIM)
    head_weights = twist_vector.reshape(kv_local, group, HEAD_DIM)
    smem = pl.BlockSpec(memory_space=pltpu.SMEM)
    pair = 2 * HEAD_DIM
    all_keys = keys + rows
    total_rows = steps * per_dev * group * kv_local
    return pl.pallas_call(
        functools.partial(attend_kernel, per_dev, group),
        grid=(kv_local,),
        out_shape=[
            jax.ShapeDtypeStruct((steps * per_dev, HEAD_DIM), jnp.float32),
            jax.ShapeDtypeStruct(gen_cache.shape, jnp.bfloat16),
        ],
        in_specs=[
            smem,
            smem,
            smem,
            pl.BlockSpec((steps, per_dev, group * HEAD_DIM), lambda c: (0, 0, c)),
            pl.BlockSpec((keys, pair), lambda c: (0, c)),
            pl.BlockSpec((per_dev, rows, pair), lambda c: (0, 0, c)),
            pl.BlockSpec((steps, per_dev, pair), lambda c: (0, 0, c)),
            pl.BlockSpec((1, group, HEAD_DIM), lambda c: (c, 0, 0)),
        ],
        out_specs=[
            pl.BlockSpec((steps * per_dev, HEAD_DIM), lambda c: (0, 0)),
            pl.BlockSpec((per_dev, rows, pair), lambda c: (0, 0, c)),
        ],
        scratch_shapes=[
            pltpu.VMEM((group * steps * per_dev, keys), jnp.float32),
            pltpu.VMEM((per_dev, rows, pair), jnp.bfloat16),
        ],
        compiler_params=pltpu.CompilerParams(vmem_limit_bytes=VMEM_BYTES),
        cost_estimate=pl.CostEstimate(
            flops=4 * total_rows * all_keys * HEAD_DIM,
            bytes_accessed=2 * (prompt_kv.size + 2 * gen_cache.size),
            transcendentals=total_rows * all_keys,
        ),
        name="attend",
    )(place, own_lengths, ancestors, queries, prompt_kv, gen_cache, new_kv, head_weights)


def deliver_kernel(per_dev, doms, steps, place_ref, anc_ref, got_ref, held_ref, out_ref, sem):
    me, odd = place_ref[0], place_ref[1]
    source = me - jnp.where(odd == 1, steps[1], steps[0])
    low, _ = named_range(anc_ref, me, source, per_dev, doms)
    copies = []
    for p in range(per_dev):
        local = anc_ref[me * per_dev + p] - source * per_dev
        named = jnp.logical_and(local >= 0, local < per_dev)
        slot = jnp.where(local == low, 0, PICKS - 1)
        copy = pltpu.make_async_copy(got_ref.at[slot], out_ref.at[p], sem.at[p])
        copies.append((named, copy))
        pl.when(named)(copy.start)
    for named, copy in copies:
        pl.when(named)(copy.wait)


def deliver(place, ancestors, got, held, steps, doms):
    per_dev = held.shape[0]
    smem = pl.BlockSpec(memory_space=pltpu.SMEM)
    hbm = pl.BlockSpec(memory_space=pl.ANY)
    return pl.pallas_call(
        functools.partial(deliver_kernel, per_dev, doms, steps),
        out_shape=jax.ShapeDtypeStruct(held.shape, held.dtype),
        in_specs=[smem, smem, hbm, hbm],
        out_specs=hbm,
        input_output_aliases={3: 0},
        scratch_shapes=[pltpu.SemaphoreType.DMA((per_dev,))],
        cost_estimate=pl.CostEstimate(
            flops=0, bytes_accessed=2 * held.size // 2, transcendentals=0
        ),
        name="deliver",
    )(place, ancestors, got, held)


def routes(doms, tps, steps):
    pairs = []
    for d in range(doms):
        for t in range(tps):
            target = d + steps[t % 2]
            if 0 <= target < doms:
                pairs.append((d * tps + t, target * tps + t))
    return pairs


def local(
    queries,
    new_kv,
    gen_cache,
    prompt_kv,
    lengths,
    ancestors,
    tokens,
    twist_vector,
    twist_bias,
    prior_weights,
):
    doms, tps = lax.axis_size("dom"), lax.axis_size("tp")
    per_dev = gen_cache.shape[0]
    me, side = lax.axis_index("dom"), lax.axis_index("tp")
    place = jnp.stack([me, side % 2]).astype(jnp.int32)

    *sends, new_lengths, own_lengths = pack(place, lengths, ancestors, new_kv, gen_cache, doms)
    step_pairs = list(zip(*ORDERS))
    arrivals = [
        lax.ppermute(send, ("dom", "tp"), routes(doms, tps, steps))
        for send, steps in zip(sends, step_pairs)
    ]

    weighted, resampled = attend(
        place, own_lengths, ancestors, queries, prompt_kv, gen_cache, new_kv, twist_vector
    )
    partial_twist = jnp.sum(weighted, axis=-1).reshape(queries.shape[:2])
    bias = jnp.take(twist_bias, tokens, axis=0)
    first_side = side == 0
    shares = jnp.concatenate(
        [
            partial_twist + jnp.where(first_side, bias, 0.0),
            jnp.where(first_side, prior_weights, 0.0)[None],
        ]
    )
    gathered = jnp.sum(
        lax.all_gather(shares, ("dom", "tp")).reshape(doms, tps, 3, per_dev), axis=1
    )
    log_weights = gathered[:, 2] + gathered[:, 1] - gathered[:, 0]
    largest = jnp.max(log_weights)
    log_total = largest + jnp.log(jnp.sum(jnp.exp(log_weights - largest)))
    mine = lax.dynamic_index_in_dim(gathered, me, 0, keepdims=False)
    twist = mine[:2]
    normalized = mine[2] + mine[1] - mine[0] - log_total

    for got, steps in zip(arrivals, step_pairs):
        resampled = deliver(place, ancestors, got, resampled, steps, doms)
    return (twist, normalized, resampled, new_lengths)


def solution(mesh):
    in_specs = (
        P(None, "dom", "tp"),
        P(None, "dom", "tp"),
        P("dom", None, "tp"),
        P(None, "tp"),
        P(),
        P(),
        P(None, "dom"),
        P("tp"),
        P(),
        P("dom"),
    )
    out_specs = (P(None, "dom"), P("dom"), P("dom", None, "tp"), P("dom"))
    return jax.shard_map(local, mesh=mesh, in_specs=in_specs, out_specs=out_specs, check_vma=False)
```

```python
import functools
import math

import jax
import jax.numpy as jnp
from jax import lax
from jax.experimental import pallas as pl
from jax.experimental.pallas import tpu as pltpu
from jax.sharding import PartitionSpec as P

HEAD_DIM = 128
SPAN = 2
PICKS = 2
NEG_FILL = -1e30
KEY_CHUNK = 512
VMEM_BYTES = 50 * 1024 * 1024

ORDERS = ((-2, 2, 1, -1), (1, -1, -2, 2))


def with_new_rows(cache, new_rows, length, slot, per_dev):
    rows = cache.shape[0]
    row_ids = lax.broadcasted_iota(jnp.int32, (rows, 2 * per_dev), 0)
    col_ids = lax.broadcasted_iota(jnp.int32, (rows, 2 * per_dev), 1)
    step_ids = col_ids // per_dev
    hit = jnp.logical_and(col_ids - step_ids * per_dev == slot, row_ids == length + step_ids)
    placed = jnp.dot(
        hit.astype(jnp.bfloat16), new_rows, preferred_element_type=jnp.float32
    )
    old = lax.broadcasted_iota(jnp.int32, cache.shape, 0) < length
    return jnp.where(old, cache.astype(jnp.float32), placed).astype(jnp.bfloat16)


def named_range(anc_ref, reader, owner, per_dev, doms):
    safe = jnp.clip(reader, 0, doms - 1) * per_dev
    low, high = jnp.int32(per_dev), jnp.int32(-1)
    for j in range(per_dev):
        local = anc_ref[safe + j] - owner * per_dev
        named = jnp.logical_and(local >= 0, local < per_dev)
        low = jnp.minimum(low, jnp.where(named, local, per_dev))
        high = jnp.maximum(high, jnp.where(named, local, -1))
    return low, high


def pack_kernel(
    per_dev, doms, step_pairs, len_hbm, anc_hbm, new_ref, gen_ref, *refs
):
    sends = refs[: len(step_pairs)]
    new_len_ref, own_len_ref, len_ref, anc_ref, held, list_sem, in_sem, out_sem = refs[
        len(step_pairs) :
    ]
    lists = [
        pltpu.make_async_copy(anc_hbm, anc_ref, list_sem.at[0]),
        pltpu.make_async_copy(len_hbm, len_ref, list_sem.at[1]),
    ]
    for copy in lists:
        copy.start()
    me, odd = lax.axis_index("dom"), lax.axis_index("tp") % 2
    for copy in lists:
        copy.wait()
    picks = []
    loads = []
    for even_step, odd_step in step_pairs:
        reader = me + jnp.where(odd == 1, odd_step, even_step)
        low, high = named_range(anc_ref, reader, me, per_dev, doms)
        for pick in (jnp.minimum(low, per_dev - 1), jnp.maximum(high, 0)):
            k = len(picks)
            picks.append(pick)
            loads.append(pltpu.make_async_copy(gen_ref.at[pick], held.at[k], in_sem.at[k]))
            loads[-1].start()
    for j in range(per_dev):
        new_len_ref[j] = len_ref[anc_ref[me * per_dev + j]] + 2
        own_len_ref[j] = len_ref[me * per_dev + j]
    new_rows = new_ref[...].reshape(2 * per_dev, new_ref.shape[-1])
    stores = []
    for k, pick in enumerate(picks):
        loads[k].wait()
        held[k] = with_new_rows(
            held[k], new_rows, len_ref[me * per_dev + pick], pick, per_dev
        )
        stores.append(
            pltpu.make_async_copy(
                held.at[k], sends[k // PICKS].at[k % PICKS], out_sem.at[k]
            )
        )
        stores[-1].start()
    for store in stores:
        store.wait()


def pack(lengths, ancestors, new_kv, gen_cache, doms, step_pairs):
    per_dev, rows, width = gen_cache.shape
    count = len(step_pairs)
    smem = pl.BlockSpec(memory_space=pltpu.SMEM)
    vmem = pl.BlockSpec(memory_space=pltpu.VMEM)
    hbm = pl.BlockSpec(memory_space=pl.ANY)
    block_bytes = PICKS * rows * width * 2
    return pl.pallas_call(
        functools.partial(pack_kernel, per_dev, doms, step_pairs),
        out_shape=[jax.ShapeDtypeStruct((PICKS, rows, width), jnp.bfloat16)] * count
        + [jax.ShapeDtypeStruct((per_dev,), jnp.int32)] * 2,
        in_specs=[hbm, hbm, vmem, hbm],
        out_specs=[hbm] * count + [smem] * 2,
        scratch_shapes=[
            pltpu.SMEM(lengths.shape, jnp.int32),
            pltpu.SMEM(ancestors.shape, jnp.int32),
            pltpu.VMEM((count * PICKS, rows, width), jnp.bfloat16),
            pltpu.SemaphoreType.DMA((2,)),
            pltpu.SemaphoreType.DMA((count * PICKS,)),
            pltpu.SemaphoreType.DMA((count * PICKS,)),
        ],
        compiler_params=pltpu.CompilerParams(vmem_limit_bytes=VMEM_BYTES),
        cost_estimate=pl.CostEstimate(
            flops=0, bytes_accessed=2 * count * block_bytes, transcendentals=0
        ),
        name="pack_sends",
    )(lengths, ancestors, new_kv, gen_cache)


def tile_rows(block, count):
    return jnp.concatenate([block] * count, axis=0)


def attend_kernel(
    per_dev,
    group,
    len_ref,
    anc_ref,
    q_ref,
    prompt_ref,
    gen_ref,
    new_ref,
    head_ref,
    extra_ref,
    share_ref,
    out_ref,
    scores,
    grown,
    acc_ref,
):
    head = pl.program_id(0)
    me = lax.axis_index("dom")
    steps = q_ref.shape[0]
    rows = gen_ref.shape[1]
    keys = prompt_ref.shape[0]
    scale = 1.0 / math.sqrt(HEAD_DIM)
    base_rows = steps * per_dev
    all_rows = group * base_rows

    new_rows = new_ref[...].reshape(steps * per_dev, new_ref.shape[-1])
    for p in range(per_dev):
        grown[p] = with_new_rows(gen_ref[p], new_rows, len_ref[p], p, per_dev)
    for p in range(per_dev):
        local = jnp.clip(anc_ref[me * per_dev + p] - me * per_dev, 0, per_dev - 1)
        out_ref[p] = grown[local]

    q2 = q_ref[...].reshape(base_rows, group * HEAD_DIM)
    queries = jnp.concatenate(
        [q2[:, h * HEAD_DIM : (h + 1) * HEAD_DIM] for h in range(group)], axis=0
    )

    row_ids = lax.broadcasted_iota(jnp.int32, (base_rows, HEAD_DIM), 0)
    step_ids = row_ids // per_dev
    owner = row_ids - step_ids * per_dev
    last = step_ids
    for p in range(per_dev):
        last = last + jnp.where(owner == p, len_ref[p], 0)
    owner = tile_rows(owner, group)
    visible = tile_rows(lax.broadcasted_iota(jnp.int32, (base_rows, rows), 1) <= last, group)

    contract_last = (((1,), (1,)), ((), ()))
    own_scores = jnp.full((all_rows, rows), NEG_FILL, jnp.float32)
    for p in range(0, per_dev, 2):
        pair_keys = jnp.concatenate(
            [grown[p, :, :HEAD_DIM], grown[p + 1, :, :HEAD_DIM]], axis=0
        )
        pair = lax.dot_general(
            queries, pair_keys, contract_last, preferred_element_type=jnp.float32
        )
        own_scores = jnp.where(owner == p, pair[:, :rows], own_scores)
        own_scores = jnp.where(owner == p + 1, pair[:, rows:], own_scores)
    own_scores = jnp.where(visible, own_scores * scale, NEG_FILL)
    top = own_scores

    for first in range(0, keys, KEY_CHUNK):
        part = lax.dot_general(
            queries,
            prompt_ref[first : first + KEY_CHUNK, :HEAD_DIM],
            contract_last,
            preferred_element_type=jnp.float32,
        )
        part = part * scale
        scores[:, first : first + KEY_CHUNK] = part
        for k in range(0, KEY_CHUNK, HEAD_DIM):
            top = jnp.maximum(top, part[:, k : k + HEAD_DIM])
    row_max = jnp.broadcast_to(
        jnp.max(top, axis=1, keepdims=True), (all_rows, HEAD_DIM)
    )

    own_exp = jnp.where(visible, jnp.exp(own_scores - row_max), 0.0)
    total = own_exp
    mixed = jnp.zeros((all_rows, HEAD_DIM), jnp.float32)
    for p in range(0, per_dev, 2):
        pair_probs = jnp.concatenate(
            [jnp.where(owner == p + i, own_exp, 0.0).astype(jnp.bfloat16) for i in range(2)],
            axis=1,
        )
        pair_values = jnp.concatenate(
            [grown[p, :, HEAD_DIM:], grown[p + 1, :, HEAD_DIM:]], axis=0
        )
        mixed = mixed + jnp.dot(pair_probs, pair_values, preferred_element_type=jnp.float32)
    wide_max = jnp.concatenate([row_max] * (KEY_CHUNK // HEAD_DIM), axis=1)
    for first in range(0, keys, KEY_CHUNK):
        exps = jnp.exp(scores[:, first : first + KEY_CHUNK] - wide_max)
        for k in range(0, KEY_CHUNK, HEAD_DIM):
            total = total + exps[:, k : k + HEAD_DIM]
        mixed = mixed + jnp.dot(
            exps.astype(jnp.bfloat16),
            prompt_ref[first : first + KEY_CHUNK, HEAD_DIM:],
            preferred_element_type=jnp.float32,
        )
    mixed = mixed / jnp.sum(total, axis=1, keepdims=True)
    weighted = jnp.zeros((base_rows, HEAD_DIM), jnp.float32)
    for h in range(group):
        weighted = weighted + mixed[h * base_rows : (h + 1) * base_rows] * head_ref[0, h : h + 1, :]

    @pl.when(head == 0)
    def _():
        acc_ref[...] = weighted

    @pl.when(head > 0)
    def _():
        acc_ref[...] += weighted

    @pl.when(head == pl.num_programs(0) - 1)
    def _():
        padding = jnp.zeros((HEAD_DIM - base_rows, HEAD_DIM), jnp.float32)
        square = jnp.concatenate([acc_ref[...], padding], axis=0)
        row = jnp.sum(square.T, axis=0, keepdims=True) + extra_ref[...]
        share_ref[...] = jnp.broadcast_to(row[None], share_ref.shape)


def attend(
    own_lengths, ancestors, queries, prompt_kv, gen_cache, new_kv, twist_vector, extra, devices
):
    steps, per_dev, width = queries.shape
    keys, kv_width = prompt_kv.shape
    rows = gen_cache.shape[1]
    kv_local = kv_width // (2 * HEAD_DIM)
    group = width // (kv_local * HEAD_DIM)
    head_weights = twist_vector.reshape(kv_local, group, HEAD_DIM)
    smem = pl.BlockSpec(memory_space=pltpu.SMEM)
    pair = 2 * HEAD_DIM
    all_keys = keys + rows
    total_rows = steps * per_dev * group * kv_local
    return pl.pallas_call(
        functools.partial(attend_kernel, per_dev, group),
        grid=(kv_local,),
        out_shape=[
            jax.ShapeDtypeStruct((devices, 1, HEAD_DIM), jnp.float32),
            jax.ShapeDtypeStruct(gen_cache.shape, jnp.bfloat16),
        ],
        in_specs=[
            smem,
            smem,
            pl.BlockSpec((steps, per_dev, group * HEAD_DIM), lambda c: (0, 0, c)),
            pl.BlockSpec((keys, pair), lambda c: (0, c)),
            pl.BlockSpec((per_dev, rows, pair), lambda c: (0, 0, c)),
            pl.BlockSpec((steps, per_dev, pair), lambda c: (0, 0, c)),
            pl.BlockSpec((1, group, HEAD_DIM), lambda c: (c, 0, 0)),
            pl.BlockSpec((1, HEAD_DIM), lambda c: (0, 0)),
        ],
        out_specs=[
            pl.BlockSpec((devices, 1, HEAD_DIM), lambda c: (0, 0, 0)),
            pl.BlockSpec((per_dev, rows, pair), lambda c: (0, 0, c)),
        ],
        scratch_shapes=[
            pltpu.VMEM((group * steps * per_dev, keys), jnp.float32),
            pltpu.VMEM((per_dev, rows, pair), jnp.bfloat16),
            pltpu.VMEM((steps * per_dev, HEAD_DIM), jnp.float32),
        ],
        compiler_params=pltpu.CompilerParams(vmem_limit_bytes=VMEM_BYTES),
        cost_estimate=pl.CostEstimate(
            flops=4 * total_rows * all_keys * HEAD_DIM,
            bytes_accessed=2 * (prompt_kv.size + 2 * gen_cache.size),
            transcendentals=total_rows * all_keys,
        ),
        name="attend",
    )(own_lengths, ancestors, queries, prompt_kv, gen_cache, new_kv, head_weights, extra)


def deliver_kernel(
    per_dev, doms, steps, anc_ref, got_ref, held_ref, out_ref, block, in_sem, out_sem
):
    loads = [
        pltpu.make_async_copy(got_ref.at[k], block.at[k], in_sem.at[k]) for k in range(PICKS)
    ]
    for load in loads:
        load.start()
    me, odd = lax.axis_index("dom"), lax.axis_index("tp") % 2
    source = me - jnp.where(odd == 1, steps[1], steps[0])
    low, _ = named_range(anc_ref, me, source, per_dev, doms)
    for load in loads:
        load.wait()
    copies = []
    for p in range(per_dev):
        local = anc_ref[me * per_dev + p] - source * per_dev
        named = jnp.logical_and(local >= 0, local < per_dev)
        slot = jnp.where(local == low, 0, PICKS - 1)
        copy = pltpu.make_async_copy(block.at[slot], out_ref.at[p], out_sem.at[p])
        copies.append((named, copy))
        pl.when(named)(copy.start)
    for named, copy in copies:
        pl.when(named)(copy.wait)


def deliver(ancestors, got, held, steps, doms):
    per_dev = held.shape[0]
    smem = pl.BlockSpec(memory_space=pltpu.SMEM)
    hbm = pl.BlockSpec(memory_space=pl.ANY)
    return pl.pallas_call(
        functools.partial(deliver_kernel, per_dev, doms, steps),
        out_shape=jax.ShapeDtypeStruct(held.shape, held.dtype),
        in_specs=[smem, hbm, hbm],
        out_specs=hbm,
        input_output_aliases={2: 0},
        scratch_shapes=[
            pltpu.VMEM(got.shape, got.dtype),
            pltpu.SemaphoreType.DMA((PICKS,)),
            pltpu.SemaphoreType.DMA((per_dev,)),
        ],
        compiler_params=pltpu.CompilerParams(vmem_limit_bytes=VMEM_BYTES),
        cost_estimate=pl.CostEstimate(
            flops=0, bytes_accessed=2 * held.size // 2, transcendentals=0
        ),
        name="deliver",
    )(ancestors, got, held)


def normalize_kernel(doms, tps, per_dev, all_ref, twist_ref, normal_ref, sums):
    for d in range(doms):
        row = all_ref[d * tps]
        for t in range(1, tps):
            row = row + all_ref[d * tps + t]
        sums[d : d + 1, :] = row
    step_0, step_1, prior = (
        slice(k * per_dev, (k + 1) * per_dev) for k in range(3)
    )
    totals = sums[...]
    log_weights = totals[:, prior] + totals[:, step_1] - totals[:, step_0]
    largest = jnp.max(log_weights, keepdims=True)
    log_total = largest + jnp.log(jnp.sum(jnp.exp(log_weights - largest), keepdims=True))
    mine = sums[pl.ds(lax.axis_index("dom"), 1), :]
    own = mine[:, prior] + mine[:, step_1] - mine[:, step_0]
    twist_ref[...] = jnp.concatenate([mine[:, step_0], mine[:, step_1]], axis=0)
    normal_ref[...] = own - log_total


def normalize(shares, doms, tps, per_dev):
    return pl.pallas_call(
        functools.partial(normalize_kernel, doms, tps, per_dev),
        out_shape=[
            jax.ShapeDtypeStruct((2, per_dev), jnp.float32),
            jax.ShapeDtypeStruct((1, per_dev), jnp.float32),
        ],
        scratch_shapes=[pltpu.VMEM((doms, HEAD_DIM), jnp.float32)],
        name="normalize",
    )(shares)


def routes(doms, tps, steps):
    pairs = []
    for d in range(doms):
        for t in range(tps):
            target = d + steps[t % 2]
            if 0 <= target < doms:
                pairs.append((d * tps + t, target * tps + t))
    return pairs


def local(
    queries,
    new_kv,
    gen_cache,
    prompt_kv,
    lengths,
    ancestors,
    tokens,
    twist_vector,
    twist_bias,
    prior_weights,
):
    doms, tps = lax.axis_size("dom"), lax.axis_size("tp")
    per_dev = gen_cache.shape[0]
    step_pairs = list(zip(*ORDERS))
    everyone = ("dom", "tp")

    *first_sends, new_lengths, own_lengths = pack(
        lengths, ancestors, new_kv, gen_cache, doms, step_pairs[:1]
    )
    *later_sends, _, _ = pack(lengths, ancestors, new_kv, gen_cache, doms, step_pairs[1:])
    arrivals = [
        lax.ppermute(send, everyone, routes(doms, tps, steps))
        for send, steps in zip(first_sends + later_sends, step_pairs)
    ]

    bias = jnp.take(twist_bias, tokens, axis=0).reshape(-1)
    extra = jnp.concatenate([bias, prior_weights])
    extra = jnp.where(lax.axis_index("tp") == 0, extra, 0.0)
    extra = jnp.pad(extra, (0, HEAD_DIM - extra.size))[None]
    shares, resampled = attend(
        own_lengths,
        ancestors,
        queries,
        prompt_kv,
        gen_cache,
        new_kv,
        twist_vector,
        extra,
        doms * tps,
    )
    shares = lax.all_to_all(shares, everyone, 0, 0, tiled=True)
    twist, normalized = normalize(shares, doms, tps, per_dev)

    for got, steps in zip(arrivals, step_pairs):
        resampled = deliver(ancestors, got, resampled, steps, doms)
    return (twist, normalized.reshape(per_dev), resampled, new_lengths)


def solution(mesh):
    in_specs = (
        P(None, "dom", "tp"),
        P(None, "dom", "tp"),
        P("dom", None, "tp"),
        P(None, "tp"),
        P(),
        P(),
        P(None, "dom"),
        P("tp"),
        P(),
        P("dom"),
    )
    out_specs = (P(None, "dom"), P("dom"), P("dom", None, "tp"), P("dom"))
    return jax.shard_map(local, mesh=mesh, in_specs=in_specs, out_specs=out_specs, check_vma=False)
```

```python
import functools
import math

import jax
import jax.numpy as jnp
from jax import lax
from jax.experimental import pallas as pl
from jax.experimental.pallas import tpu as pltpu
from jax.sharding import PartitionSpec as P

HEAD_DIM = 128
SPAN = 2
PICKS = 2
NEG_FILL = -1e30
KEY_CHUNK = 512
VMEM_BYTES = 44 * 1024 * 1024
ROW_TILE = 16
WINDOW = 2 * ROW_TILE

ORDERS = ((-2, 2, 1, -1), (1, -1, -2, 2))


def in_hbm(x):
    return pltpu.with_memory_space_constraint(x, pltpu.HBM)


def place_new_rows(cache, new_rows, length, slot, per_dev):
    rows, width = cache.shape
    first = pl.multiple_of(
        jnp.minimum(length // ROW_TILE * ROW_TILE, rows - WINDOW), ROW_TILE
    )
    row_ids = first + lax.broadcasted_iota(jnp.int32, (WINDOW, width), 0)
    old = cache[pl.ds(first, WINDOW), :].astype(jnp.float32)
    later = jnp.where(row_ids == length + 1, new_rows[pl.ds(per_dev + slot, 1), :], 0.0)
    later = jnp.where(row_ids == length, new_rows[pl.ds(slot, 1), :], later)
    cache[pl.ds(first, WINDOW), :] = jnp.where(row_ids < length, old, later).astype(
        jnp.bfloat16
    )

    def clear(tile, carry):
        start = pl.multiple_of(tile * ROW_TILE, ROW_TILE)
        cache[pl.ds(start, ROW_TILE), :] = jnp.zeros((ROW_TILE, width), jnp.bfloat16)
        return carry

    lax.fori_loop(first // ROW_TILE + WINDOW // ROW_TILE, rows // ROW_TILE, clear, 0)


def named_range(anc_ref, first, owner, per_dev):
    low, high = jnp.int32(per_dev), jnp.int32(-1)
    for j in range(per_dev):
        local = anc_ref[first + j] - owner * per_dev
        named = jnp.logical_and(local >= 0, local < per_dev)
        low = jnp.minimum(low, jnp.where(named, local, per_dev))
        high = jnp.maximum(high, jnp.where(named, local, -1))
    return low, high


def pack_kernel(per_dev, doms, step_pairs, len_hbm, anc_hbm, new_hbm, gen_hbm, *refs):
    sends = refs[: len(step_pairs)]
    new_len_ref, own_len_ref, own_anc_ref = refs[len(step_pairs) : len(step_pairs) + 3]
    len_ref, anc_ref, new_bf16, new_rows, list_sem, load_sem = refs[len(step_pairs) + 3 :]
    lists = [
        pltpu.make_async_copy(anc_hbm, anc_ref, list_sem.at[0]),
        pltpu.make_async_copy(len_hbm, len_ref, list_sem.at[1]),
        pltpu.make_async_copy(new_hbm, new_bf16, list_sem.at[2]),
    ]
    for copy in lists:
        copy.start()
    me, odd = lax.axis_index("dom"), lax.axis_index("tp") % 2
    lists[0].wait()
    picks = []
    loads = []
    for k, (even_step, odd_step) in enumerate(step_pairs):
        reader = jnp.clip(me + jnp.where(odd == 1, odd_step, even_step), 0, doms - 1)
        low, high = named_range(anc_ref, reader * per_dev, me, per_dev)
        for i, pick in enumerate((jnp.minimum(low, per_dev - 1), jnp.maximum(high, 0))):
            target = sends[k].at[i]
            load = pltpu.make_async_copy(gen_hbm.at[pick], target, load_sem.at[len(loads)])
            load.start()
            picks.append((pick, target))
            loads.append(load)
    lists[1].wait()
    for j in range(per_dev):
        own_anc_ref[j] = anc_ref[me * per_dev + j]
        new_len_ref[j] = len_ref[anc_ref[me * per_dev + j]] + 2
        own_len_ref[j] = len_ref[me * per_dev + j]
    lists[2].wait()
    new_rows[...] = new_bf16[...].astype(jnp.float32).reshape(new_rows.shape)
    for load, (pick, target) in zip(loads, picks):
        load.wait()
        place_new_rows(target, new_rows, len_ref[me * per_dev + pick], pick, per_dev)


def pack(lengths, ancestors, new_kv, gen_cache, doms, step_pairs):
    per_dev, rows, width = gen_cache.shape
    count = len(step_pairs)
    smem = pl.BlockSpec(memory_space=pltpu.SMEM)
    vmem = pl.BlockSpec(memory_space=pltpu.VMEM)
    hbm = pl.BlockSpec(memory_space=pltpu.HBM)
    block_bytes = PICKS * rows * width * 2
    return pl.pallas_call(
        functools.partial(pack_kernel, per_dev, doms, step_pairs),
        out_shape=[jax.ShapeDtypeStruct((PICKS, rows, width), jnp.bfloat16)] * count
        + [jax.ShapeDtypeStruct((per_dev,), jnp.int32)] * 3,
        in_specs=[hbm] * 4,
        out_specs=[vmem] * count + [smem] * 3,
        scratch_shapes=[
            pltpu.SMEM(lengths.shape, jnp.int32),
            pltpu.SMEM(ancestors.shape, jnp.int32),
            pltpu.VMEM(new_kv.shape, jnp.bfloat16),
            pltpu.VMEM((2 * per_dev, width), jnp.float32),
            pltpu.SemaphoreType.DMA((3,)),
            pltpu.SemaphoreType.DMA((count * PICKS,)),
        ],
        compiler_params=pltpu.CompilerParams(vmem_limit_bytes=VMEM_BYTES),
        cost_estimate=pl.CostEstimate(
            flops=0, bytes_accessed=2 * count * block_bytes, transcendentals=0
        ),
        name="pack_sends",
    )(*(in_hbm(x) for x in (lengths, ancestors, new_kv, gen_cache)))


def tile_rows(block, count):
    return jnp.concatenate([block] * count, axis=0)


def attend_kernel(
    per_dev,
    group,
    len_ref,
    anc_ref,
    q_ref,
    prompt_ref,
    gen_ref,
    new_ref,
    head_ref,
    extra_ref,
    share_ref,
    out_ref,
    scores,
    grown,
    new_rows,
    acc_ref,
):
    head = pl.program_id(0)
    me = lax.axis_index("dom")
    steps = q_ref.shape[0]
    rows = gen_ref.shape[1]
    keys = prompt_ref.shape[0]
    scale = 1.0 / math.sqrt(HEAD_DIM)
    base_rows = steps * per_dev
    all_rows = group * base_rows

    new_rows[...] = new_ref[...].astype(jnp.float32).reshape(new_rows.shape)
    for p in range(per_dev):
        grown[p] = gen_ref[p]
        place_new_rows(grown.at[p], new_rows, len_ref[p], p, per_dev)
    for p in range(per_dev):
        local = jnp.clip(anc_ref[p] - me * per_dev, 0, per_dev - 1)
        out_ref[p] = grown[local]

    q2 = q_ref[...].reshape(base_rows, group * HEAD_DIM)
    queries = jnp.concatenate(
        [q2[:, h * HEAD_DIM : (h + 1) * HEAD_DIM] for h in range(group)], axis=0
    )

    row_ids = lax.broadcasted_iota(jnp.int32, (base_rows, HEAD_DIM), 0)
    step_ids = row_ids // per_dev
    owner = row_ids - step_ids * per_dev
    last = step_ids
    for p in range(per_dev):
        last = last + jnp.where(owner == p, len_ref[p], 0)
    owner = tile_rows(owner, group)
    visible = tile_rows(lax.broadcasted_iota(jnp.int32, (base_rows, rows), 1) <= last, group)

    contract_last = (((1,), (1,)), ((), ()))
    own_scores = jnp.full((all_rows, rows), NEG_FILL, jnp.float32)
    for p in range(0, per_dev, 2):
        pair_keys = jnp.concatenate(
            [grown[p, :, :HEAD_DIM], grown[p + 1, :, :HEAD_DIM]], axis=0
        )
        pair = lax.dot_general(
            queries, pair_keys, contract_last, preferred_element_type=jnp.float32
        )
        own_scores = jnp.where(owner == p, pair[:, :rows], own_scores)
        own_scores = jnp.where(owner == p + 1, pair[:, rows:], own_scores)
    own_scores = jnp.where(visible, own_scores * scale, NEG_FILL)
    top = own_scores

    for first in range(0, keys, KEY_CHUNK):
        part = lax.dot_general(
            queries,
            prompt_ref[first : first + KEY_CHUNK, :HEAD_DIM],
            contract_last,
            preferred_element_type=jnp.float32,
        )
        part = part * scale
        scores[:, first : first + KEY_CHUNK] = part
        for k in range(0, KEY_CHUNK, HEAD_DIM):
            top = jnp.maximum(top, part[:, k : k + HEAD_DIM])
    row_max = jnp.broadcast_to(
        jnp.max(top, axis=1, keepdims=True), (all_rows, HEAD_DIM)
    )

    own_exp = jnp.where(visible, jnp.exp(own_scores - row_max), 0.0)
    total = own_exp
    mixed = jnp.zeros((all_rows, HEAD_DIM), jnp.float32)
    for p in range(0, per_dev, 2):
        pair_probs = jnp.concatenate(
            [jnp.where(owner == p + i, own_exp, 0.0).astype(jnp.bfloat16) for i in range(2)],
            axis=1,
        )
        pair_values = jnp.concatenate(
            [grown[p, :, HEAD_DIM:], grown[p + 1, :, HEAD_DIM:]], axis=0
        )
        mixed = mixed + jnp.dot(pair_probs, pair_values, preferred_element_type=jnp.float32)
    wide_max = jnp.concatenate([row_max] * (KEY_CHUNK // HEAD_DIM), axis=1)
    for first in range(0, keys, KEY_CHUNK):
        exps = jnp.exp(scores[:, first : first + KEY_CHUNK] - wide_max)
        for k in range(0, KEY_CHUNK, HEAD_DIM):
            total = total + exps[:, k : k + HEAD_DIM]
        mixed = mixed + jnp.dot(
            exps.astype(jnp.bfloat16),
            prompt_ref[first : first + KEY_CHUNK, HEAD_DIM:],
            preferred_element_type=jnp.float32,
        )
    mixed = mixed / jnp.sum(total, axis=1, keepdims=True)
    weighted = jnp.zeros((base_rows, HEAD_DIM), jnp.float32)
    for h in range(group):
        weighted = weighted + mixed[h * base_rows : (h + 1) * base_rows] * head_ref[0, h : h + 1, :]

    @pl.when(head == 0)
    def _():
        acc_ref[...] = weighted

    @pl.when(head > 0)
    def _():
        acc_ref[...] += weighted

    @pl.when(head == pl.num_programs(0) - 1)
    def _():
        padding = jnp.zeros((HEAD_DIM - base_rows, HEAD_DIM), jnp.float32)
        square = jnp.concatenate([acc_ref[...], padding], axis=0)
        row = jnp.sum(square.T, axis=0, keepdims=True) + extra_ref[...]
        share_ref[...] = jnp.broadcast_to(row[None], share_ref.shape)


def attend(
    own_lengths, own_ancestors, queries, prompt_kv, gen_cache, new_kv, twist_vector, extra, devices
):
    steps, per_dev, width = queries.shape
    keys, kv_width = prompt_kv.shape
    rows = gen_cache.shape[1]
    kv_local = kv_width // (2 * HEAD_DIM)
    group = width // (kv_local * HEAD_DIM)
    head_weights = twist_vector.reshape(kv_local, group, HEAD_DIM)
    smem = pl.BlockSpec(memory_space=pltpu.SMEM)
    pair = 2 * HEAD_DIM
    all_keys = keys + rows
    total_rows = steps * per_dev * group * kv_local
    return pl.pallas_call(
        functools.partial(attend_kernel, per_dev, group),
        grid=(kv_local,),
        out_shape=[
            jax.ShapeDtypeStruct((devices, 1, HEAD_DIM), jnp.float32),
            jax.ShapeDtypeStruct(gen_cache.shape, jnp.bfloat16),
        ],
        in_specs=[
            smem,
            smem,
            pl.BlockSpec((steps, per_dev, group * HEAD_DIM), lambda c: (0, 0, c)),
            pl.BlockSpec((keys, pair), lambda c: (0, c)),
            pl.BlockSpec((per_dev, rows, pair), lambda c: (0, 0, c)),
            pl.BlockSpec((steps, per_dev, pair), lambda c: (0, 0, c)),
            pl.BlockSpec((1, group, HEAD_DIM), lambda c: (c, 0, 0)),
            pl.BlockSpec((1, HEAD_DIM), lambda c: (0, 0)),
        ],
        out_specs=[
            pl.BlockSpec((devices, 1, HEAD_DIM), lambda c: (0, 0, 0)),
            pl.BlockSpec((per_dev, rows, pair), lambda c: (0, 0, c)),
        ],
        scratch_shapes=[
            pltpu.VMEM((group * steps * per_dev, keys), jnp.float32),
            pltpu.VMEM((per_dev, rows, pair), jnp.bfloat16),
            pltpu.VMEM((steps * per_dev, pair), jnp.float32),
            pltpu.VMEM((steps * per_dev, HEAD_DIM), jnp.float32),
        ],
        compiler_params=pltpu.CompilerParams(vmem_limit_bytes=VMEM_BYTES),
        cost_estimate=pl.CostEstimate(
            flops=4 * total_rows * all_keys * HEAD_DIM,
            bytes_accessed=2 * (prompt_kv.size + 2 * gen_cache.size),
            transcendentals=total_rows * all_keys,
        ),
        name="attend",
    )(own_lengths, own_ancestors, queries, prompt_kv, gen_cache, new_kv, head_weights, extra)


def start_delivery(per_dev, step_pairs, anc_ref, gots, out_ref, sem):
    me, odd = lax.axis_index("dom"), lax.axis_index("tp") % 2
    copies = []
    for k, (got, steps) in enumerate(zip(gots, step_pairs)):
        source = me - jnp.where(odd == 1, steps[1], steps[0])
        low, _ = named_range(anc_ref, 0, source, per_dev)
        for p in range(per_dev):
            local = anc_ref[p] - source * per_dev
            named = jnp.logical_and(local >= 0, local < per_dev)
            slot = jnp.where(local == low, 0, PICKS - 1)
            copy = pltpu.make_async_copy(got.at[slot], out_ref.at[p], sem.at[k, p])
            copies.append((named, copy))
            pl.when(named)(copy.start)
    return copies


def finish_kernel(per_dev, doms, tps, step_pairs, anc_ref, *refs):
    gots = refs[: len(step_pairs)]
    _, all_ref, out_ref, twist_ref, normal_ref, sums, sem = refs[len(step_pairs) :]
    copies = start_delivery(per_dev, step_pairs, anc_ref, gots, out_ref, sem)
    for d in range(doms):
        row = all_ref[d * tps]
        for t in range(1, tps):
            row = row + all_ref[d * tps + t]
        sums[d : d + 1, :] = row
    step_0, step_1, prior = (
        slice(k * per_dev, (k + 1) * per_dev) for k in range(3)
    )
    totals = sums[...]
    log_weights = totals[:, prior] + totals[:, step_1] - totals[:, step_0]
    largest = jnp.max(log_weights, keepdims=True)
    log_total = largest + jnp.log(jnp.sum(jnp.exp(log_weights - largest), keepdims=True))
    mine = sums[pl.ds(lax.axis_index("dom"), 1), :]
    own = mine[:, prior] + mine[:, step_1] - mine[:, step_0]
    twist_ref[...] = jnp.concatenate([mine[:, step_0], mine[:, step_1]], axis=0)
    normal_ref[...] = own - log_total
    for named, copy in copies:
        pl.when(named)(copy.wait)


def finish(own_ancestors, gots, held, shares, step_pairs, doms, tps):
    per_dev = held.shape[0]
    count = len(gots)
    smem = pl.BlockSpec(memory_space=pltpu.SMEM)
    vmem = pl.BlockSpec(memory_space=pltpu.VMEM)
    hbm = pl.BlockSpec(memory_space=pl.ANY)
    return pl.pallas_call(
        functools.partial(finish_kernel, per_dev, doms, tps, step_pairs),
        out_shape=[
            jax.ShapeDtypeStruct(held.shape, held.dtype),
            jax.ShapeDtypeStruct((2, per_dev), jnp.float32),
            jax.ShapeDtypeStruct((1, per_dev), jnp.float32),
        ],
        in_specs=[smem] + [vmem] * count + [hbm, vmem],
        out_specs=[hbm, vmem, vmem],
        input_output_aliases={1 + count: 0},
        scratch_shapes=[
            pltpu.VMEM((doms, HEAD_DIM), jnp.float32),
            pltpu.SemaphoreType.DMA((count, per_dev)),
        ],
        compiler_params=pltpu.CompilerParams(vmem_limit_bytes=VMEM_BYTES),
        cost_estimate=pl.CostEstimate(
            flops=0, bytes_accessed=held.size, transcendentals=0
        ),
        name="finish",
    )(own_ancestors, *gots, held, shares)


def routes(doms, tps, steps):
    pairs = []
    for d in range(doms):
        for t in range(tps):
            target = d + steps[t % 2]
            if 0 <= target < doms:
                pairs.append((d * tps + t, target * tps + t))
    return pairs


def local(
    queries,
    new_kv,
    gen_cache,
    prompt_kv,
    lengths,
    ancestors,
    tokens,
    twist_vector,
    twist_bias,
    prior_weights,
):
    doms, tps = lax.axis_size("dom"), lax.axis_size("tp")
    per_dev = gen_cache.shape[0]
    step_pairs = list(zip(*ORDERS))
    everyone = ("dom", "tp")

    *sends, new_lengths, own_lengths, own_ancestors = pack(
        lengths, ancestors, new_kv, gen_cache, doms, step_pairs
    )
    arrivals = [
        lax.ppermute(send, everyone, routes(doms, tps, steps))
        for send, steps in zip(sends, step_pairs)
    ]

    bias = jnp.take(twist_bias, tokens, axis=0).reshape(-1)
    extra = jnp.concatenate([bias, prior_weights])
    extra = jnp.where(lax.axis_index("tp") == 0, extra, 0.0)
    extra = jnp.pad(extra, (0, HEAD_DIM - extra.size))[None]
    shares, resampled = attend(
        own_lengths,
        own_ancestors,
        queries,
        in_hbm(prompt_kv),
        in_hbm(gen_cache),
        new_kv,
        twist_vector,
        extra,
        doms * tps,
    )
    shares = lax.all_to_all(shares, everyone, 0, 0, tiled=True)
    resampled, twist, normalized = finish(
        own_ancestors, arrivals, resampled, shares, step_pairs, doms, tps
    )
    return (twist, normalized.reshape(per_dev), resampled, new_lengths)


def solution(mesh):
    in_specs = (
        P(None, "dom", "tp"),
        P(None, "dom", "tp"),
        P("dom", None, "tp"),
        P(None, "tp"),
        P(),
        P(),
        P(None, "dom"),
        P("tp"),
        P(),
        P("dom"),
    )
    out_specs = (P(None, "dom"), P("dom"), P("dom", None, "tp"), P("dom"))
    return jax.shard_map(local, mesh=mesh, in_specs=in_specs, out_specs=out_specs, check_vma=False)
```

```python
import functools
import math

import jax
import jax.numpy as jnp
from jax import lax
from jax.experimental import pallas as pl
from jax.experimental.pallas import tpu as pltpu
from jax.sharding import PartitionSpec as P

HEAD_DIM = 128
SPAN = 2
PICKS = 2
NEG_FILL = -1e30
KEY_CHUNK = 512
VMEM_BYTES = 44 * 1024 * 1024
ROW_TILE = 16
WINDOW = 2 * ROW_TILE

ORDERS = ((-2, 2, 1, -1), (1, -1, -2, 2))


def in_hbm(x):
    return pltpu.with_memory_space_constraint(x, pltpu.HBM)


def place_new_rows(cache, new_rows, length, slot, per_dev):
    rows, width = cache.shape
    first = pl.multiple_of(
        jnp.minimum(length // ROW_TILE * ROW_TILE, rows - WINDOW), ROW_TILE
    )
    row_ids = first + lax.broadcasted_iota(jnp.int32, (WINDOW, width), 0)
    old = cache[pl.ds(first, WINDOW), :].astype(jnp.float32)
    later = jnp.where(row_ids == length + 1, new_rows[pl.ds(per_dev + slot, 1), :], 0.0)
    later = jnp.where(row_ids == length, new_rows[pl.ds(slot, 1), :], later)
    cache[pl.ds(first, WINDOW), :] = jnp.where(row_ids < length, old, later).astype(
        jnp.bfloat16
    )

    def clear(tile, carry):
        start = pl.multiple_of(tile * ROW_TILE, ROW_TILE)
        cache[pl.ds(start, ROW_TILE), :] = jnp.zeros((ROW_TILE, width), jnp.bfloat16)
        return carry

    lax.fori_loop(first // ROW_TILE + WINDOW // ROW_TILE, rows // ROW_TILE, clear, 0)


def named_range(anc_ref, first, owner, per_dev):
    low, high = jnp.int32(per_dev), jnp.int32(-1)
    for j in range(per_dev):
        local = anc_ref[first + j] - owner * per_dev
        named = jnp.logical_and(local >= 0, local < per_dev)
        low = jnp.minimum(low, jnp.where(named, local, per_dev))
        high = jnp.maximum(high, jnp.where(named, local, -1))
    return low, high


def pack_kernel(per_dev, doms, step_pairs, len_hbm, anc_hbm, new_hbm, gen_hbm, *refs):
    sends = refs[: len(step_pairs)]
    new_len_ref, own_len_ref, own_anc_ref, slot_ref = refs[len(step_pairs) : len(step_pairs) + 4]
    len_ref, anc_ref, new_bf16, new_rows, list_sem, load_sem = refs[len(step_pairs) + 4 :]
    lists = [
        pltpu.make_async_copy(anc_hbm, anc_ref, list_sem.at[0]),
        pltpu.make_async_copy(len_hbm, len_ref, list_sem.at[1]),
        pltpu.make_async_copy(new_hbm, new_bf16, list_sem.at[2]),
    ]
    for copy in lists:
        copy.start()
    me, odd = lax.axis_index("dom"), lax.axis_index("tp") % 2
    lists[0].wait()
    picks = []
    loads = []
    for k, (even_step, odd_step) in enumerate(step_pairs):
        reader = jnp.clip(me + jnp.where(odd == 1, odd_step, even_step), 0, doms - 1)
        low, high = named_range(anc_ref, reader * per_dev, me, per_dev)
        for i, pick in enumerate((jnp.minimum(low, per_dev - 1), jnp.maximum(high, 0))):
            target = sends[k].at[i]
            load = pltpu.make_async_copy(gen_hbm.at[pick], target, load_sem.at[len(loads)])
            load.start()
            picks.append((pick, target))
            loads.append(load)
    lists[1].wait()
    for j in range(per_dev):
        own_anc_ref[j] = anc_ref[me * per_dev + j]
        new_len_ref[j] = len_ref[anc_ref[me * per_dev + j]] + 2
        own_len_ref[j] = len_ref[me * per_dev + j]
        slot_ref[j] = -1
    for k, (even_step, odd_step) in enumerate(step_pairs):
        source = me - jnp.where(odd == 1, odd_step, even_step)
        low, _ = named_range(anc_ref, me * per_dev, source, per_dev)
        for j in range(per_dev):
            local = anc_ref[me * per_dev + j] - source * per_dev
            named = jnp.logical_and(local >= 0, local < per_dev)
            slot = k * PICKS + jnp.where(local == low, 0, PICKS - 1)
            slot_ref[j] = jnp.where(named, slot, slot_ref[j])
    lists[2].wait()
    new_rows[...] = new_bf16[...].astype(jnp.float32).reshape(new_rows.shape)
    for load, (pick, target) in zip(loads, picks):
        load.wait()
        place_new_rows(target, new_rows, len_ref[me * per_dev + pick], pick, per_dev)


def pack(lengths, ancestors, new_kv, gen_cache, doms, step_pairs):
    per_dev, rows, width = gen_cache.shape
    count = len(step_pairs)
    smem = pl.BlockSpec(memory_space=pltpu.SMEM)
    vmem = pl.BlockSpec(memory_space=pltpu.VMEM)
    hbm = pl.BlockSpec(memory_space=pltpu.HBM)
    block_bytes = PICKS * rows * width * 2
    return pl.pallas_call(
        functools.partial(pack_kernel, per_dev, doms, step_pairs),
        out_shape=[jax.ShapeDtypeStruct((PICKS, rows, width), jnp.bfloat16)] * count
        + [jax.ShapeDtypeStruct((per_dev,), jnp.int32)] * 4,
        in_specs=[hbm] * 4,
        out_specs=[vmem] * count + [smem] * 4,
        scratch_shapes=[
            pltpu.SMEM(lengths.shape, jnp.int32),
            pltpu.SMEM(ancestors.shape, jnp.int32),
            pltpu.VMEM(new_kv.shape, jnp.bfloat16),
            pltpu.VMEM((2 * per_dev, width), jnp.float32),
            pltpu.SemaphoreType.DMA((3,)),
            pltpu.SemaphoreType.DMA((count * PICKS,)),
        ],
        compiler_params=pltpu.CompilerParams(vmem_limit_bytes=VMEM_BYTES),
        cost_estimate=pl.CostEstimate(
            flops=0, bytes_accessed=2 * count * block_bytes, transcendentals=0
        ),
        name="pack_sends",
    )(*(in_hbm(x) for x in (lengths, ancestors, new_kv, gen_cache)))


def fold_rows(block, combine):
    return combine(block.reshape(block.shape[0] // 8, 8, block.shape[1]), axis=0)


def attend_kernel(
    per_dev,
    group,
    len_ref,
    anc_ref,
    q_ref,
    prompt_ref,
    gen_ref,
    new_ref,
    head_ref,
    extra_ref,
    share_ref,
    out_ref,
    scores,
    grown,
    acc_ref,
):
    head = pl.program_id(0)
    me = lax.axis_index("dom")
    steps = q_ref.shape[0]
    rows, pair = gen_ref.shape[1:]
    keys = prompt_ref.shape[0]
    scale = 1.0 / math.sqrt(HEAD_DIM)
    base = steps * per_dev
    lanes = group * base

    new_rows = new_ref[...].astype(jnp.float32).reshape(base, pair)
    row_ids = lax.broadcasted_iota(jnp.int32, (rows, pair), 0)
    for p in range(per_dev):
        behind = row_ids - len_ref[p]
        tail = jnp.where(behind == 1, new_rows[per_dev + p : per_dev + p + 1], 0.0)
        tail = jnp.where(behind == 0, new_rows[p : p + 1], tail)
        grown[p] = jnp.where(behind < 0, gen_ref[p].astype(jnp.float32), tail).astype(
            jnp.bfloat16
        )
    for p in range(per_dev):
        local = jnp.clip(anc_ref[p] - me * per_dev, 0, per_dev - 1)
        out_ref[p] = grown[local]

    q2 = q_ref[...].reshape(base, group * HEAD_DIM)
    queries = jnp.concatenate(
        [q2[:, h * HEAD_DIM : (h + 1) * HEAD_DIM] for h in range(group)], axis=0
    )
    lane_ids = lax.broadcasted_iota(jnp.int32, (rows, lanes), 1)
    owner = lane_ids % per_dev
    last = lane_ids // per_dev % steps
    for p in range(per_dev):
        last = last + jnp.where(owner == p, len_ref[p], 0)
    visible = lax.broadcasted_iota(jnp.int32, (rows, lanes), 0) <= last

    def score(keys_block):
        return lax.dot_general(
            keys_block, queries, (((1,), (1,)), ((), ())), preferred_element_type=jnp.float32
        )

    def mix(values, probs):
        return lax.dot_general(
            values, probs, (((0,), (0,)), ((), ())), preferred_element_type=jnp.float32
        )

    own_scores = jnp.full((rows, lanes), NEG_FILL, jnp.float32)
    for p in range(per_dev):
        own_scores = jnp.where(owner == p, score(grown[p, :, :HEAD_DIM]), own_scores)
    own_scores = jnp.where(visible, own_scores * scale, NEG_FILL)
    top = fold_rows(own_scores, jnp.max)
    for first in range(0, keys, KEY_CHUNK):
        part = score(prompt_ref[first : first + KEY_CHUNK, :HEAD_DIM]) * scale
        scores[first : first + KEY_CHUNK] = part
        top = jnp.maximum(top, fold_rows(part, jnp.max))
    row_max = jnp.max(top, axis=0, keepdims=True)

    own_exp = jnp.where(visible, jnp.exp(own_scores - row_max), 0.0)
    total = fold_rows(own_exp, jnp.sum)
    mixed = jnp.zeros((HEAD_DIM, lanes), jnp.float32)
    for p in range(0, per_dev, 2):
        probs = jnp.concatenate(
            [jnp.where(owner == p + i, own_exp, 0.0).astype(jnp.bfloat16) for i in range(2)],
            axis=0,
        )
        values = jnp.concatenate([grown[p + i, :, HEAD_DIM:] for i in range(2)], axis=0)
        mixed = mixed + mix(values, probs)
    for first in range(0, keys, KEY_CHUNK):
        exps = jnp.exp(scores[first : first + KEY_CHUNK] - row_max)
        total = total + fold_rows(exps, jnp.sum)
        mixed = mixed + mix(
            prompt_ref[first : first + KEY_CHUNK, HEAD_DIM:], exps.astype(jnp.bfloat16)
        )
    mixed = (mixed / jnp.sum(total, axis=0, keepdims=True)).T
    weighted = jnp.zeros((base, HEAD_DIM), jnp.float32)
    for h in range(group):
        weighted = weighted + mixed[h * base : (h + 1) * base] * head_ref[0, h : h + 1, :]

    @pl.when(head == 0)
    def _():
        acc_ref[...] = weighted

    @pl.when(head > 0)
    def _():
        acc_ref[...] += weighted

    @pl.when(head == pl.num_programs(0) - 1)
    def _():
        padding = jnp.zeros((HEAD_DIM - base, HEAD_DIM), jnp.float32)
        square = jnp.concatenate([acc_ref[...], padding], axis=0)
        row = jnp.sum(square.T, axis=0, keepdims=True) + extra_ref[...]
        share_ref[...] = jnp.broadcast_to(row[None], share_ref.shape)


def attend(
    own_lengths, own_ancestors, queries, prompt_kv, gen_cache, new_kv, twist_vector, extra, devices
):
    steps, per_dev, width = queries.shape
    keys, kv_width = prompt_kv.shape
    rows = gen_cache.shape[1]
    kv_local = kv_width // (2 * HEAD_DIM)
    group = width // (kv_local * HEAD_DIM)
    head_weights = twist_vector.reshape(kv_local, group, HEAD_DIM)
    smem = pl.BlockSpec(memory_space=pltpu.SMEM)
    pair = 2 * HEAD_DIM
    all_keys = keys + rows
    total_rows = steps * per_dev * group * kv_local
    return pl.pallas_call(
        functools.partial(attend_kernel, per_dev, group),
        grid=(kv_local,),
        out_shape=[
            jax.ShapeDtypeStruct((devices, 1, HEAD_DIM), jnp.float32),
            jax.ShapeDtypeStruct(gen_cache.shape, jnp.bfloat16),
        ],
        in_specs=[
            smem,
            smem,
            pl.BlockSpec((steps, per_dev, group * HEAD_DIM), lambda c: (0, 0, c)),
            pl.BlockSpec((keys, pair), lambda c: (0, c)),
            pl.BlockSpec((per_dev, rows, pair), lambda c: (0, 0, c)),
            pl.BlockSpec((steps, per_dev, pair), lambda c: (0, 0, c)),
            pl.BlockSpec((1, group, HEAD_DIM), lambda c: (c, 0, 0)),
            pl.BlockSpec((1, HEAD_DIM), lambda c: (0, 0)),
        ],
        out_specs=[
            pl.BlockSpec((devices, 1, HEAD_DIM), lambda c: (0, 0, 0)),
            pl.BlockSpec((per_dev, rows, pair), lambda c: (0, 0, c)),
        ],
        scratch_shapes=[
            pltpu.VMEM((keys, group * steps * per_dev), jnp.float32),
            pltpu.VMEM((per_dev, rows, pair), jnp.bfloat16),
            pltpu.VMEM((steps * per_dev, HEAD_DIM), jnp.float32),
        ],
        compiler_params=pltpu.CompilerParams(vmem_limit_bytes=VMEM_BYTES),
        cost_estimate=pl.CostEstimate(
            flops=4 * total_rows * all_keys * HEAD_DIM,
            bytes_accessed=2 * (prompt_kv.size + 2 * gen_cache.size),
            transcendentals=total_rows * all_keys,
        ),
        name="attend",
    )(own_lengths, own_ancestors, queries, prompt_kv, gen_cache, new_kv, head_weights, extra)


def finish_kernel(doms, tps, slot_ref, *refs):
    gots = refs[: len(ORDERS[0])]
    _, all_ref, out_ref, twist_ref, normal_ref, sums, sem = refs[len(gots) :]
    per_dev = out_ref.shape[0]
    for p in range(per_dev):
        slot = slot_ref[p]
        for k, got in enumerate(gots):
            for i in range(PICKS):
                copy = pltpu.make_async_copy(got.at[i], out_ref.at[p], sem.at[p])
                pl.when(slot == k * PICKS + i)(copy.start)
    for d in range(doms):
        row = all_ref[d * tps]
        for t in range(1, tps):
            row = row + all_ref[d * tps + t]
        sums[d : d + 1, :] = row
    step_0, step_1, prior = (
        slice(k * per_dev, (k + 1) * per_dev) for k in range(3)
    )
    totals = sums[...]
    log_weights = totals[:, prior] + totals[:, step_1] - totals[:, step_0]
    largest = jnp.max(log_weights, keepdims=True)
    log_total = largest + jnp.log(jnp.sum(jnp.exp(log_weights - largest), keepdims=True))
    mine = sums[pl.ds(lax.axis_index("dom"), 1), :]
    own = mine[:, prior] + mine[:, step_1] - mine[:, step_0]
    twist_ref[...] = jnp.concatenate([mine[:, step_0], mine[:, step_1]], axis=0)
    normal_ref[...] = own - log_total
    for p in range(per_dev):
        copy = pltpu.make_async_copy(gots[0].at[0], out_ref.at[p], sem.at[p])
        pl.when(slot_ref[p] >= 0)(copy.wait)


def finish(slots, gots, held, shares, doms, tps):
    per_dev = held.shape[0]
    count = len(gots)
    smem = pl.BlockSpec(memory_space=pltpu.SMEM)
    vmem = pl.BlockSpec(memory_space=pltpu.VMEM)
    hbm = pl.BlockSpec(memory_space=pl.ANY)
    return pl.pallas_call(
        functools.partial(finish_kernel, doms, tps),
        out_shape=[
            jax.ShapeDtypeStruct(held.shape, held.dtype),
            jax.ShapeDtypeStruct((2, per_dev), jnp.float32),
            jax.ShapeDtypeStruct((1, per_dev), jnp.float32),
        ],
        in_specs=[smem] + [vmem] * count + [hbm, vmem],
        out_specs=[hbm, vmem, vmem],
        input_output_aliases={1 + count: 0},
        scratch_shapes=[
            pltpu.VMEM((doms, HEAD_DIM), jnp.float32),
            pltpu.SemaphoreType.DMA((per_dev,)),
        ],
        compiler_params=pltpu.CompilerParams(vmem_limit_bytes=VMEM_BYTES),
        cost_estimate=pl.CostEstimate(
            flops=0, bytes_accessed=held.size, transcendentals=0
        ),
        name="finish",
    )(slots, *gots, held, shares)


def routes(doms, tps, steps):
    pairs = []
    for d in range(doms):
        for t in range(tps):
            target = d + steps[t % 2]
            if 0 <= target < doms:
                pairs.append((d * tps + t, target * tps + t))
    return pairs


def local(
    queries,
    new_kv,
    gen_cache,
    prompt_kv,
    lengths,
    ancestors,
    tokens,
    twist_vector,
    twist_bias,
    prior_weights,
):
    doms, tps = lax.axis_size("dom"), lax.axis_size("tp")
    per_dev = gen_cache.shape[0]
    step_pairs = list(zip(*ORDERS))
    everyone = ("dom", "tp")

    *sends, new_lengths, own_lengths, own_ancestors, slots = pack(
        lengths, ancestors, new_kv, gen_cache, doms, step_pairs
    )
    arrivals = [
        lax.ppermute(send, everyone, routes(doms, tps, steps))
        for send, steps in zip(sends, step_pairs)
    ]

    bias = jnp.take(twist_bias, tokens, axis=0).reshape(-1)
    extra = jnp.concatenate([bias, prior_weights])
    extra = jnp.where(lax.axis_index("tp") == 0, extra, 0.0)
    extra = jnp.pad(extra, (0, HEAD_DIM - extra.size))[None]
    shares, resampled = attend(
        own_lengths,
        own_ancestors,
        queries,
        in_hbm(prompt_kv),
        in_hbm(gen_cache),
        new_kv,
        twist_vector,
        extra,
        doms * tps,
    )
    shares = lax.all_to_all(shares, everyone, 0, 0, tiled=True)
    resampled, twist, normalized = finish(slots, arrivals, resampled, shares, doms, tps)
    return (twist, normalized.reshape(per_dev), resampled, new_lengths)


def solution(mesh):
    in_specs = (
        P(None, "dom", "tp"),
        P(None, "dom", "tp"),
        P("dom", None, "tp"),
        P(None, "tp"),
        P(),
        P(),
        P(None, "dom"),
        P("tp"),
        P(),
        P("dom"),
    )
    out_specs = (P(None, "dom"), P("dom"), P("dom", None, "tp"), P("dom"))
    return jax.shard_map(local, mesh=mesh, in_specs=in_specs, out_specs=out_specs, check_vma=False)
```

```python
import functools
import math

import jax
import jax.numpy as jnp
from jax import lax
from jax.experimental import pallas as pl
from jax.experimental.pallas import tpu as pltpu
from jax.sharding import PartitionSpec as P

HEAD_DIM = 128
SPAN = 2
PICKS = 2
NEG_FILL = -1e30
KEY_CHUNK = 512
VMEM_BYTES = 44 * 1024 * 1024
ROW_TILE = 16
WINDOW = 2 * ROW_TILE

ORDERS = ((-2, 2, 1, -1), (1, -1, -2, 2))


def in_hbm(x):
    return pltpu.with_memory_space_constraint(x, pltpu.HBM)


def place_new_rows(cache, new_rows, length, slot, per_dev):
    rows, width = cache.shape
    first = pl.multiple_of(
        jnp.minimum(length // ROW_TILE * ROW_TILE, rows - WINDOW), ROW_TILE
    )
    row_ids = first + lax.broadcasted_iota(jnp.int32, (WINDOW, width), 0)
    old = cache[pl.ds(first, WINDOW), :].astype(jnp.float32)
    later = jnp.where(row_ids == length + 1, new_rows[pl.ds(per_dev + slot, 1), :], 0.0)
    later = jnp.where(row_ids == length, new_rows[pl.ds(slot, 1), :], later)
    cache[pl.ds(first, WINDOW), :] = jnp.where(row_ids < length, old, later).astype(
        jnp.bfloat16
    )

    def clear(tile, carry):
        start = pl.multiple_of(tile * ROW_TILE, ROW_TILE)
        cache[pl.ds(start, ROW_TILE), :] = jnp.zeros((ROW_TILE, width), jnp.bfloat16)
        return carry

    lax.fori_loop(first // ROW_TILE + WINDOW // ROW_TILE, rows // ROW_TILE, clear, 0)


def named_range(anc_ref, first, owner, per_dev):
    low, high = jnp.int32(per_dev), jnp.int32(-1)
    for j in range(per_dev):
        local = anc_ref[first + j] - owner * per_dev
        named = jnp.logical_and(local >= 0, local < per_dev)
        low = jnp.minimum(low, jnp.where(named, local, per_dev))
        high = jnp.maximum(high, jnp.where(named, local, -1))
    return low, high


def pack_kernel(per_dev, doms, step_pairs, len_hbm, anc_hbm, new_hbm, gen_hbm, *refs):
    sends = refs[: len(step_pairs)]
    new_len_ref, own_len_ref, own_anc_ref, slot_ref = refs[len(step_pairs) : len(step_pairs) + 4]
    len_ref, anc_ref, new_bf16, new_rows, list_sem, load_sem = refs[len(step_pairs) + 4 :]
    lists = [
        pltpu.make_async_copy(anc_hbm, anc_ref, list_sem.at[0]),
        pltpu.make_async_copy(len_hbm, len_ref, list_sem.at[1]),
        pltpu.make_async_copy(new_hbm, new_bf16, list_sem.at[2]),
    ]
    for copy in lists:
        copy.start()
    me, odd = lax.axis_index("dom"), lax.axis_index("tp") % 2
    lists[0].wait()
    picks = []
    loads = []
    for k, (even_step, odd_step) in enumerate(step_pairs):
        reader = jnp.clip(me + jnp.where(odd == 1, odd_step, even_step), 0, doms - 1)
        low, high = named_range(anc_ref, reader * per_dev, me, per_dev)
        for i, pick in enumerate((jnp.minimum(low, per_dev - 1), jnp.maximum(high, 0))):
            target = sends[k].at[i]
            load = pltpu.make_async_copy(gen_hbm.at[pick], target, load_sem.at[len(loads)])
            load.start()
            picks.append((pick, target))
            loads.append(load)
    lists[1].wait()
    for j in range(per_dev):
        own_anc_ref[j] = anc_ref[me * per_dev + j]
        new_len_ref[j] = len_ref[anc_ref[me * per_dev + j]] + 2
        own_len_ref[j] = len_ref[me * per_dev + j]
        slot_ref[j] = -1
    for k, (even_step, odd_step) in enumerate(step_pairs):
        source = me - jnp.where(odd == 1, odd_step, even_step)
        low, _ = named_range(anc_ref, me * per_dev, source, per_dev)
        for j in range(per_dev):
            local = anc_ref[me * per_dev + j] - source * per_dev
            named = jnp.logical_and(local >= 0, local < per_dev)
            slot = k * PICKS + jnp.where(local == low, 0, PICKS - 1)
            slot_ref[j] = jnp.where(named, slot, slot_ref[j])
    lists[2].wait()
    new_rows[...] = new_bf16[...].astype(jnp.float32).reshape(new_rows.shape)
    for load, (pick, target) in zip(loads, picks):
        load.wait()
        place_new_rows(target, new_rows, len_ref[me * per_dev + pick], pick, per_dev)


def pack(lengths, ancestors, new_kv, gen_cache, doms, step_pairs):
    per_dev, rows, width = gen_cache.shape
    count = len(step_pairs)
    smem = pl.BlockSpec(memory_space=pltpu.SMEM)
    vmem = pl.BlockSpec(memory_space=pltpu.VMEM)
    hbm = pl.BlockSpec(memory_space=pltpu.HBM)
    block_bytes = PICKS * rows * width * 2
    return pl.pallas_call(
        functools.partial(pack_kernel, per_dev, doms, step_pairs),
        out_shape=[jax.ShapeDtypeStruct((PICKS, rows, width), jnp.bfloat16)] * count
        + [jax.ShapeDtypeStruct((per_dev,), jnp.int32)] * 4,
        in_specs=[hbm] * 4,
        out_specs=[vmem] * count + [smem] * 4,
        scratch_shapes=[
            pltpu.SMEM(lengths.shape, jnp.int32),
            pltpu.SMEM(ancestors.shape, jnp.int32),
            pltpu.VMEM(new_kv.shape, jnp.bfloat16),
            pltpu.VMEM((2 * per_dev, width), jnp.float32),
            pltpu.SemaphoreType.DMA((3,)),
            pltpu.SemaphoreType.DMA((count * PICKS,)),
        ],
        compiler_params=pltpu.CompilerParams(vmem_limit_bytes=VMEM_BYTES),
        cost_estimate=pl.CostEstimate(
            flops=0, bytes_accessed=2 * count * block_bytes, transcendentals=0
        ),
        name="pack_sends",
    )(*(in_hbm(x) for x in (lengths, ancestors, new_kv, gen_cache)))


def fold_rows(block, combine):
    return combine(block.reshape(block.shape[0] // 8, 8, block.shape[1]), axis=0)


def attend_kernel(
    per_dev,
    group,
    kv_local,
    chunk,
    len_ref,
    anc_ref,
    q_ref,
    prompt_hbm,
    gen_hbm,
    new_ref,
    head_ref,
    extra_ref,
    share_ref,
    out_hbm,
    prompt,
    grown,
    scores,
    mixed_ref,
    prompt_sem,
    gen_sem,
    out_sem,
):
    me = lax.axis_index("dom")
    steps = q_ref.shape[0]
    rows, width = grown.shape[1:]
    chunks = prompt.shape[0] // chunk
    pair = 2 * HEAD_DIM
    scale = 1.0 / math.sqrt(HEAD_DIM)
    base = steps * per_dev
    lanes = group * base

    loads = [
        pltpu.make_async_copy(gen_hbm.at[p], grown.at[p], gen_sem.at[p]) for p in range(per_dev)
    ]
    for load in loads:
        load.start()

    def prompt_load(j):
        part = pl.ds(pl.multiple_of(j * chunk, chunk), chunk)
        return pltpu.make_async_copy(prompt_hbm.at[part], prompt.at[part], prompt_sem.at[j])

    for j in range(chunks):
        prompt_load(j).start()

    new_rows = new_ref[...].astype(jnp.float32).reshape(base, width)
    row_ids = lax.broadcasted_iota(jnp.int32, (rows, width), 0)
    for p in range(per_dev):
        loads[p].wait()
        behind = row_ids - len_ref[p]
        tail = jnp.where(behind == 1, new_rows[per_dev + p : per_dev + p + 1], 0.0)
        tail = jnp.where(behind == 0, new_rows[p : p + 1], tail)
        grown[p] = jnp.where(behind < 0, grown[p].astype(jnp.float32), tail).astype(
            jnp.bfloat16
        )
    homes = []
    for p in range(per_dev):
        local = anc_ref[p] - me * per_dev
        home = jnp.logical_and(local >= 0, local < per_dev)
        source = grown.at[jnp.clip(local, 0, per_dev - 1)]
        copy = pltpu.make_async_copy(source, out_hbm.at[p], out_sem.at[p])
        homes.append((home, copy))
        pl.when(home)(copy.start)

    q2 = q_ref[...].reshape(base, q_ref.shape[-1])
    queries = [
        jnp.concatenate(
            [q2[:, h * HEAD_DIM : (h + 1) * HEAD_DIM] for h in range(c * group, (c + 1) * group)],
            axis=0,
        )
        for c in range(kv_local)
    ]

    def score(keys, c):
        return lax.dot_general(
            keys, queries[c], (((1,), (1,)), ((), ())), preferred_element_type=jnp.float32
        )

    def mix(values, probs):
        return lax.dot_general(
            values, probs, (((0,), (0,)), ((), ())), preferred_element_type=jnp.float32
        )

    lane_ids = lax.broadcasted_iota(jnp.int32, (rows, lanes), 1)
    owner = lane_ids % per_dev
    last = lane_ids // per_dev % steps
    for p in range(per_dev):
        last = last + jnp.where(owner == p, len_ref[p], 0)
    visible = lax.broadcasted_iota(jnp.int32, (rows, lanes), 0) <= last

    own_scores = []
    tops = []
    for c in range(kv_local):
        keys = grown[:, :, c * pair : c * pair + HEAD_DIM].reshape(per_dev * rows, HEAD_DIM)
        every = score(keys, c)
        own = every[:rows]
        for p in range(1, per_dev):
            own = jnp.where(owner == p, every[p * rows : (p + 1) * rows], own)
        own = jnp.where(visible, own * scale, NEG_FILL)
        own_scores.append(own)
        tops.append(fold_rows(own, jnp.max))

    def score_chunk(j, tops):
        prompt_load(j).wait()
        part = pl.ds(pl.multiple_of(j * chunk, chunk), chunk)
        raised = []
        for c in range(kv_local):
            block = score(prompt[part, c * pair : c * pair + HEAD_DIM], c) * scale
            scores[c, part] = block
            raised.append(jnp.maximum(tops[c], fold_rows(block, jnp.max)))
        return tuple(raised)

    tops = lax.fori_loop(0, chunks, score_chunk, tuple(tops))
    maxima = [jnp.max(top, axis=0, keepdims=True) for top in tops]

    totals = []
    for c in range(kv_local):
        exps = jnp.where(visible, jnp.exp(own_scores[c] - maxima[c]), 0.0)
        totals.append(fold_rows(exps, jnp.sum))
        probs = jnp.concatenate(
            [jnp.where(owner == p, exps, 0.0).astype(jnp.bfloat16) for p in range(per_dev)],
            axis=0,
        )
        values = grown[:, :, c * pair + HEAD_DIM : (c + 1) * pair]
        mixed_ref[c] = mix(values.reshape(per_dev * rows, HEAD_DIM), probs)

    def mix_chunk(j, totals):
        part = pl.ds(pl.multiple_of(j * chunk, chunk), chunk)
        grew = []
        for c in range(kv_local):
            exps = jnp.exp(scores[c, part] - maxima[c])
            grew.append(totals[c] + fold_rows(exps, jnp.sum))
            mixed_ref[c] += mix(
                prompt[part, c * pair + HEAD_DIM : (c + 1) * pair], exps.astype(jnp.bfloat16)
            )
        return tuple(grew)

    totals = lax.fori_loop(0, chunks, mix_chunk, tuple(totals))
    weighted = jnp.zeros((base, HEAD_DIM), jnp.float32)
    for c in range(kv_local):
        mixed = (mixed_ref[c] / jnp.sum(totals[c], axis=0, keepdims=True)).T
        for h in range(group):
            weighted = (
                weighted + mixed[h * base : (h + 1) * base] * head_ref[c * group + h][None, :]
            )
    padding = jnp.zeros((HEAD_DIM - base, HEAD_DIM), jnp.float32)
    square = jnp.concatenate([weighted, padding], axis=0)
    row = jnp.sum(square.T, axis=0, keepdims=True) + extra_ref[...]
    share_ref[...] = jnp.broadcast_to(row[None], share_ref.shape)
    for home, copy in homes:
        pl.when(home)(copy.wait)


def attend(
    own_lengths, own_ancestors, queries, prompt_kv, gen_cache, new_kv, twist_vector, extra, devices
):
    steps, per_dev, width = queries.shape
    keys, kv_width = prompt_kv.shape
    rows = gen_cache.shape[1]
    kv_local = kv_width // (2 * HEAD_DIM)
    group = width // (kv_local * HEAD_DIM)
    lanes = steps * per_dev * group
    chunk = min(KEY_CHUNK, keys)
    head_weights = twist_vector.reshape(kv_local * group, HEAD_DIM)
    smem = pl.BlockSpec(memory_space=pltpu.SMEM)
    vmem = pl.BlockSpec(memory_space=pltpu.VMEM)
    hbm = pl.BlockSpec(memory_space=pltpu.HBM)
    score_count = lanes * kv_local * (keys + rows)
    return pl.pallas_call(
        functools.partial(attend_kernel, per_dev, group, kv_local, chunk),
        out_shape=[
            jax.ShapeDtypeStruct((devices, 1, HEAD_DIM), jnp.float32),
            jax.ShapeDtypeStruct(gen_cache.shape, jnp.bfloat16),
        ],
        in_specs=[smem, smem, vmem, hbm, hbm, vmem, vmem, vmem],
        out_specs=[vmem, hbm],
        scratch_shapes=[
            pltpu.VMEM(prompt_kv.shape, jnp.bfloat16),
            pltpu.VMEM(gen_cache.shape, jnp.bfloat16),
            pltpu.VMEM((kv_local, keys, lanes), jnp.float32),
            pltpu.VMEM((kv_local, HEAD_DIM, lanes), jnp.float32),
            pltpu.SemaphoreType.DMA((keys // chunk,)),
            pltpu.SemaphoreType.DMA((per_dev,)),
            pltpu.SemaphoreType.DMA((per_dev,)),
        ],
        compiler_params=pltpu.CompilerParams(vmem_limit_bytes=VMEM_BYTES),
        cost_estimate=pl.CostEstimate(
            flops=4 * score_count * HEAD_DIM,
            bytes_accessed=2 * (prompt_kv.size + 2 * gen_cache.size),
            transcendentals=score_count,
        ),
        name="attend",
    )(
        own_lengths,
        own_ancestors,
        queries,
        in_hbm(prompt_kv),
        in_hbm(gen_cache),
        new_kv,
        head_weights,
        extra,
    )


def finish_kernel(doms, tps, slot_ref, *refs):
    gots = refs[: len(ORDERS[0])]
    _, all_ref, out_ref, twist_ref, normal_ref, sums, sem = refs[len(gots) :]
    per_dev = out_ref.shape[0]
    for p in range(per_dev):
        slot = slot_ref[p]
        for k, got in enumerate(gots):
            for i in range(PICKS):
                copy = pltpu.make_async_copy(got.at[i], out_ref.at[p], sem.at[p])
                pl.when(slot == k * PICKS + i)(copy.start)
    for d in range(doms):
        row = all_ref[d * tps]
        for t in range(1, tps):
            row = row + all_ref[d * tps + t]
        sums[d : d + 1, :] = row
    step_0, step_1, prior = (
        slice(k * per_dev, (k + 1) * per_dev) for k in range(3)
    )
    totals = sums[...]
    log_weights = totals[:, prior] + totals[:, step_1] - totals[:, step_0]
    largest = jnp.max(log_weights, keepdims=True)
    log_total = largest + jnp.log(jnp.sum(jnp.exp(log_weights - largest), keepdims=True))
    mine = sums[pl.ds(lax.axis_index("dom"), 1), :]
    own = mine[:, prior] + mine[:, step_1] - mine[:, step_0]
    twist_ref[...] = jnp.concatenate([mine[:, step_0], mine[:, step_1]], axis=0)
    normal_ref[...] = own - log_total
    for p in range(per_dev):
        copy = pltpu.make_async_copy(gots[0].at[0], out_ref.at[p], sem.at[p])
        pl.when(slot_ref[p] >= 0)(copy.wait)


def finish(slots, gots, held, shares, doms, tps):
    per_dev = held.shape[0]
    count = len(gots)
    smem = pl.BlockSpec(memory_space=pltpu.SMEM)
    vmem = pl.BlockSpec(memory_space=pltpu.VMEM)
    hbm = pl.BlockSpec(memory_space=pl.ANY)
    return pl.pallas_call(
        functools.partial(finish_kernel, doms, tps),
        out_shape=[
            jax.ShapeDtypeStruct(held.shape, held.dtype),
            jax.ShapeDtypeStruct((2, per_dev), jnp.float32),
            jax.ShapeDtypeStruct((1, per_dev), jnp.float32),
        ],
        in_specs=[smem] + [vmem] * count + [hbm, vmem],
        out_specs=[hbm, vmem, vmem],
        input_output_aliases={1 + count: 0},
        scratch_shapes=[
            pltpu.VMEM((doms, HEAD_DIM), jnp.float32),
            pltpu.SemaphoreType.DMA((per_dev,)),
        ],
        compiler_params=pltpu.CompilerParams(vmem_limit_bytes=VMEM_BYTES),
        cost_estimate=pl.CostEstimate(
            flops=0, bytes_accessed=held.size, transcendentals=0
        ),
        name="finish",
    )(slots, *gots, held, shares)


def routes(doms, tps, steps):
    pairs = []
    for d in range(doms):
        for t in range(tps):
            target = d + steps[t % 2]
            if 0 <= target < doms:
                pairs.append((d * tps + t, target * tps + t))
    return pairs


def local(
    queries,
    new_kv,
    gen_cache,
    prompt_kv,
    lengths,
    ancestors,
    tokens,
    twist_vector,
    twist_bias,
    prior_weights,
):
    doms, tps = lax.axis_size("dom"), lax.axis_size("tp")
    per_dev = gen_cache.shape[0]
    step_pairs = list(zip(*ORDERS))
    everyone = ("dom", "tp")

    *sends, new_lengths, own_lengths, own_ancestors, slots = pack(
        lengths, ancestors, new_kv, gen_cache, doms, step_pairs
    )
    arrivals = [
        lax.ppermute(send, everyone, routes(doms, tps, steps))
        for send, steps in zip(sends, step_pairs)
    ]

    bias = jnp.take(twist_bias, tokens, axis=0).reshape(-1)
    extra = jnp.concatenate([bias, prior_weights])
    extra = jnp.where(lax.axis_index("tp") == 0, extra, 0.0)
    extra = jnp.pad(extra, (0, HEAD_DIM - extra.size))[None]
    shares, resampled = attend(
        own_lengths,
        own_ancestors,
        queries,
        prompt_kv,
        gen_cache,
        new_kv,
        twist_vector,
        extra,
        doms * tps,
    )
    shares = lax.all_to_all(shares, everyone, 0, 0, tiled=True)
    resampled, twist, normalized = finish(slots, arrivals, resampled, shares, doms, tps)
    return (twist, normalized.reshape(per_dev), resampled, new_lengths)


def solution(mesh):
    in_specs = (
        P(None, "dom", "tp"),
        P(None, "dom", "tp"),
        P("dom", None, "tp"),
        P(None, "tp"),
        P(),
        P(),
        P(None, "dom"),
        P("tp"),
        P(),
        P("dom"),
    )
    out_specs = (P(None, "dom"), P("dom"), P("dom", None, "tp"), P("dom"))
    return jax.shard_map(local, mesh=mesh, in_specs=in_specs, out_specs=out_specs, check_vma=False)
```

```python
import functools
import math

import jax
import jax.numpy as jnp
from jax import lax
from jax.experimental import pallas as pl
from jax.experimental.pallas import tpu as pltpu
from jax.sharding import PartitionSpec as P

HEAD_DIM = 128
SPAN = 2
PICKS = 2
NEG_FILL = -1e30
KEY_CHUNK = 512
VMEM_BYTES = 44 * 1024 * 1024
ROW_TILE = 16
WINDOW = 2 * ROW_TILE

ORDERS = ((-2, 2, 1, -1), (1, -1, -2, 2))


def in_hbm(x):
    return pltpu.with_memory_space_constraint(x, pltpu.HBM)


def place_new_rows(cache, new_rows, length, slot, per_dev):
    rows, width = cache.shape
    first = pl.multiple_of(
        jnp.minimum(length // ROW_TILE * ROW_TILE, rows - WINDOW), ROW_TILE
    )
    row_ids = first + lax.broadcasted_iota(jnp.int32, (WINDOW, width), 0)
    old = cache[pl.ds(first, WINDOW), :].astype(jnp.float32)
    later = jnp.where(row_ids == length + 1, new_rows[pl.ds(per_dev + slot, 1), :], 0.0)
    later = jnp.where(row_ids == length, new_rows[pl.ds(slot, 1), :], later)
    cache[pl.ds(first, WINDOW), :] = jnp.where(row_ids < length, old, later).astype(
        jnp.bfloat16
    )

    def clear(tile, carry):
        start = pl.multiple_of(tile * ROW_TILE, ROW_TILE)
        cache[pl.ds(start, ROW_TILE), :] = jnp.zeros((ROW_TILE, width), jnp.bfloat16)
        return carry

    lax.fori_loop(first // ROW_TILE + WINDOW // ROW_TILE, rows // ROW_TILE, clear, 0)


def named_range(anc_ref, first, owner, per_dev):
    low, high = jnp.int32(per_dev), jnp.int32(-1)
    for j in range(per_dev):
        local = anc_ref[first + j] - owner * per_dev
        named = jnp.logical_and(local >= 0, local < per_dev)
        low = jnp.minimum(low, jnp.where(named, local, per_dev))
        high = jnp.maximum(high, jnp.where(named, local, -1))
    return low, high


def pack_kernel(per_dev, doms, step_pairs, len_hbm, anc_hbm, new_hbm, gen_hbm, *refs):
    sends = refs[: len(step_pairs)]
    new_len_ref, own_len_ref, own_anc_ref, slot_ref = refs[len(step_pairs) : len(step_pairs) + 4]
    len_ref, anc_ref, new_bf16, new_rows, list_sem, load_sem = refs[len(step_pairs) + 4 :]
    lists = [
        pltpu.make_async_copy(anc_hbm, anc_ref, list_sem.at[0]),
        pltpu.make_async_copy(len_hbm, len_ref, list_sem.at[1]),
        pltpu.make_async_copy(new_hbm, new_bf16, list_sem.at[2]),
    ]
    for copy in lists:
        copy.start()
    me, odd = lax.axis_index("dom"), lax.axis_index("tp") % 2
    lists[0].wait()
    picks = []
    loads = []
    for k, (even_step, odd_step) in enumerate(step_pairs):
        reader = jnp.clip(me + jnp.where(odd == 1, odd_step, even_step), 0, doms - 1)
        low, high = named_range(anc_ref, reader * per_dev, me, per_dev)
        for i, pick in enumerate((jnp.minimum(low, per_dev - 1), jnp.maximum(high, 0))):
            target = sends[k].at[i]
            load = pltpu.make_async_copy(gen_hbm.at[pick], target, load_sem.at[len(loads)])
            load.start()
            picks.append((pick, target))
            loads.append(load)
    lists[1].wait()
    for j in range(per_dev):
        own_anc_ref[j] = anc_ref[me * per_dev + j]
        new_len_ref[j] = len_ref[anc_ref[me * per_dev + j]] + 2
        own_len_ref[j] = len_ref[me * per_dev + j]
        slot_ref[j] = -1
    for k, (even_step, odd_step) in enumerate(step_pairs):
        source = me - jnp.where(odd == 1, odd_step, even_step)
        low, _ = named_range(anc_ref, me * per_dev, source, per_dev)
        for j in range(per_dev):
            local = anc_ref[me * per_dev + j] - source * per_dev
            named = jnp.logical_and(local >= 0, local < per_dev)
            slot = k * PICKS + jnp.where(local == low, 0, PICKS - 1)
            slot_ref[j] = jnp.where(named, slot, slot_ref[j])
    lists[2].wait()
    new_rows[...] = new_bf16[...].astype(jnp.float32).reshape(new_rows.shape)
    for load, (pick, target) in zip(loads, picks):
        load.wait()
        place_new_rows(target, new_rows, len_ref[me * per_dev + pick], pick, per_dev)


def pack(lengths, ancestors, new_kv, gen_cache, doms, step_pairs):
    per_dev, rows, width = gen_cache.shape
    count = len(step_pairs)
    smem = pl.BlockSpec(memory_space=pltpu.SMEM)
    vmem = pl.BlockSpec(memory_space=pltpu.VMEM)
    hbm = pl.BlockSpec(memory_space=pltpu.HBM)
    block_bytes = PICKS * rows * width * 2
    return pl.pallas_call(
        functools.partial(pack_kernel, per_dev, doms, step_pairs),
        out_shape=[jax.ShapeDtypeStruct((PICKS, rows, width), jnp.bfloat16)] * count
        + [jax.ShapeDtypeStruct((per_dev,), jnp.int32)] * 4,
        in_specs=[hbm] * 4,
        out_specs=[vmem] * count + [smem] * 4,
        scratch_shapes=[
            pltpu.SMEM(lengths.shape, jnp.int32),
            pltpu.SMEM(ancestors.shape, jnp.int32),
            pltpu.VMEM(new_kv.shape, jnp.bfloat16),
            pltpu.VMEM((2 * per_dev, width), jnp.float32),
            pltpu.SemaphoreType.DMA((3,)),
            pltpu.SemaphoreType.DMA((count * PICKS,)),
        ],
        compiler_params=pltpu.CompilerParams(vmem_limit_bytes=VMEM_BYTES),
        cost_estimate=pl.CostEstimate(
            flops=0, bytes_accessed=2 * count * block_bytes, transcendentals=0
        ),
        name="pack_sends",
    )(*(in_hbm(x) for x in (lengths, ancestors, new_kv, gen_cache)))


def fold_rows(block, combine):
    return combine(block.reshape(block.shape[0] // 8, 8, block.shape[1]), axis=0)


def attend_kernel(
    per_dev,
    group,
    kv_local,
    chunk,
    len_ref,
    anc_ref,
    q_ref,
    prompt_hbm,
    gen_hbm,
    new_ref,
    head_ref,
    extra_ref,
    share_ref,
    out_hbm,
    prompt,
    grown,
    scores,
    mixed_ref,
    prompt_sem,
    gen_sem,
    out_sem,
):
    me = lax.axis_index("dom")
    steps = q_ref.shape[0]
    rows, width = grown.shape[1:]
    chunks = prompt.shape[0] // chunk
    pair = 2 * HEAD_DIM
    scale = 1.0 / math.sqrt(HEAD_DIM)
    base = steps * per_dev
    lanes = group * base

    loads = [
        pltpu.make_async_copy(gen_hbm.at[p], grown.at[p], gen_sem.at[p]) for p in range(per_dev)
    ]
    for load in loads:
        load.start()

    def prompt_load(j):
        part = pl.ds(pl.multiple_of(j * chunk, chunk), chunk)
        return pltpu.make_async_copy(prompt_hbm.at[part], prompt.at[part], prompt_sem.at[j])

    for j in range(chunks):
        prompt_load(j).start()

    new_rows = new_ref[...].astype(jnp.float32).reshape(base, width)
    row_ids = lax.broadcasted_iota(jnp.int32, (rows, width), 0)
    for p in range(per_dev):
        loads[p].wait()
        behind = row_ids - len_ref[p]
        tail = jnp.where(behind == 1, new_rows[per_dev + p : per_dev + p + 1], 0.0)
        tail = jnp.where(behind == 0, new_rows[p : p + 1], tail)
        grown[p] = jnp.where(behind < 0, grown[p].astype(jnp.float32), tail).astype(
            jnp.bfloat16
        )
    homes = []
    for p in range(per_dev):
        local = anc_ref[p] - me * per_dev
        home = jnp.logical_and(local >= 0, local < per_dev)
        source = grown.at[jnp.clip(local, 0, per_dev - 1)]
        copy = pltpu.make_async_copy(source, out_hbm.at[p], out_sem.at[p])
        homes.append((home, copy))
        pl.when(home)(copy.start)

    q2 = q_ref[...].reshape(base, q_ref.shape[-1])
    queries = [
        jnp.concatenate(
            [q2[:, h * HEAD_DIM : (h + 1) * HEAD_DIM] for h in range(c * group, (c + 1) * group)],
            axis=0,
        )
        for c in range(kv_local)
    ]

    def score(keys, c):
        return lax.dot_general(
            keys, queries[c], (((1,), (1,)), ((), ())), preferred_element_type=jnp.float32
        )

    def mix(values, probs):
        return lax.dot_general(
            values, probs, (((0,), (0,)), ((), ())), preferred_element_type=jnp.float32
        )

    lane_ids = lax.broadcasted_iota(jnp.int32, (rows, lanes), 1)
    owner = lane_ids % per_dev
    last = lane_ids // per_dev % steps
    for p in range(per_dev):
        last = last + jnp.where(owner == p, len_ref[p], 0)
    visible = lax.broadcasted_iota(jnp.int32, (rows, lanes), 0) <= last

    own_scores = []
    tops = []
    for c in range(kv_local):
        keys = grown[:, :, c * pair : c * pair + HEAD_DIM].reshape(per_dev * rows, HEAD_DIM)
        every = score(keys, c)
        own = every[:rows]
        for p in range(1, per_dev):
            own = jnp.where(owner == p, every[p * rows : (p + 1) * rows], own)
        own = jnp.where(visible, own * scale, NEG_FILL)
        own_scores.append(own)
        tops.append(fold_rows(own, jnp.max))

    def score_chunk(j, tops):
        prompt_load(j).wait()
        part = pl.ds(pl.multiple_of(j * chunk, chunk), chunk)
        raised = []
        for c in range(kv_local):
            block = score(prompt[part, c * pair : c * pair + HEAD_DIM], c) * scale
            scores[c, part] = block
            raised.append(jnp.maximum(tops[c], fold_rows(block, jnp.max)))
        return tuple(raised)

    tops = lax.fori_loop(0, chunks, score_chunk, tuple(tops))
    maxima = [jnp.max(top, axis=0, keepdims=True) for top in tops]

    totals = []
    for c in range(kv_local):
        exps = jnp.where(visible, jnp.exp(own_scores[c] - maxima[c]), 0.0)
        totals.append(fold_rows(exps, jnp.sum))
        probs = jnp.concatenate(
            [jnp.where(owner == p, exps, 0.0).astype(jnp.bfloat16) for p in range(per_dev)],
            axis=0,
        )
        values = grown[:, :, c * pair + HEAD_DIM : (c + 1) * pair]
        mixed_ref[c] = mix(values.reshape(per_dev * rows, HEAD_DIM), probs)

    def mix_chunk(j, totals):
        part = pl.ds(pl.multiple_of(j * chunk, chunk), chunk)
        grew = []
        for c in range(kv_local):
            exps = jnp.exp(scores[c, part] - maxima[c])
            grew.append(totals[c] + fold_rows(exps, jnp.sum))
            mixed_ref[c] += mix(
                prompt[part, c * pair + HEAD_DIM : (c + 1) * pair], exps.astype(jnp.bfloat16)
            )
        return tuple(grew)

    totals = lax.fori_loop(0, chunks, mix_chunk, tuple(totals))
    weighted = jnp.zeros((base, HEAD_DIM), jnp.float32)
    for c in range(kv_local):
        mixed = (mixed_ref[c] / jnp.sum(totals[c], axis=0, keepdims=True)).T
        for h in range(group):
            weighted = (
                weighted + mixed[h * base : (h + 1) * base] * head_ref[c * group + h][None, :]
            )
    padding = jnp.zeros((HEAD_DIM - base, HEAD_DIM), jnp.float32)
    square = jnp.concatenate([weighted, padding], axis=0)
    row = jnp.sum(square.T, axis=0, keepdims=True) + extra_ref[...]
    share_ref[...] = jnp.broadcast_to(row, share_ref.shape)
    for home, copy in homes:
        pl.when(home)(copy.wait)


def attend(
    own_lengths, own_ancestors, queries, prompt_kv, gen_cache, new_kv, twist_vector, extra
):
    steps, per_dev, width = queries.shape
    keys, kv_width = prompt_kv.shape
    rows = gen_cache.shape[1]
    kv_local = kv_width // (2 * HEAD_DIM)
    group = width // (kv_local * HEAD_DIM)
    lanes = steps * per_dev * group
    chunk = min(KEY_CHUNK, keys)
    head_weights = twist_vector.reshape(kv_local * group, HEAD_DIM)
    smem = pl.BlockSpec(memory_space=pltpu.SMEM)
    vmem = pl.BlockSpec(memory_space=pltpu.VMEM)
    hbm = pl.BlockSpec(memory_space=pltpu.HBM)
    score_count = lanes * kv_local * (keys + rows)
    return pl.pallas_call(
        functools.partial(attend_kernel, per_dev, group, kv_local, chunk),
        out_shape=[
            jax.ShapeDtypeStruct((8, HEAD_DIM), jnp.float32),
            jax.ShapeDtypeStruct(gen_cache.shape, jnp.bfloat16),
        ],
        in_specs=[smem, smem, vmem, hbm, hbm, vmem, vmem, vmem],
        out_specs=[vmem, hbm],
        scratch_shapes=[
            pltpu.VMEM(prompt_kv.shape, jnp.bfloat16),
            pltpu.VMEM(gen_cache.shape, jnp.bfloat16),
            pltpu.VMEM((kv_local, keys, lanes), jnp.float32),
            pltpu.VMEM((kv_local, HEAD_DIM, lanes), jnp.float32),
            pltpu.SemaphoreType.DMA((keys // chunk,)),
            pltpu.SemaphoreType.DMA((per_dev,)),
            pltpu.SemaphoreType.DMA((per_dev,)),
        ],
        compiler_params=pltpu.CompilerParams(vmem_limit_bytes=VMEM_BYTES),
        cost_estimate=pl.CostEstimate(
            flops=4 * score_count * HEAD_DIM,
            bytes_accessed=2 * (prompt_kv.size + 2 * gen_cache.size),
            transcendentals=score_count,
        ),
        name="attend",
    )(
        own_lengths,
        own_ancestors,
        queries,
        in_hbm(prompt_kv),
        in_hbm(gen_cache),
        new_kv,
        head_weights,
        extra,
    )


def deliver_kernel(slot_ref, *refs):
    gots = refs[: len(ORDERS[0])]
    _, out_ref, sem = refs[len(gots) :]
    per_dev = out_ref.shape[0]
    for p in range(per_dev):
        slot = slot_ref[p]
        for k, got in enumerate(gots):
            for i in range(PICKS):
                copy = pltpu.make_async_copy(got.at[i], out_ref.at[p], sem.at[p])
                pl.when(slot == k * PICKS + i)(copy.start)
    for p in range(per_dev):
        copy = pltpu.make_async_copy(gots[0].at[0], out_ref.at[p], sem.at[p])
        pl.when(slot_ref[p] >= 0)(copy.wait)


def deliver(slots, gots, held):
    smem = pl.BlockSpec(memory_space=pltpu.SMEM)
    vmem = pl.BlockSpec(memory_space=pltpu.VMEM)
    hbm = pl.BlockSpec(memory_space=pl.ANY)
    return pl.pallas_call(
        deliver_kernel,
        out_shape=jax.ShapeDtypeStruct(held.shape, held.dtype),
        in_specs=[smem] + [vmem] * len(gots) + [hbm],
        out_specs=hbm,
        input_output_aliases={1 + len(gots): 0},
        scratch_shapes=[pltpu.SemaphoreType.DMA((held.shape[0],))],
        compiler_params=pltpu.CompilerParams(vmem_limit_bytes=VMEM_BYTES),
        cost_estimate=pl.CostEstimate(
            flops=0, bytes_accessed=held.size, transcendentals=0
        ),
        name="deliver",
    )(slots, *gots, held)


def normalize_kernel(doms, tps, all_ref, twist_ref, normal_ref, sums):
    per_dev = normal_ref.shape[1]
    for d in range(doms):
        row = all_ref[d * tps, :1]
        for t in range(1, tps):
            row = row + all_ref[d * tps + t, :1]
        sums[d : d + 1, :] = row
    step_0, step_1, prior = (
        slice(k * per_dev, (k + 1) * per_dev) for k in range(3)
    )
    totals = sums[...]
    log_weights = totals[:, prior] + totals[:, step_1] - totals[:, step_0]
    largest = jnp.max(log_weights, keepdims=True)
    log_total = largest + jnp.log(jnp.sum(jnp.exp(log_weights - largest), keepdims=True))
    mine = sums[pl.ds(lax.axis_index("dom"), 1), :]
    own = mine[:, prior] + mine[:, step_1] - mine[:, step_0]
    twist_ref[...] = jnp.concatenate([mine[:, step_0], mine[:, step_1]], axis=0)
    normal_ref[...] = own - log_total


def normalize(shares, doms, tps, per_dev):
    return pl.pallas_call(
        functools.partial(normalize_kernel, doms, tps),
        out_shape=[
            jax.ShapeDtypeStruct((2, per_dev), jnp.float32),
            jax.ShapeDtypeStruct((1, per_dev), jnp.float32),
        ],
        scratch_shapes=[pltpu.VMEM((doms, HEAD_DIM), jnp.float32)],
        name="normalize",
    )(shares)


def routes(doms, tps, steps):
    pairs = []
    for d in range(doms):
        for t in range(tps):
            target = d + steps[t % 2]
            if 0 <= target < doms:
                pairs.append((d * tps + t, target * tps + t))
    return pairs


def local(
    queries,
    new_kv,
    gen_cache,
    prompt_kv,
    lengths,
    ancestors,
    tokens,
    twist_vector,
    twist_bias,
    prior_weights,
):
    doms, tps = lax.axis_size("dom"), lax.axis_size("tp")
    per_dev = gen_cache.shape[0]
    step_pairs = list(zip(*ORDERS))
    everyone = ("dom", "tp")

    *sends, new_lengths, own_lengths, own_ancestors, slots = pack(
        lengths, ancestors, new_kv, gen_cache, doms, step_pairs
    )
    arrivals = [
        lax.ppermute(send, everyone, routes(doms, tps, steps))
        for send, steps in zip(sends, step_pairs)
    ]

    bias = jnp.take(twist_bias, tokens, axis=0).reshape(-1)
    extra = jnp.concatenate([bias, prior_weights])
    extra = jnp.where(lax.axis_index("tp") == 0, extra, 0.0)
    extra = jnp.pad(extra, (0, HEAD_DIM - extra.size))[None]
    shares, resampled = attend(
        own_lengths,
        own_ancestors,
        queries,
        prompt_kv,
        gen_cache,
        new_kv,
        twist_vector,
        extra,
    )
    shares = lax.all_gather(shares, everyone)
    resampled = deliver(slots, arrivals, resampled)
    twist, normalized = normalize(shares, doms, tps, per_dev)
    return (twist, normalized.reshape(per_dev), resampled, new_lengths)


def solution(mesh):
    in_specs = (
        P(None, "dom", "tp"),
        P(None, "dom", "tp"),
        P("dom", None, "tp"),
        P(None, "tp"),
        P(),
        P(),
        P(None, "dom"),
        P("tp"),
        P(),
        P("dom"),
    )
    out_specs = (P(None, "dom"), P("dom"), P("dom", None, "tp"), P("dom"))
    return jax.shard_map(local, mesh=mesh, in_specs=in_specs, out_specs=out_specs, check_vma=False)
```

```python
import functools
import math

import jax
import jax.numpy as jnp
from jax import lax
from jax.experimental import pallas as pl
from jax.experimental.pallas import tpu as pltpu
from jax.sharding import PartitionSpec as P

HEAD_DIM = 128
SPAN = 2
PICKS = 2
NEG_FILL = -1e30
KEY_CHUNK = 512
VMEM_BYTES = 44 * 1024 * 1024
ROW_TILE = 16
WINDOW = 2 * ROW_TILE

ORDERS = ((-2, 2, 1, -1), (1, -1, -2, 2))


def in_hbm(x):
    return pltpu.with_memory_space_constraint(x, pltpu.HBM)


def place_new_rows(cache, new_rows, length, slot, per_dev):
    rows, width = cache.shape
    first = pl.multiple_of(
        jnp.minimum(length // ROW_TILE * ROW_TILE, rows - WINDOW), ROW_TILE
    )
    row_ids = first + lax.broadcasted_iota(jnp.int32, (WINDOW, width), 0)
    old = cache[pl.ds(first, WINDOW), :].astype(jnp.float32)
    later = jnp.where(row_ids == length + 1, new_rows[pl.ds(per_dev + slot, 1), :], 0.0)
    later = jnp.where(row_ids == length, new_rows[pl.ds(slot, 1), :], later)
    cache[pl.ds(first, WINDOW), :] = jnp.where(row_ids < length, old, later).astype(
        jnp.bfloat16
    )

    def clear(tile, carry):
        start = pl.multiple_of(tile * ROW_TILE, ROW_TILE)
        cache[pl.ds(start, ROW_TILE), :] = jnp.zeros((ROW_TILE, width), jnp.bfloat16)
        return carry

    lax.fori_loop(first // ROW_TILE + WINDOW // ROW_TILE, rows // ROW_TILE, clear, 0)


def named_range(anc_ref, first, owner, per_dev):
    low, high = jnp.int32(per_dev), jnp.int32(-1)
    for j in range(per_dev):
        local = anc_ref[first + j] - owner * per_dev
        named = jnp.logical_and(local >= 0, local < per_dev)
        low = jnp.minimum(low, jnp.where(named, local, per_dev))
        high = jnp.maximum(high, jnp.where(named, local, -1))
    return low, high


def pack_kernel(per_dev, doms, step_pairs, len_hbm, anc_hbm, new_hbm, gen_hbm, *refs):
    sends = refs[: len(step_pairs)]
    new_len_ref, own_len_ref, own_anc_ref, slot_ref = refs[len(step_pairs) : len(step_pairs) + 4]
    len_ref, anc_ref, new_bf16, new_rows, list_sem, load_sem = refs[len(step_pairs) + 4 :]
    lists = [
        pltpu.make_async_copy(anc_hbm, anc_ref, list_sem.at[0]),
        pltpu.make_async_copy(len_hbm, len_ref, list_sem.at[1]),
        pltpu.make_async_copy(new_hbm, new_bf16, list_sem.at[2]),
    ]
    for copy in lists:
        copy.start()
    me, odd = lax.axis_index("dom"), lax.axis_index("tp") % 2
    lists[0].wait()
    picks = []
    loads = []
    for k, (even_step, odd_step) in enumerate(step_pairs):
        reader = jnp.clip(me + jnp.where(odd == 1, odd_step, even_step), 0, doms - 1)
        low, high = named_range(anc_ref, reader * per_dev, me, per_dev)
        for i, pick in enumerate((jnp.minimum(low, per_dev - 1), jnp.maximum(high, 0))):
            target = sends[k].at[i]
            load = pltpu.make_async_copy(gen_hbm.at[pick], target, load_sem.at[len(loads)])
            load.start()
            picks.append((pick, target))
            loads.append(load)
    lists[1].wait()
    for j in range(per_dev):
        own_anc_ref[j] = anc_ref[me * per_dev + j]
        new_len_ref[j] = len_ref[anc_ref[me * per_dev + j]] + 2
        own_len_ref[j] = len_ref[me * per_dev + j]
        slot_ref[j] = -1
    for k, (even_step, odd_step) in enumerate(step_pairs):
        source = me - jnp.where(odd == 1, odd_step, even_step)
        low, _ = named_range(anc_ref, me * per_dev, source, per_dev)
        for j in range(per_dev):
            local = anc_ref[me * per_dev + j] - source * per_dev
            named = jnp.logical_and(local >= 0, local < per_dev)
            slot = k * PICKS + jnp.where(local == low, 0, PICKS - 1)
            slot_ref[j] = jnp.where(named, slot, slot_ref[j])
    lists[2].wait()
    new_rows[...] = new_bf16[...].astype(jnp.float32).reshape(new_rows.shape)
    for load, (pick, target) in zip(loads, picks):
        load.wait()
        place_new_rows(target, new_rows, len_ref[me * per_dev + pick], pick, per_dev)


def pack(lengths, ancestors, new_kv, gen_cache, doms, step_pairs):
    per_dev, rows, width = gen_cache.shape
    count = len(step_pairs)
    smem = pl.BlockSpec(memory_space=pltpu.SMEM)
    vmem = pl.BlockSpec(memory_space=pltpu.VMEM)
    hbm = pl.BlockSpec(memory_space=pltpu.HBM)
    block_bytes = PICKS * rows * width * 2
    return pl.pallas_call(
        functools.partial(pack_kernel, per_dev, doms, step_pairs),
        out_shape=[jax.ShapeDtypeStruct((PICKS, rows, width), jnp.bfloat16)] * count
        + [jax.ShapeDtypeStruct((per_dev,), jnp.int32)] * 4,
        in_specs=[hbm] * 4,
        out_specs=[vmem] * count + [smem] * 4,
        scratch_shapes=[
            pltpu.SMEM(lengths.shape, jnp.int32),
            pltpu.SMEM(ancestors.shape, jnp.int32),
            pltpu.VMEM(new_kv.shape, jnp.bfloat16),
            pltpu.VMEM((2 * per_dev, width), jnp.float32),
            pltpu.SemaphoreType.DMA((3,)),
            pltpu.SemaphoreType.DMA((count * PICKS,)),
        ],
        compiler_params=pltpu.CompilerParams(vmem_limit_bytes=VMEM_BYTES),
        cost_estimate=pl.CostEstimate(
            flops=0, bytes_accessed=2 * count * block_bytes, transcendentals=0
        ),
        name="pack_sends",
    )(*(in_hbm(x) for x in (lengths, ancestors, new_kv, gen_cache)))


def fold_rows(block, combine):
    return combine(block.reshape(block.shape[0] // 8, 8, block.shape[1]), axis=0)


def attend_kernel(
    per_dev,
    group,
    kv_local,
    chunk,
    len_ref,
    anc_ref,
    q_ref,
    prompt_hbm,
    gen_hbm,
    new_ref,
    head_ref,
    extra_ref,
    share_ref,
    out_hbm,
    prompt,
    grown,
    new_rows,
    scores,
    mixed_ref,
    prompt_sem,
    gen_sem,
    out_sem,
):
    me = lax.axis_index("dom")
    steps = q_ref.shape[0]
    rows, width = grown.shape[1:]
    chunks = prompt.shape[0] // chunk
    pair = 2 * HEAD_DIM
    scale = 1.0 / math.sqrt(HEAD_DIM)
    base = steps * per_dev
    lanes = group * base

    half = per_dev // 2
    per_chunk = per_dev // chunks

    def gen_load(p):
        return pltpu.make_async_copy(gen_hbm.at[p], grown.at[p], gen_sem.at[p])

    def prompt_load(j):
        part = pl.ds(pl.multiple_of(j * chunk, chunk), chunk)
        return pltpu.make_async_copy(prompt_hbm.at[part], prompt.at[part], prompt_sem.at[j])

    for j in range(chunks):
        prompt_load(j).start()
        for i in range(per_chunk):
            gen_load(j * per_chunk + i).start()

    new_rows[...] = new_ref[...].astype(jnp.float32).reshape(base, width)
    row_ids = lax.broadcasted_iota(jnp.int32, (rows, width), 0)

    def patch(p):
        gen_load(p).wait()
        behind = row_ids - len_ref[p]
        tail = jnp.where(behind == 1, new_rows[pl.ds(per_dev + p, 1), :], 0.0)
        tail = jnp.where(behind == 0, new_rows[pl.ds(p, 1), :], tail)
        grown[p] = jnp.where(behind < 0, grown[p].astype(jnp.float32), tail).astype(
            jnp.bfloat16
        )

    q2 = q_ref[...].reshape(base, q_ref.shape[-1])
    queries = [
        jnp.concatenate(
            [q2[:, h * HEAD_DIM : (h + 1) * HEAD_DIM] for h in range(c * group, (c + 1) * group)],
            axis=0,
        )
        for c in range(kv_local)
    ]

    def score(keys, rows):
        return lax.dot_general(
            keys, rows, (((1,), (1,)), ((), ())), preferred_element_type=jnp.float32
        )

    def mix(values, probs):
        return lax.dot_general(
            values, probs, (((0,), (0,)), ((), ())), preferred_element_type=jnp.float32
        )

    def score_chunk(j, tops):
        prompt_load(j).wait()
        part = pl.ds(pl.multiple_of(j * chunk, chunk), chunk)
        raised = []
        for c in range(kv_local):
            block = score(prompt[part, c * pair : c * pair + HEAD_DIM], queries[c]) * scale
            scores[c, part] = block
            raised.append(jnp.maximum(tops[c], fold_rows(block, jnp.max)))
        for i in range(per_chunk):
            patch(j * per_chunk + i)
        return tuple(raised)

    lowest = jnp.full((8, lanes), NEG_FILL, jnp.float32)
    tops = lax.fori_loop(0, chunks, score_chunk, (lowest,) * kv_local)

    homes = []
    for p in range(per_dev):
        local = anc_ref[p] - me * per_dev
        home = jnp.logical_and(local >= 0, local < per_dev)
        source = grown.at[jnp.clip(local, 0, per_dev - 1)]
        copy = pltpu.make_async_copy(source, out_hbm.at[p], out_sem.at[p])
        homes.append((home, copy))
        pl.when(home)(copy.start)

    lane_ids = lax.broadcasted_iota(jnp.int32, (rows, lanes), 1)
    owner = lane_ids % per_dev
    lower, seat = owner < half, owner % half
    last = lane_ids // per_dev % steps
    for p in range(per_dev):
        last = last + jnp.where(owner == p, len_ref[p], 0)
    visible = lax.broadcasted_iota(jnp.int32, (rows, lanes), 0) <= last
    query_lower = lax.broadcasted_iota(jnp.int32, (lanes, HEAD_DIM), 0) % per_dev < half

    def halves(block, lower, axis):
        block = block.astype(jnp.float32)
        parts = [jnp.where(lower, block, 0.0), jnp.where(lower, 0.0, block)]
        return jnp.concatenate(parts, axis=axis).astype(jnp.bfloat16)

    def by_seat(blocks):
        size = blocks.shape[0] // half
        chosen = blocks[:size]
        for i in range(1, half):
            chosen = jnp.where(seat == i, blocks[i * size : (i + 1) * size], chosen)
        return chosen

    totals = []
    maxima = []
    for c in range(kv_local):
        columns = slice(c * pair, c * pair + HEAD_DIM)
        keys = jnp.concatenate(
            [
                jnp.concatenate([grown[i, :, columns], grown[i + half, :, columns]], axis=1)
                for i in range(half)
            ],
            axis=0,
        )
        own = by_seat(score(keys, halves(queries[c], query_lower, 1)))
        own = jnp.where(visible, own * scale, NEG_FILL)
        top = jnp.maximum(tops[c], fold_rows(own, jnp.max))
        maxima.append(jnp.max(top, axis=0, keepdims=True))
        exps = jnp.where(visible, jnp.exp(own - maxima[c]), 0.0)
        totals.append(fold_rows(exps, jnp.sum))
        columns = slice(c * pair + HEAD_DIM, (c + 1) * pair)
        values = jnp.concatenate(
            [
                jnp.concatenate([grown[i, :, columns], grown[i + half, :, columns]], axis=0)
                for i in range(half)
            ],
            axis=1,
        )
        mixed_ref[c] = by_seat(mix(values, halves(exps, lower, 0)))

    def mix_chunk(j, totals):
        part = pl.ds(pl.multiple_of(j * chunk, chunk), chunk)
        grew = []
        for c in range(kv_local):
            exps = jnp.exp(scores[c, part] - maxima[c])
            grew.append(totals[c] + fold_rows(exps, jnp.sum))
            mixed_ref[c] += mix(
                prompt[part, c * pair + HEAD_DIM : (c + 1) * pair], exps.astype(jnp.bfloat16)
            )
        return tuple(grew)

    totals = lax.fori_loop(0, chunks, mix_chunk, tuple(totals))
    weighted = jnp.zeros((base, HEAD_DIM), jnp.float32)
    for c in range(kv_local):
        mixed = (mixed_ref[c] / jnp.sum(totals[c], axis=0, keepdims=True)).T
        for h in range(group):
            weighted = (
                weighted + mixed[h * base : (h + 1) * base] * head_ref[c * group + h][None, :]
            )
    padding = jnp.zeros((HEAD_DIM - base, HEAD_DIM), jnp.float32)
    square = jnp.concatenate([weighted, padding], axis=0)
    row = jnp.sum(square.T, axis=0, keepdims=True) + extra_ref[...]
    share_ref[...] = jnp.broadcast_to(row[None], share_ref.shape)
    for home, copy in homes:
        pl.when(home)(copy.wait)


def attend(
    own_lengths, own_ancestors, queries, prompt_kv, gen_cache, new_kv, twist_vector, extra, devices
):
    steps, per_dev, width = queries.shape
    keys, kv_width = prompt_kv.shape
    rows = gen_cache.shape[1]
    kv_local = kv_width // (2 * HEAD_DIM)
    group = width // (kv_local * HEAD_DIM)
    lanes = steps * per_dev * group
    chunk = min(KEY_CHUNK, keys)
    head_weights = twist_vector.reshape(kv_local * group, HEAD_DIM)
    smem = pl.BlockSpec(memory_space=pltpu.SMEM)
    vmem = pl.BlockSpec(memory_space=pltpu.VMEM)
    hbm = pl.BlockSpec(memory_space=pltpu.HBM)
    score_count = lanes * kv_local * (keys + rows)
    return pl.pallas_call(
        functools.partial(attend_kernel, per_dev, group, kv_local, chunk),
        out_shape=[
            jax.ShapeDtypeStruct((devices, 1, HEAD_DIM), jnp.float32),
            jax.ShapeDtypeStruct(gen_cache.shape, jnp.bfloat16),
        ],
        in_specs=[smem, smem, vmem, hbm, hbm, vmem, vmem, vmem],
        out_specs=[vmem, hbm],
        scratch_shapes=[
            pltpu.VMEM(prompt_kv.shape, jnp.bfloat16),
            pltpu.VMEM(gen_cache.shape, jnp.bfloat16),
            pltpu.VMEM((steps * per_dev, kv_width), jnp.float32),
            pltpu.VMEM((kv_local, keys, lanes), jnp.float32),
            pltpu.VMEM((kv_local, HEAD_DIM, lanes), jnp.float32),
            pltpu.SemaphoreType.DMA((keys // chunk,)),
            pltpu.SemaphoreType.DMA((per_dev,)),
            pltpu.SemaphoreType.DMA((per_dev,)),
        ],
        compiler_params=pltpu.CompilerParams(vmem_limit_bytes=VMEM_BYTES),
        cost_estimate=pl.CostEstimate(
            flops=4 * score_count * HEAD_DIM,
            bytes_accessed=2 * (prompt_kv.size + 2 * gen_cache.size),
            transcendentals=score_count,
        ),
        name="attend",
    )(
        own_lengths,
        own_ancestors,
        queries,
        in_hbm(prompt_kv),
        in_hbm(gen_cache),
        new_kv,
        head_weights,
        extra,
    )


def finish_kernel(doms, tps, slot_ref, *refs):
    gots = refs[: len(ORDERS[0])]
    _, all_ref, out_ref, twist_ref, normal_ref, sums, sem = refs[len(gots) :]
    per_dev = out_ref.shape[0]
    for p in range(per_dev):
        slot = slot_ref[p]
        for k, got in enumerate(gots):
            for i in range(PICKS):
                copy = pltpu.make_async_copy(got.at[i], out_ref.at[p], sem.at[p])
                pl.when(slot == k * PICKS + i)(copy.start)
    for d in range(doms):
        row = all_ref[d * tps]
        for t in range(1, tps):
            row = row + all_ref[d * tps + t]
        sums[d : d + 1, :] = row
    step_0, step_1, prior = (
        slice(k * per_dev, (k + 1) * per_dev) for k in range(3)
    )
    totals = sums[...]
    log_weights = totals[:, prior] + totals[:, step_1] - totals[:, step_0]
    largest = jnp.max(log_weights, keepdims=True)
    log_total = largest + jnp.log(jnp.sum(jnp.exp(log_weights - largest), keepdims=True))
    mine = sums[pl.ds(lax.axis_index("dom"), 1), :]
    own = mine[:, prior] + mine[:, step_1] - mine[:, step_0]
    twist_ref[...] = jnp.concatenate([mine[:, step_0], mine[:, step_1]], axis=0)
    normal_ref[...] = own - log_total
    for p in range(per_dev):
        copy = pltpu.make_async_copy(gots[0].at[0], out_ref.at[p], sem.at[p])
        pl.when(slot_ref[p] >= 0)(copy.wait)


def finish(slots, gots, held, shares, doms, tps):
    per_dev = held.shape[0]
    count = len(gots)
    smem = pl.BlockSpec(memory_space=pltpu.SMEM)
    vmem = pl.BlockSpec(memory_space=pltpu.VMEM)
    hbm = pl.BlockSpec(memory_space=pl.ANY)
    return pl.pallas_call(
        functools.partial(finish_kernel, doms, tps),
        out_shape=[
            jax.ShapeDtypeStruct(held.shape, held.dtype),
            jax.ShapeDtypeStruct((2, per_dev), jnp.float32),
            jax.ShapeDtypeStruct((1, per_dev), jnp.float32),
        ],
        in_specs=[smem] + [vmem] * count + [hbm, vmem],
        out_specs=[hbm, vmem, vmem],
        input_output_aliases={1 + count: 0},
        scratch_shapes=[
            pltpu.VMEM((doms, HEAD_DIM), jnp.float32),
            pltpu.SemaphoreType.DMA((per_dev,)),
        ],
        compiler_params=pltpu.CompilerParams(vmem_limit_bytes=VMEM_BYTES),
        cost_estimate=pl.CostEstimate(
            flops=0, bytes_accessed=held.size, transcendentals=0
        ),
        name="finish",
    )(slots, *gots, held, shares)


def routes(doms, tps, steps):
    pairs = []
    for d in range(doms):
        for t in range(tps):
            target = d + steps[t % 2]
            if 0 <= target < doms:
                pairs.append((d * tps + t, target * tps + t))
    return pairs


def local(
    queries,
    new_kv,
    gen_cache,
    prompt_kv,
    lengths,
    ancestors,
    tokens,
    twist_vector,
    twist_bias,
    prior_weights,
):
    doms, tps = lax.axis_size("dom"), lax.axis_size("tp")
    per_dev = gen_cache.shape[0]
    step_pairs = list(zip(*ORDERS))
    everyone = ("dom", "tp")

    *sends, new_lengths, own_lengths, own_ancestors, slots = pack(
        lengths, ancestors, new_kv, gen_cache, doms, step_pairs
    )
    arrivals = [
        lax.ppermute(send, everyone, routes(doms, tps, steps))
        for send, steps in zip(sends, step_pairs)
    ]

    bias = jnp.take(twist_bias, tokens, axis=0).reshape(-1)
    extra = jnp.concatenate([bias, prior_weights])
    extra = jnp.where(lax.axis_index("tp") == 0, extra, 0.0)
    extra = jnp.pad(extra, (0, HEAD_DIM - extra.size))[None]
    shares, resampled = attend(
        own_lengths,
        own_ancestors,
        queries,
        prompt_kv,
        gen_cache,
        new_kv,
        twist_vector,
        extra,
        doms * tps,
    )
    shares = lax.all_to_all(shares, everyone, 0, 0, tiled=True)
    resampled, twist, normalized = finish(slots, arrivals, resampled, shares, doms, tps)
    return (twist, normalized.reshape(per_dev), resampled, new_lengths)


def solution(mesh):
    in_specs = (
        P(None, "dom", "tp"),
        P(None, "dom", "tp"),
        P("dom", None, "tp"),
        P(None, "tp"),
        P(),
        P(),
        P(None, "dom"),
        P("tp"),
        P(),
        P("dom"),
    )
    out_specs = (P(None, "dom"), P("dom"), P("dom", None, "tp"), P("dom"))
    return jax.shard_map(local, mesh=mesh, in_specs=in_specs, out_specs=out_specs, check_vma=False)
```

```python
import functools
import math

import jax
import jax.numpy as jnp
from jax import lax
from jax.experimental import pallas as pl
from jax.experimental.pallas import tpu as pltpu
from jax.sharding import PartitionSpec as P

HEAD_DIM = 128
SPAN = 2
PICKS = 2
NEG_FILL = -1e30
KEY_CHUNK = 512
VMEM_BYTES = 44 * 1024 * 1024
ROW_TILE = 16
WINDOW = 2 * ROW_TILE

ORDERS = ((-2, 2, 1, -1), (1, -1, -2, 2))


def in_hbm(x):
    return pltpu.with_memory_space_constraint(x, pltpu.HBM)


def place_new_rows(cache, new_rows, length, slot, per_dev):
    rows, width = cache.shape
    first = pl.multiple_of(
        jnp.minimum(length // ROW_TILE * ROW_TILE, rows - WINDOW), ROW_TILE
    )
    row_ids = first + lax.broadcasted_iota(jnp.int32, (WINDOW, width), 0)
    old = cache[pl.ds(first, WINDOW), :].astype(jnp.float32)
    later = jnp.where(row_ids == length + 1, new_rows[pl.ds(per_dev + slot, 1), :], 0.0)
    later = jnp.where(row_ids == length, new_rows[pl.ds(slot, 1), :], later)
    cache[pl.ds(first, WINDOW), :] = jnp.where(row_ids < length, old, later).astype(
        jnp.bfloat16
    )

    def clear(tile, carry):
        start = pl.multiple_of(tile * ROW_TILE, ROW_TILE)
        cache[pl.ds(start, ROW_TILE), :] = jnp.zeros((ROW_TILE, width), jnp.bfloat16)
        return carry

    lax.fori_loop(first // ROW_TILE + WINDOW // ROW_TILE, rows // ROW_TILE, clear, 0)


def named_range(anc_ref, first, owner, per_dev):
    low, high = jnp.int32(per_dev), jnp.int32(-1)
    for j in range(per_dev):
        local = anc_ref[first + j] - owner * per_dev
        named = jnp.logical_and(local >= 0, local < per_dev)
        low = jnp.minimum(low, jnp.where(named, local, per_dev))
        high = jnp.maximum(high, jnp.where(named, local, -1))
    return low, high


def pack_kernel(per_dev, doms, step_pairs, len_hbm, anc_hbm, new_hbm, gen_hbm, *refs):
    sends = refs[: len(step_pairs)]
    new_len_ref, own_len_ref, own_anc_ref, slot_ref = refs[len(step_pairs) : len(step_pairs) + 4]
    len_ref, anc_ref, new_bf16, new_rows, list_sem, load_sem = refs[len(step_pairs) + 4 :]
    lists = [
        pltpu.make_async_copy(anc_hbm, anc_ref, list_sem.at[0]),
        pltpu.make_async_copy(len_hbm, len_ref, list_sem.at[1]),
        pltpu.make_async_copy(new_hbm, new_bf16, list_sem.at[2]),
    ]
    for copy in lists:
        copy.start()
    me, odd = lax.axis_index("dom"), lax.axis_index("tp") % 2
    lists[0].wait()
    picks = []
    loads = []
    for k, (even_step, odd_step) in enumerate(step_pairs):
        reader = jnp.clip(me + jnp.where(odd == 1, odd_step, even_step), 0, doms - 1)
        low, high = named_range(anc_ref, reader * per_dev, me, per_dev)
        for i, pick in enumerate((jnp.minimum(low, per_dev - 1), jnp.maximum(high, 0))):
            target = sends[k].at[i]
            load = pltpu.make_async_copy(gen_hbm.at[pick], target, load_sem.at[len(loads)])
            load.start()
            picks.append((pick, target))
            loads.append(load)
    lists[1].wait()
    for j in range(per_dev):
        own_anc_ref[j] = anc_ref[me * per_dev + j]
        new_len_ref[j] = len_ref[anc_ref[me * per_dev + j]] + 2
        own_len_ref[j] = len_ref[me * per_dev + j]
        slot_ref[j] = -1
    for k, (even_step, odd_step) in enumerate(step_pairs):
        source = me - jnp.where(odd == 1, odd_step, even_step)
        low, _ = named_range(anc_ref, me * per_dev, source, per_dev)
        for j in range(per_dev):
            local = anc_ref[me * per_dev + j] - source * per_dev
            named = jnp.logical_and(local >= 0, local < per_dev)
            slot = k * PICKS + jnp.where(local == low, 0, PICKS - 1)
            slot_ref[j] = jnp.where(named, slot, slot_ref[j])
    lists[2].wait()
    new_rows[...] = new_bf16[...].astype(jnp.float32).reshape(new_rows.shape)
    for load, (pick, target) in zip(loads, picks):
        load.wait()
        place_new_rows(target, new_rows, len_ref[me * per_dev + pick], pick, per_dev)


def pack(lengths, ancestors, new_kv, gen_cache, doms, step_pairs):
    per_dev, rows, width = gen_cache.shape
    count = len(step_pairs)
    smem = pl.BlockSpec(memory_space=pltpu.SMEM)
    vmem = pl.BlockSpec(memory_space=pltpu.VMEM)
    hbm = pl.BlockSpec(memory_space=pltpu.HBM)
    block_bytes = PICKS * rows * width * 2
    return pl.pallas_call(
        functools.partial(pack_kernel, per_dev, doms, step_pairs),
        out_shape=[jax.ShapeDtypeStruct((PICKS, rows, width), jnp.bfloat16)] * count
        + [jax.ShapeDtypeStruct((per_dev,), jnp.int32)] * 4,
        in_specs=[hbm] * 4,
        out_specs=[vmem] * count + [smem] * 4,
        scratch_shapes=[
            pltpu.SMEM(lengths.shape, jnp.int32),
            pltpu.SMEM(ancestors.shape, jnp.int32),
            pltpu.VMEM(new_kv.shape, jnp.bfloat16),
            pltpu.VMEM((2 * per_dev, width), jnp.float32),
            pltpu.SemaphoreType.DMA((3,)),
            pltpu.SemaphoreType.DMA((count * PICKS,)),
        ],
        compiler_params=pltpu.CompilerParams(vmem_limit_bytes=VMEM_BYTES),
        cost_estimate=pl.CostEstimate(
            flops=0, bytes_accessed=2 * count * block_bytes, transcendentals=0
        ),
        name="pack_sends",
    )(*(in_hbm(x) for x in (lengths, ancestors, new_kv, gen_cache)))


def fold_lanes(block, combine, start):
    for first in range(0, block.shape[1], HEAD_DIM):
        start = combine(start, block[:, first : first + HEAD_DIM])
    return start


def attend_kernel(
    per_dev,
    group,
    kv_local,
    chunk,
    len_ref,
    anc_ref,
    q_ref,
    prompt_hbm,
    gen_hbm,
    new_ref,
    head_ref,
    extra_ref,
    share_ref,
    out_hbm,
    prompt,
    grown,
    new_rows,
    scores,
    tops,
    totals,
    mixed_ref,
    prompt_sem,
    gen_sem,
    out_sem,
):
    me = lax.axis_index("dom")
    steps = q_ref.shape[0]
    rows, width = grown.shape[1:]
    chunks = prompt.shape[0] // chunk
    pair = 2 * HEAD_DIM
    scale = 1.0 / math.sqrt(HEAD_DIM)
    base = steps * per_dev

    half = per_dev // 2
    per_chunk = per_dev // chunks

    def gen_load(p):
        return pltpu.make_async_copy(gen_hbm.at[p], grown.at[p], gen_sem.at[p])

    def prompt_load(j):
        part = pl.ds(pl.multiple_of(j * chunk, chunk), chunk)
        return pltpu.make_async_copy(prompt_hbm.at[part], prompt.at[part], prompt_sem.at[j])

    for j in range(chunks):
        prompt_load(j).start()
        for i in range(per_chunk):
            gen_load(j * per_chunk + i).start()

    new_rows[...] = new_ref[...].astype(jnp.float32).reshape(base, width)
    row_ids = lax.broadcasted_iota(jnp.int32, (rows, width), 0)

    def patch(p):
        gen_load(p).wait()
        behind = row_ids - len_ref[p]
        tail = jnp.where(behind == 1, new_rows[pl.ds(per_dev + p, 1), :], 0.0)
        tail = jnp.where(behind == 0, new_rows[pl.ds(p, 1), :], tail)
        grown[p] = jnp.where(behind < 0, grown[p].astype(jnp.float32), tail).astype(
            jnp.bfloat16
        )

    q2 = q_ref[...].reshape(base, q_ref.shape[-1])
    queries = [
        jnp.concatenate(
            [q2[:, h * HEAD_DIM : (h + 1) * HEAD_DIM] for h in range(c * group, (c + 1) * group)],
            axis=0,
        )
        for c in range(kv_local)
    ]

    def score(query_rows, keys):
        return lax.dot_general(
            query_rows, keys, (((1,), (1,)), ((), ())), preferred_element_type=jnp.float32
        )

    def mix(probs, values):
        return jnp.dot(probs, values, preferred_element_type=jnp.float32)

    tops[...] = jnp.full(tops.shape, NEG_FILL, jnp.float32)

    def score_chunk(j, carry):
        prompt_load(j).wait()
        part = pl.ds(pl.multiple_of(j * chunk, chunk), chunk)
        for c in range(kv_local):
            block = score(queries[c], prompt[part, c * pair : c * pair + HEAD_DIM]) * scale
            scores[c, j] = block
            tops[c] = fold_lanes(block, jnp.maximum, tops[c])
        for i in range(per_chunk):
            patch(j * per_chunk + i)
        return carry

    lax.fori_loop(0, chunks, score_chunk, 0)

    homes = []
    for p in range(per_dev):
        local = anc_ref[p] - me * per_dev
        home = jnp.logical_and(local >= 0, local < per_dev)
        source = grown.at[jnp.clip(local, 0, per_dev - 1)]
        copy = pltpu.make_async_copy(source, out_hbm.at[p], out_sem.at[p])
        homes.append((home, copy))
        pl.when(home)(copy.start)

    row_ids = lax.broadcasted_iota(jnp.int32, (base, rows), 0)
    owner = row_ids % per_dev
    last = row_ids // per_dev
    for p in range(per_dev):
        last = last + jnp.where(owner == p, len_ref[p], 0)
    visible = lax.broadcasted_iota(jnp.int32, (base, rows), 1) <= last
    visible, lower, seat = (
        jnp.concatenate([part.astype(jnp.int32)] * group, axis=0)
        for part in (visible, owner < half, owner % half)
    )
    visible, lower = visible == 1, lower == 1

    def halves(block):
        block = block.astype(jnp.float32)
        parts = [jnp.where(lower, block, 0.0), jnp.where(lower, 0.0, block)]
        return jnp.concatenate(parts, axis=1).astype(jnp.bfloat16)

    def by_seat(blocks):
        chosen = blocks[:, :HEAD_DIM]
        for i in range(1, half):
            chosen = jnp.where(seat == i, blocks[:, i * HEAD_DIM : (i + 1) * HEAD_DIM], chosen)
        return chosen

    for c in range(kv_local):
        columns = slice(c * pair, c * pair + HEAD_DIM)
        keys = jnp.concatenate(
            [
                jnp.concatenate([grown[i, :, columns], grown[i + half, :, columns]], axis=1)
                for i in range(half)
            ],
            axis=0,
        )
        own = jnp.where(visible, by_seat(score(halves(queries[c]), keys)) * scale, NEG_FILL)
        top = jnp.max(jnp.maximum(tops[c], own), axis=1, keepdims=True)
        top = jnp.broadcast_to(top, own.shape)
        tops[c] = top
        exps = jnp.where(visible, jnp.exp(own - top), 0.0)
        totals[c] = exps
        columns = slice(c * pair + HEAD_DIM, (c + 1) * pair)
        values = jnp.concatenate(
            [
                jnp.concatenate([grown[i, :, columns], grown[i + half, :, columns]], axis=0)
                for i in range(half)
            ],
            axis=1,
        )
        mixed_ref[c] = by_seat(mix(halves(exps), values))

    def mix_chunk(j, carry):
        part = pl.ds(pl.multiple_of(j * chunk, chunk), chunk)
        for c in range(kv_local):
            top = jnp.concatenate([tops[c]] * (chunk // HEAD_DIM), axis=1)
            exps = jnp.exp(scores[c, j] - top)
            totals[c] = fold_lanes(exps, jnp.add, totals[c])
            mixed_ref[c] += mix(
                exps.astype(jnp.bfloat16), prompt[part, c * pair + HEAD_DIM : (c + 1) * pair]
            )
        return carry

    lax.fori_loop(0, chunks, mix_chunk, 0)
    weighted = jnp.zeros((base, HEAD_DIM), jnp.float32)
    for c in range(kv_local):
        mixed = mixed_ref[c] / jnp.sum(totals[c], axis=1, keepdims=True)
        for h in range(group):
            weighted = (
                weighted + mixed[h * base : (h + 1) * base] * head_ref[c * group + h][None, :]
            )
    padding = jnp.zeros((HEAD_DIM - base, HEAD_DIM), jnp.float32)
    square = jnp.concatenate([weighted, padding], axis=0)
    row = jnp.sum(square.T, axis=0, keepdims=True) + extra_ref[...]
    share_ref[...] = jnp.broadcast_to(row[None], share_ref.shape)
    for home, copy in homes:
        pl.when(home)(copy.wait)


def attend(
    own_lengths, own_ancestors, queries, prompt_kv, gen_cache, new_kv, twist_vector, extra, devices
):
    steps, per_dev, width = queries.shape
    keys, kv_width = prompt_kv.shape
    rows = gen_cache.shape[1]
    kv_local = kv_width // (2 * HEAD_DIM)
    group = width // (kv_local * HEAD_DIM)
    score_rows = steps * per_dev * group
    chunk = min(KEY_CHUNK, keys)
    head_weights = twist_vector.reshape(kv_local * group, HEAD_DIM)
    smem = pl.BlockSpec(memory_space=pltpu.SMEM)
    vmem = pl.BlockSpec(memory_space=pltpu.VMEM)
    hbm = pl.BlockSpec(memory_space=pltpu.HBM)
    score_count = score_rows * kv_local * (keys + rows)
    return pl.pallas_call(
        functools.partial(attend_kernel, per_dev, group, kv_local, chunk),
        out_shape=[
            jax.ShapeDtypeStruct((devices, 1, HEAD_DIM), jnp.float32),
            jax.ShapeDtypeStruct(gen_cache.shape, jnp.bfloat16),
        ],
        in_specs=[smem, smem, vmem, hbm, hbm, vmem, vmem, vmem],
        out_specs=[vmem, hbm],
        scratch_shapes=[
            pltpu.VMEM(prompt_kv.shape, jnp.bfloat16),
            pltpu.VMEM(gen_cache.shape, jnp.bfloat16),
            pltpu.VMEM((steps * per_dev, kv_width), jnp.float32),
            pltpu.VMEM((kv_local, keys // chunk, score_rows, chunk), jnp.float32),
            pltpu.VMEM((kv_local, score_rows, HEAD_DIM), jnp.float32),
            pltpu.VMEM((kv_local, score_rows, HEAD_DIM), jnp.float32),
            pltpu.VMEM((kv_local, score_rows, HEAD_DIM), jnp.float32),
            pltpu.SemaphoreType.DMA((keys // chunk,)),
            pltpu.SemaphoreType.DMA((per_dev,)),
            pltpu.SemaphoreType.DMA((per_dev,)),
        ],
        compiler_params=pltpu.CompilerParams(vmem_limit_bytes=VMEM_BYTES),
        cost_estimate=pl.CostEstimate(
            flops=4 * score_count * HEAD_DIM,
            bytes_accessed=2 * (prompt_kv.size + 2 * gen_cache.size),
            transcendentals=score_count,
        ),
        name="attend",
    )(
        own_lengths,
        own_ancestors,
        queries,
        in_hbm(prompt_kv),
        in_hbm(gen_cache),
        new_kv,
        head_weights,
        extra,
    )


def finish_kernel(doms, tps, slot_ref, *refs):
    gots = refs[: len(ORDERS[0])]
    _, all_ref, out_ref, twist_ref, normal_ref, sums, sem = refs[len(gots) :]
    per_dev = out_ref.shape[0]
    for p in range(per_dev):
        slot = slot_ref[p]
        for k, got in enumerate(gots):
            for i in range(PICKS):
                copy = pltpu.make_async_copy(got.at[i], out_ref.at[p], sem.at[p])
                pl.when(slot == k * PICKS + i)(copy.start)
    for d in range(doms):
        row = all_ref[d * tps]
        for t in range(1, tps):
            row = row + all_ref[d * tps + t]
        sums[d : d + 1, :] = row
    step_0, step_1, prior = (
        slice(k * per_dev, (k + 1) * per_dev) for k in range(3)
    )
    totals = sums[...]
    log_weights = totals[:, prior] + totals[:, step_1] - totals[:, step_0]
    largest = jnp.max(log_weights, keepdims=True)
    log_total = largest + jnp.log(jnp.sum(jnp.exp(log_weights - largest), keepdims=True))
    mine = sums[pl.ds(lax.axis_index("dom"), 1), :]
    own = mine[:, prior] + mine[:, step_1] - mine[:, step_0]
    twist_ref[...] = jnp.concatenate([mine[:, step_0], mine[:, step_1]], axis=0)
    normal_ref[...] = own - log_total
    for p in range(per_dev):
        copy = pltpu.make_async_copy(gots[0].at[0], out_ref.at[p], sem.at[p])
        pl.when(slot_ref[p] >= 0)(copy.wait)


def finish(slots, gots, held, shares, doms, tps):
    per_dev = held.shape[0]
    count = len(gots)
    smem = pl.BlockSpec(memory_space=pltpu.SMEM)
    vmem = pl.BlockSpec(memory_space=pltpu.VMEM)
    hbm = pl.BlockSpec(memory_space=pl.ANY)
    return pl.pallas_call(
        functools.partial(finish_kernel, doms, tps),
        out_shape=[
            jax.ShapeDtypeStruct(held.shape, held.dtype),
            jax.ShapeDtypeStruct((2, per_dev), jnp.float32),
            jax.ShapeDtypeStruct((1, per_dev), jnp.float32),
        ],
        in_specs=[smem] + [vmem] * count + [hbm, vmem],
        out_specs=[hbm, vmem, vmem],
        input_output_aliases={1 + count: 0},
        scratch_shapes=[
            pltpu.VMEM((doms, HEAD_DIM), jnp.float32),
            pltpu.SemaphoreType.DMA((per_dev,)),
        ],
        compiler_params=pltpu.CompilerParams(vmem_limit_bytes=VMEM_BYTES),
        cost_estimate=pl.CostEstimate(
            flops=0, bytes_accessed=held.size, transcendentals=0
        ),
        name="finish",
    )(slots, *gots, held, shares)


def routes(doms, tps, steps):
    pairs = []
    for d in range(doms):
        for t in range(tps):
            target = d + steps[t % 2]
            if 0 <= target < doms:
                pairs.append((d * tps + t, target * tps + t))
    return pairs


def local(
    queries,
    new_kv,
    gen_cache,
    prompt_kv,
    lengths,
    ancestors,
    tokens,
    twist_vector,
    twist_bias,
    prior_weights,
):
    doms, tps = lax.axis_size("dom"), lax.axis_size("tp")
    per_dev = gen_cache.shape[0]
    step_pairs = list(zip(*ORDERS))
    everyone = ("dom", "tp")

    *sends, new_lengths, own_lengths, own_ancestors, slots = pack(
        lengths, ancestors, new_kv, gen_cache, doms, step_pairs
    )
    arrivals = [
        lax.ppermute(send, everyone, routes(doms, tps, steps))
        for send, steps in zip(sends, step_pairs)
    ]

    bias = jnp.take(twist_bias, tokens, axis=0).reshape(-1)
    extra = jnp.concatenate([bias, prior_weights])
    extra = jnp.where(lax.axis_index("tp") == 0, extra, 0.0)
    extra = jnp.pad(extra, (0, HEAD_DIM - extra.size))[None]
    shares, resampled = attend(
        own_lengths,
        own_ancestors,
        queries,
        prompt_kv,
        gen_cache,
        new_kv,
        twist_vector,
        extra,
        doms * tps,
    )
    shares = lax.all_to_all(shares, everyone, 0, 0, tiled=True)
    resampled, twist, normalized = finish(slots, arrivals, resampled, shares, doms, tps)
    return (twist, normalized.reshape(per_dev), resampled, new_lengths)


def solution(mesh):
    in_specs = (
        P(None, "dom", "tp"),
        P(None, "dom", "tp"),
        P("dom", None, "tp"),
        P(None, "tp"),
        P(),
        P(),
        P(None, "dom"),
        P("tp"),
        P(),
        P("dom"),
    )
    out_specs = (P(None, "dom"), P("dom"), P("dom", None, "tp"), P("dom"))
    return jax.shard_map(local, mesh=mesh, in_specs=in_specs, out_specs=out_specs, check_vma=False)
```

```python
import functools
import math

import jax
import jax.numpy as jnp
from jax import lax
from jax.experimental import pallas as pl
from jax.experimental.pallas import tpu as pltpu
from jax.sharding import PartitionSpec as P

HEAD_DIM = 128
SPAN = 2
PICKS = 2
NEG_FILL = -1e30
LOG2_E = math.log2(math.e)
KEY_CHUNK = 512
VMEM_BYTES = 44 * 1024 * 1024
ROW_TILE = 16
WINDOW = 2 * ROW_TILE

ORDERS = ((-2, 2, 1, -1), (1, -1, -2, 2))


def in_hbm(x):
    return pltpu.with_memory_space_constraint(x, pltpu.HBM)


def place_new_rows(cache, new_rows, length, slot, per_dev):
    rows, width = cache.shape
    first = pl.multiple_of(
        jnp.minimum(length // ROW_TILE * ROW_TILE, rows - WINDOW), ROW_TILE
    )
    row_ids = first + lax.broadcasted_iota(jnp.int32, (WINDOW, width), 0)
    old = cache[pl.ds(first, WINDOW), :].astype(jnp.float32)
    later = jnp.where(row_ids == length + 1, new_rows[pl.ds(per_dev + slot, 1), :], 0.0)
    later = jnp.where(row_ids == length, new_rows[pl.ds(slot, 1), :], later)
    cache[pl.ds(first, WINDOW), :] = jnp.where(row_ids < length, old, later).astype(
        jnp.bfloat16
    )

    def clear(tile, carry):
        start = pl.multiple_of(tile * ROW_TILE, ROW_TILE)
        cache[pl.ds(start, ROW_TILE), :] = jnp.zeros((ROW_TILE, width), jnp.bfloat16)
        return carry

    lax.fori_loop(first // ROW_TILE + WINDOW // ROW_TILE, rows // ROW_TILE, clear, 0)


def named_range(anc_ref, first, owner, per_dev):
    low, high = jnp.int32(per_dev), jnp.int32(-1)
    for j in range(per_dev):
        local = anc_ref[first + j] - owner * per_dev
        named = jnp.logical_and(local >= 0, local < per_dev)
        low = jnp.minimum(low, jnp.where(named, local, per_dev))
        high = jnp.maximum(high, jnp.where(named, local, -1))
    return low, high


def pack_kernel(per_dev, doms, step_pairs, len_hbm, anc_hbm, new_hbm, gen_hbm, *refs):
    sends = refs[: len(step_pairs)]
    new_len_ref, own_len_ref, own_anc_ref, slot_ref = refs[len(step_pairs) : len(step_pairs) + 4]
    len_ref, anc_ref, new_bf16, new_rows, list_sem, load_sem = refs[len(step_pairs) + 4 :]
    lists = [
        pltpu.make_async_copy(anc_hbm, anc_ref, list_sem.at[0]),
        pltpu.make_async_copy(len_hbm, len_ref, list_sem.at[1]),
        pltpu.make_async_copy(new_hbm, new_bf16, list_sem.at[2]),
    ]
    for copy in lists:
        copy.start()
    me, odd = lax.axis_index("dom"), lax.axis_index("tp") % 2
    lists[0].wait()
    picks = []
    loads = []
    for k, (even_step, odd_step) in enumerate(step_pairs):
        reader = jnp.clip(me + jnp.where(odd == 1, odd_step, even_step), 0, doms - 1)
        low, high = named_range(anc_ref, reader * per_dev, me, per_dev)
        for i, pick in enumerate((jnp.minimum(low, per_dev - 1), jnp.maximum(high, 0))):
            target = sends[k].at[i]
            load = pltpu.make_async_copy(gen_hbm.at[pick], target, load_sem.at[len(loads)])
            load.start()
            picks.append((pick, target))
            loads.append(load)
    lists[1].wait()
    for j in range(per_dev):
        own_anc_ref[j] = anc_ref[me * per_dev + j]
        new_len_ref[j] = len_ref[anc_ref[me * per_dev + j]] + 2
        own_len_ref[j] = len_ref[me * per_dev + j]
        slot_ref[j] = -1
    for k, (even_step, odd_step) in enumerate(step_pairs):
        source = me - jnp.where(odd == 1, odd_step, even_step)
        low, _ = named_range(anc_ref, me * per_dev, source, per_dev)
        for j in range(per_dev):
            local = anc_ref[me * per_dev + j] - source * per_dev
            named = jnp.logical_and(local >= 0, local < per_dev)
            slot = k * PICKS + jnp.where(local == low, 0, PICKS - 1)
            slot_ref[j] = jnp.where(named, slot, slot_ref[j])
    lists[2].wait()
    new_rows[...] = new_bf16[...].astype(jnp.float32).reshape(new_rows.shape)
    for load, (pick, target) in zip(loads, picks):
        load.wait()
        place_new_rows(target, new_rows, len_ref[me * per_dev + pick], pick, per_dev)


def pack(lengths, ancestors, new_kv, gen_cache, doms, step_pairs):
    per_dev, rows, width = gen_cache.shape
    count = len(step_pairs)
    smem = pl.BlockSpec(memory_space=pltpu.SMEM)
    vmem = pl.BlockSpec(memory_space=pltpu.VMEM)
    hbm = pl.BlockSpec(memory_space=pltpu.HBM)
    block_bytes = PICKS * rows * width * 2
    return pl.pallas_call(
        functools.partial(pack_kernel, per_dev, doms, step_pairs),
        out_shape=[jax.ShapeDtypeStruct((PICKS, rows, width), jnp.bfloat16)] * count
        + [jax.ShapeDtypeStruct((per_dev,), jnp.int32)] * 4,
        in_specs=[hbm] * 4,
        out_specs=[vmem] * count + [smem] * 4,
        scratch_shapes=[
            pltpu.SMEM(lengths.shape, jnp.int32),
            pltpu.SMEM(ancestors.shape, jnp.int32),
            pltpu.VMEM(new_kv.shape, jnp.bfloat16),
            pltpu.VMEM((2 * per_dev, width), jnp.float32),
            pltpu.SemaphoreType.DMA((3,)),
            pltpu.SemaphoreType.DMA((count * PICKS,)),
        ],
        compiler_params=pltpu.CompilerParams(vmem_limit_bytes=VMEM_BYTES),
        cost_estimate=pl.CostEstimate(
            flops=0, bytes_accessed=2 * count * block_bytes, transcendentals=0
        ),
        name="pack_sends",
    )(*(in_hbm(x) for x in (lengths, ancestors, new_kv, gen_cache)))


def fold_lanes(block, combine, start):
    for first in range(0, block.shape[1], HEAD_DIM):
        start = combine(start, block[:, first : first + HEAD_DIM])
    return start


def attend_kernel(
    per_dev,
    group,
    kv_local,
    chunk,
    len_ref,
    anc_ref,
    q_ref,
    prompt_hbm,
    gen_hbm,
    new_ref,
    head_ref,
    extra_ref,
    share_ref,
    out_hbm,
    prompt,
    grown,
    new_rows,
    scores,
    tops,
    totals,
    mixed_ref,
    prompt_sem,
    gen_sem,
    out_sem,
):
    me = lax.axis_index("dom")
    steps = q_ref.shape[0]
    rows, width = grown.shape[1:]
    chunks = prompt.shape[0] // chunk
    pair = 2 * HEAD_DIM
    scale = LOG2_E / math.sqrt(HEAD_DIM)
    base = steps * per_dev

    half = per_dev // 2
    per_chunk = per_dev // chunks

    def gen_load(p):
        return pltpu.make_async_copy(gen_hbm.at[p], grown.at[p], gen_sem.at[p])

    def prompt_load(j):
        part = pl.ds(pl.multiple_of(j * chunk, chunk), chunk)
        return pltpu.make_async_copy(prompt_hbm.at[part], prompt.at[part], prompt_sem.at[j])

    for j in range(chunks):
        prompt_load(j).start()
        for i in range(per_chunk):
            gen_load(j * per_chunk + i).start()

    new_rows[...] = new_ref[...].astype(jnp.float32).reshape(base, width)
    row_ids = lax.broadcasted_iota(jnp.int32, (rows, width), 0)

    def patch(p):
        gen_load(p).wait()
        behind = row_ids - len_ref[p]
        tail = jnp.where(behind == 1, new_rows[pl.ds(per_dev + p, 1), :], 0.0)
        tail = jnp.where(behind == 0, new_rows[pl.ds(p, 1), :], tail)
        grown[p] = jnp.where(behind < 0, grown[p].astype(jnp.float32), tail).astype(
            jnp.bfloat16
        )

    q2 = q_ref[...].reshape(base, q_ref.shape[-1])
    queries = [
        jnp.concatenate(
            [q2[:, h * HEAD_DIM : (h + 1) * HEAD_DIM] for h in range(c * group, (c + 1) * group)],
            axis=0,
        )
        for c in range(kv_local)
    ]

    def score(query_rows, keys):
        return lax.dot_general(
            query_rows, keys, (((1,), (1,)), ((), ())), preferred_element_type=jnp.float32
        )

    def mix(probs, values):
        return jnp.dot(probs, values, preferred_element_type=jnp.float32)

    tops[...] = jnp.full(tops.shape, NEG_FILL, jnp.float32)

    def score_chunk(j, carry):
        prompt_load(j).wait()
        part = pl.ds(pl.multiple_of(j * chunk, chunk), chunk)
        for c in range(kv_local):
            block = score(queries[c], prompt[part, c * pair : c * pair + HEAD_DIM])
            scores[c, j] = block
            tops[c] = fold_lanes(block, jnp.maximum, tops[c])
        for i in range(per_chunk):
            patch(j * per_chunk + i)
        return carry

    lax.fori_loop(0, chunks, score_chunk, 0)

    homes = []
    for p in range(per_dev):
        local = anc_ref[p] - me * per_dev
        home = jnp.logical_and(local >= 0, local < per_dev)
        source = grown.at[jnp.clip(local, 0, per_dev - 1)]
        copy = pltpu.make_async_copy(source, out_hbm.at[p], out_sem.at[p])
        homes.append((home, copy))
        pl.when(home)(copy.start)

    row_ids = lax.broadcasted_iota(jnp.int32, (base, rows), 0)
    owner = row_ids % per_dev
    last = row_ids // per_dev
    for p in range(per_dev):
        last = last + jnp.where(owner == p, len_ref[p], 0)
    visible = lax.broadcasted_iota(jnp.int32, (base, rows), 1) <= last
    visible, lower, seat = (
        jnp.concatenate([part.astype(jnp.int32)] * group, axis=0)
        for part in (visible, owner < half, owner % half)
    )
    visible, lower = visible == 1, lower == 1

    def halves(block):
        block = block.astype(jnp.float32)
        parts = [jnp.where(lower, block, 0.0), jnp.where(lower, 0.0, block)]
        return jnp.concatenate(parts, axis=1).astype(jnp.bfloat16)

    def by_seat(blocks):
        chosen = blocks[:, :HEAD_DIM]
        for i in range(1, half):
            chosen = jnp.where(seat == i, blocks[:, i * HEAD_DIM : (i + 1) * HEAD_DIM], chosen)
        return chosen

    for c in range(kv_local):
        columns = slice(c * pair, c * pair + HEAD_DIM)
        keys = jnp.concatenate(
            [
                jnp.concatenate([grown[i, :, columns], grown[i + half, :, columns]], axis=1)
                for i in range(half)
            ],
            axis=0,
        )
        own = jnp.where(visible, by_seat(score(halves(queries[c]), keys)), NEG_FILL)
        top = jnp.max(jnp.maximum(tops[c], own), axis=1, keepdims=True)
        top = jnp.broadcast_to(top, own.shape)
        tops[c] = top
        exps = jnp.where(visible, jnp.exp2((own - top) * scale), 0.0)
        totals[c] = exps
        columns = slice(c * pair + HEAD_DIM, (c + 1) * pair)
        values = jnp.concatenate(
            [
                jnp.concatenate([grown[i, :, columns], grown[i + half, :, columns]], axis=0)
                for i in range(half)
            ],
            axis=1,
        )
        mixed_ref[c] = by_seat(mix(halves(exps), values))

    def mix_chunk(j, carry):
        part = pl.ds(pl.multiple_of(j * chunk, chunk), chunk)
        for c in range(kv_local):
            top = jnp.concatenate([tops[c]] * (chunk // HEAD_DIM), axis=1)
            exps = jnp.exp2((scores[c, j] - top) * scale)
            totals[c] = fold_lanes(exps, jnp.add, totals[c])
            mixed_ref[c] += mix(
                exps.astype(jnp.bfloat16), prompt[part, c * pair + HEAD_DIM : (c + 1) * pair]
            )
        return carry

    lax.fori_loop(0, chunks, mix_chunk, 0)
    weighted = jnp.zeros((base, HEAD_DIM), jnp.float32)
    for c in range(kv_local):
        mixed = mixed_ref[c] / jnp.sum(totals[c], axis=1, keepdims=True)
        for h in range(group):
            weighted = (
                weighted + mixed[h * base : (h + 1) * base] * head_ref[c * group + h][None, :]
            )
    padding = jnp.zeros((HEAD_DIM - base, HEAD_DIM), jnp.float32)
    square = jnp.concatenate([weighted, padding], axis=0)
    row = jnp.sum(square.T, axis=0, keepdims=True) + extra_ref[...]
    share_ref[...] = jnp.broadcast_to(row[None], share_ref.shape)
    for home, copy in homes:
        pl.when(home)(copy.wait)


def attend(
    own_lengths, own_ancestors, queries, prompt_kv, gen_cache, new_kv, twist_vector, extra, devices
):
    steps, per_dev, width = queries.shape
    keys, kv_width = prompt_kv.shape
    rows = gen_cache.shape[1]
    kv_local = kv_width // (2 * HEAD_DIM)
    group = width // (kv_local * HEAD_DIM)
    score_rows = steps * per_dev * group
    chunk = min(KEY_CHUNK, keys)
    head_weights = twist_vector.reshape(kv_local * group, HEAD_DIM)
    smem = pl.BlockSpec(memory_space=pltpu.SMEM)
    vmem = pl.BlockSpec(memory_space=pltpu.VMEM)
    hbm = pl.BlockSpec(memory_space=pltpu.HBM)
    score_count = score_rows * kv_local * (keys + rows)
    return pl.pallas_call(
        functools.partial(attend_kernel, per_dev, group, kv_local, chunk),
        out_shape=[
            jax.ShapeDtypeStruct((devices, 1, HEAD_DIM), jnp.float32),
            jax.ShapeDtypeStruct(gen_cache.shape, jnp.bfloat16),
        ],
        in_specs=[smem, smem, vmem, hbm, hbm, vmem, vmem, vmem],
        out_specs=[vmem, hbm],
        scratch_shapes=[
            pltpu.VMEM(prompt_kv.shape, jnp.bfloat16),
            pltpu.VMEM(gen_cache.shape, jnp.bfloat16),
            pltpu.VMEM((steps * per_dev, kv_width), jnp.float32),
            pltpu.VMEM((kv_local, keys // chunk, score_rows, chunk), jnp.float32),
            pltpu.VMEM((kv_local, score_rows, HEAD_DIM), jnp.float32),
            pltpu.VMEM((kv_local, score_rows, HEAD_DIM), jnp.float32),
            pltpu.VMEM((kv_local, score_rows, HEAD_DIM), jnp.float32),
            pltpu.SemaphoreType.DMA((keys // chunk,)),
            pltpu.SemaphoreType.DMA((per_dev,)),
            pltpu.SemaphoreType.DMA((per_dev,)),
        ],
        compiler_params=pltpu.CompilerParams(vmem_limit_bytes=VMEM_BYTES),
        cost_estimate=pl.CostEstimate(
            flops=4 * score_count * HEAD_DIM,
            bytes_accessed=2 * (prompt_kv.size + 2 * gen_cache.size),
            transcendentals=score_count,
        ),
        name="attend",
    )(
        own_lengths,
        own_ancestors,
        queries,
        in_hbm(prompt_kv),
        in_hbm(gen_cache),
        new_kv,
        head_weights,
        extra,
    )


def deliver_kernel(slot_ref, *refs):
    gots = refs[: len(ORDERS[0])]
    _, _, out_ref, _, sem = refs[len(gots) :]
    per_dev = out_ref.shape[0]
    for p in range(per_dev):
        slot = slot_ref[p]
        for k, got in enumerate(gots):
            for i in range(PICKS):
                copy = pltpu.make_async_copy(got.at[i], out_ref.at[p], sem.at[p])
                pl.when(slot == k * PICKS + i)(copy.start)
    for p in range(per_dev):
        copy = pltpu.make_async_copy(gots[0].at[0], out_ref.at[p], sem.at[p])
        pl.when(slot_ref[p] >= 0)(copy.wait)


def deliver(slots, gots, held, shares):
    smem = pl.BlockSpec(memory_space=pltpu.SMEM)
    vmem = pl.BlockSpec(memory_space=pltpu.VMEM)
    hbm = pl.BlockSpec(memory_space=pl.ANY)
    return pl.pallas_call(
        deliver_kernel,
        out_shape=[
            jax.ShapeDtypeStruct(held.shape, held.dtype),
            jax.ShapeDtypeStruct(shares.shape, shares.dtype),
        ],
        in_specs=[smem] + [vmem] * len(gots) + [hbm, hbm],
        out_specs=[hbm, hbm],
        input_output_aliases={1 + len(gots): 0, 2 + len(gots): 1},
        scratch_shapes=[pltpu.SemaphoreType.DMA((held.shape[0],))],
        compiler_params=pltpu.CompilerParams(vmem_limit_bytes=VMEM_BYTES),
        cost_estimate=pl.CostEstimate(
            flops=0, bytes_accessed=held.size, transcendentals=0
        ),
        name="deliver",
    )(slots, *gots, held, shares)


def normalize_kernel(doms, tps, all_ref, twist_ref, normal_ref, sums):
    per_dev = normal_ref.shape[1]
    for d in range(doms):
        row = all_ref[d * tps]
        for t in range(1, tps):
            row = row + all_ref[d * tps + t]
        sums[d : d + 1, :] = row
    step_0, step_1, prior = (
        slice(k * per_dev, (k + 1) * per_dev) for k in range(3)
    )
    totals = sums[...]
    log_weights = totals[:, prior] + totals[:, step_1] - totals[:, step_0]
    largest = jnp.max(log_weights, keepdims=True)
    log_total = largest + jnp.log(jnp.sum(jnp.exp(log_weights - largest), keepdims=True))
    mine = sums[pl.ds(lax.axis_index("dom"), 1), :]
    own = mine[:, prior] + mine[:, step_1] - mine[:, step_0]
    twist_ref[...] = jnp.concatenate([mine[:, step_0], mine[:, step_1]], axis=0)
    normal_ref[...] = own - log_total


def normalize(shares, doms, tps, per_dev):
    return pl.pallas_call(
        functools.partial(normalize_kernel, doms, tps),
        out_shape=[
            jax.ShapeDtypeStruct((2, per_dev), jnp.float32),
            jax.ShapeDtypeStruct((1, per_dev), jnp.float32),
        ],
        scratch_shapes=[pltpu.VMEM((doms, HEAD_DIM), jnp.float32)],
        name="normalize",
    )(shares)


def routes(doms, tps, steps):
    pairs = []
    for d in range(doms):
        for t in range(tps):
            target = d + steps[t % 2]
            if 0 <= target < doms:
                pairs.append((d * tps + t, target * tps + t))
    return pairs


def local(
    queries,
    new_kv,
    gen_cache,
    prompt_kv,
    lengths,
    ancestors,
    tokens,
    twist_vector,
    twist_bias,
    prior_weights,
):
    doms, tps = lax.axis_size("dom"), lax.axis_size("tp")
    per_dev = gen_cache.shape[0]
    step_pairs = list(zip(*ORDERS))
    everyone = ("dom", "tp")

    *sends, new_lengths, own_lengths, own_ancestors, slots = pack(
        lengths, ancestors, new_kv, gen_cache, doms, step_pairs
    )
    arrivals = [
        lax.ppermute(send, everyone, routes(doms, tps, steps))
        for send, steps in zip(sends, step_pairs)
    ]

    bias = jnp.take(twist_bias, tokens, axis=0).reshape(-1)
    extra = jnp.concatenate([bias, prior_weights])
    extra = jnp.where(lax.axis_index("tp") == 0, extra, 0.0)
    extra = jnp.pad(extra, (0, HEAD_DIM - extra.size))[None]
    shares, resampled = attend(
        own_lengths,
        own_ancestors,
        queries,
        prompt_kv,
        gen_cache,
        new_kv,
        twist_vector,
        extra,
        doms * tps,
    )
    resampled, shares = deliver(slots, arrivals, resampled, shares)
    shares = lax.all_to_all(shares, everyone, 0, 0, tiled=True)
    twist, normalized = normalize(shares, doms, tps, per_dev)
    return (twist, normalized.reshape(per_dev), resampled, new_lengths)


def solution(mesh):
    in_specs = (
        P(None, "dom", "tp"),
        P(None, "dom", "tp"),
        P("dom", None, "tp"),
        P(None, "tp"),
        P(),
        P(),
        P(None, "dom"),
        P("tp"),
        P(),
        P("dom"),
    )
    out_specs = (P(None, "dom"), P("dom"), P("dom", None, "tp"), P("dom"))
    return jax.shard_map(local, mesh=mesh, in_specs=in_specs, out_specs=out_specs, check_vma=False)
```

```python
import functools
import math

import jax
import jax.numpy as jnp
from jax import lax
from jax.experimental import pallas as pl
from jax.experimental.pallas import tpu as pltpu
from jax.sharding import PartitionSpec as P

HEAD_DIM = 128
SPAN = 2
PICKS = 2
NEG_FILL = -1e30
LOG2_E = math.log2(math.e)
KEY_CHUNK = 1024
VMEM_BYTES = 44 * 1024 * 1024
ROW_TILE = 16
WINDOW = 2 * ROW_TILE

ORDERS = ((-2, 2, 1, -1), (1, -1, -2, 2))


def in_hbm(x):
    return pltpu.with_memory_space_constraint(x, pltpu.HBM)


def place_new_rows(cache, new_rows, length, slot, per_dev):
    rows, width = cache.shape
    first = pl.multiple_of(
        jnp.minimum(length // ROW_TILE * ROW_TILE, rows - WINDOW), ROW_TILE
    )
    row_ids = first + lax.broadcasted_iota(jnp.int32, (WINDOW, width), 0)
    old = cache[pl.ds(first, WINDOW), :].astype(jnp.float32)
    later = jnp.where(row_ids == length + 1, new_rows[pl.ds(per_dev + slot, 1), :], 0.0)
    later = jnp.where(row_ids == length, new_rows[pl.ds(slot, 1), :], later)
    cache[pl.ds(first, WINDOW), :] = jnp.where(row_ids < length, old, later).astype(
        jnp.bfloat16
    )

    def clear(tile, carry):
        start = pl.multiple_of(tile * ROW_TILE, ROW_TILE)
        cache[pl.ds(start, ROW_TILE), :] = jnp.zeros((ROW_TILE, width), jnp.bfloat16)
        return carry

    lax.fori_loop(first // ROW_TILE + WINDOW // ROW_TILE, rows // ROW_TILE, clear, 0)


def named_range(anc_ref, first, owner, per_dev):
    low, high = jnp.int32(per_dev), jnp.int32(-1)
    for j in range(per_dev):
        local = anc_ref[first + j] - owner * per_dev
        named = jnp.logical_and(local >= 0, local < per_dev)
        low = jnp.minimum(low, jnp.where(named, local, per_dev))
        high = jnp.maximum(high, jnp.where(named, local, -1))
    return low, high


def pack_kernel(per_dev, doms, step_pairs, len_hbm, anc_hbm, new_hbm, gen_hbm, *refs):
    sends = refs[: len(step_pairs)]
    new_len_ref, own_len_ref, own_anc_ref, slot_ref = refs[len(step_pairs) : len(step_pairs) + 4]
    len_ref, anc_ref, new_bf16, new_rows, list_sem, load_sem = refs[len(step_pairs) + 4 :]
    lists = [
        pltpu.make_async_copy(anc_hbm, anc_ref, list_sem.at[0]),
        pltpu.make_async_copy(len_hbm, len_ref, list_sem.at[1]),
        pltpu.make_async_copy(new_hbm, new_bf16, list_sem.at[2]),
    ]
    for copy in lists:
        copy.start()
    me, odd = lax.axis_index("dom"), lax.axis_index("tp") % 2
    lists[0].wait()
    picks = []
    loads = []
    for k, (even_step, odd_step) in enumerate(step_pairs):
        reader = jnp.clip(me + jnp.where(odd == 1, odd_step, even_step), 0, doms - 1)
        low, high = named_range(anc_ref, reader * per_dev, me, per_dev)
        for i, pick in enumerate((jnp.minimum(low, per_dev - 1), jnp.maximum(high, 0))):
            target = sends[k].at[i]
            load = pltpu.make_async_copy(gen_hbm.at[pick], target, load_sem.at[len(loads)])
            load.start()
            picks.append((pick, target))
            loads.append(load)
    lists[1].wait()
    for j in range(per_dev):
        own_anc_ref[j] = anc_ref[me * per_dev + j]
        new_len_ref[j] = len_ref[anc_ref[me * per_dev + j]] + 2
        own_len_ref[j] = len_ref[me * per_dev + j]
        slot_ref[j] = -PICKS
    for k, (even_step, odd_step) in enumerate(step_pairs):
        source = me - jnp.where(odd == 1, odd_step, even_step)
        low, _ = named_range(anc_ref, me * per_dev, source, per_dev)
        for j in range(per_dev):
            local = anc_ref[me * per_dev + j] - source * per_dev
            named = jnp.logical_and(local >= 0, local < per_dev)
            slot = k * PICKS + jnp.where(local == low, 0, PICKS - 1)
            slot_ref[j] = jnp.where(named, slot, slot_ref[j])
    lists[2].wait()
    new_rows[...] = new_bf16[...].astype(jnp.float32).reshape(new_rows.shape)
    for load, (pick, target) in zip(loads, picks):
        load.wait()
        place_new_rows(target, new_rows, len_ref[me * per_dev + pick], pick, per_dev)


def pack(lengths, ancestors, new_kv, gen_cache, doms, step_pairs):
    per_dev, rows, width = gen_cache.shape
    count = len(step_pairs)
    smem = pl.BlockSpec(memory_space=pltpu.SMEM)
    vmem = pl.BlockSpec(memory_space=pltpu.VMEM)
    hbm = pl.BlockSpec(memory_space=pltpu.HBM)
    block_bytes = PICKS * rows * width * 2
    return pl.pallas_call(
        functools.partial(pack_kernel, per_dev, doms, step_pairs),
        out_shape=[jax.ShapeDtypeStruct((PICKS, rows, width), jnp.bfloat16)] * count
        + [jax.ShapeDtypeStruct((per_dev,), jnp.int32)] * 4,
        in_specs=[hbm] * 4,
        out_specs=[vmem] * count + [smem] * 4,
        scratch_shapes=[
            pltpu.SMEM(lengths.shape, jnp.int32),
            pltpu.SMEM(ancestors.shape, jnp.int32),
            pltpu.VMEM(new_kv.shape, jnp.bfloat16),
            pltpu.VMEM((2 * per_dev, width), jnp.float32),
            pltpu.SemaphoreType.DMA((3,)),
            pltpu.SemaphoreType.DMA((count * PICKS,)),
        ],
        compiler_params=pltpu.CompilerParams(vmem_limit_bytes=VMEM_BYTES),
        cost_estimate=pl.CostEstimate(
            flops=0, bytes_accessed=2 * count * block_bytes, transcendentals=0
        ),
        name="pack_sends",
    )(*(in_hbm(x) for x in (lengths, ancestors, new_kv, gen_cache)))


def fold_lanes(block, combine, start):
    for first in range(0, block.shape[1], HEAD_DIM):
        start = combine(start, block[:, first : first + HEAD_DIM])
    return start


def attend_kernel(
    per_dev,
    group,
    kv_local,
    chunk,
    len_ref,
    anc_ref,
    q_ref,
    prompt_hbm,
    gen_hbm,
    token_ref,
    bias_hbm,
    new_ref,
    head_ref,
    prior_ref,
    share_ref,
    out_hbm,
    prompt,
    grown,
    new_rows,
    scores,
    tops,
    totals,
    mixed_ref,
    bias_rows,
    extra,
    prompt_sem,
    gen_sem,
    out_sem,
    bias_sem,
):
    me = lax.axis_index("dom")
    steps = q_ref.shape[0]
    rows, width = grown.shape[1:]
    chunks = prompt.shape[0] // chunk
    pair = 2 * HEAD_DIM
    scale = LOG2_E / math.sqrt(HEAD_DIM)
    base = steps * per_dev

    half = per_dev // 2
    per_chunk = per_dev // chunks

    def gen_load(p):
        return pltpu.make_async_copy(gen_hbm.at[p], grown.at[p], gen_sem.at[p])

    def prompt_load(j):
        part = pl.ds(pl.multiple_of(j * chunk, chunk), chunk)
        return pltpu.make_async_copy(prompt_hbm.at[part], prompt.at[part], prompt_sem.at[j])

    for j in range(chunks):
        prompt_load(j).start()
        for i in range(per_chunk):
            gen_load(j * per_chunk + i).start()

    for i in range(base):
        row = token_ref[i // per_dev, i % per_dev] // HEAD_DIM
        pltpu.make_async_copy(bias_hbm.at[pl.ds(pl.multiple_of(row * HEAD_DIM, HEAD_DIM), HEAD_DIM)], bias_rows.at[i, 0], bias_sem.at[i]).start()

    new_rows[...] = new_ref[...].astype(jnp.float32).reshape(base, width)
    row_ids = lax.broadcasted_iota(jnp.int32, (rows, width), 0)

    def patch(p):
        gen_load(p).wait()
        behind = row_ids - len_ref[p]
        tail = jnp.where(behind == 1, new_rows[pl.ds(per_dev + p, 1), :], 0.0)
        tail = jnp.where(behind == 0, new_rows[pl.ds(p, 1), :], tail)
        grown[p] = jnp.where(behind < 0, grown[p].astype(jnp.float32), tail).astype(
            jnp.bfloat16
        )

    q2 = q_ref[...].reshape(base, q_ref.shape[-1])
    queries = [
        jnp.concatenate(
            [q2[:, h * HEAD_DIM : (h + 1) * HEAD_DIM] for h in range(c * group, (c + 1) * group)],
            axis=0,
        )
        for c in range(kv_local)
    ]

    def score(query_rows, keys):
        return lax.dot_general(
            query_rows, keys, (((1,), (1,)), ((), ())), preferred_element_type=jnp.float32
        )

    def mix(probs, values):
        return jnp.dot(probs, values, preferred_element_type=jnp.float32)

    tops[...] = jnp.full(tops.shape, NEG_FILL, jnp.float32)

    def score_chunk(j, carry):
        prompt_load(j).wait()
        part = pl.ds(pl.multiple_of(j * chunk, chunk), chunk)
        for c in range(kv_local):
            block = score(queries[c], prompt[part, c * pair : c * pair + HEAD_DIM])
            scores[c, j] = block
            tops[c] = fold_lanes(block, jnp.maximum, tops[c])
        for i in range(per_chunk):
            patch(j * per_chunk + i)
        return carry

    lax.fori_loop(0, chunks, score_chunk, 0)

    homes = []
    for p in range(per_dev):
        local = anc_ref[p] - me * per_dev
        home = jnp.logical_and(local >= 0, local < per_dev)
        source = grown.at[jnp.clip(local, 0, per_dev - 1)]
        copy = pltpu.make_async_copy(source, out_hbm.at[p], out_sem.at[p])
        homes.append((home, copy))
        pl.when(home)(copy.start)

    row_ids = lax.broadcasted_iota(jnp.int32, (base, rows), 0)
    owner = row_ids % per_dev
    last = row_ids // per_dev
    for p in range(per_dev):
        last = last + jnp.where(owner == p, len_ref[p], 0)
    visible = lax.broadcasted_iota(jnp.int32, (base, rows), 1) <= last
    visible, lower, seat = (
        jnp.concatenate([part.astype(jnp.int32)] * group, axis=0)
        for part in (visible, owner < half, owner % half)
    )
    visible, lower = visible == 1, lower == 1

    def halves(block):
        block = block.astype(jnp.float32)
        parts = [jnp.where(lower, block, 0.0), jnp.where(lower, 0.0, block)]
        return jnp.concatenate(parts, axis=1).astype(jnp.bfloat16)

    def by_seat(blocks):
        chosen = blocks[:, :HEAD_DIM]
        for i in range(1, half):
            chosen = jnp.where(seat == i, blocks[:, i * HEAD_DIM : (i + 1) * HEAD_DIM], chosen)
        return chosen

    for c in range(kv_local):
        columns = slice(c * pair, c * pair + HEAD_DIM)
        keys = jnp.concatenate(
            [
                jnp.concatenate([grown[i, :, columns], grown[i + half, :, columns]], axis=1)
                for i in range(half)
            ],
            axis=0,
        )
        own = jnp.where(visible, by_seat(score(halves(queries[c]), keys)), NEG_FILL)
        top = jnp.max(jnp.maximum(tops[c], own), axis=1, keepdims=True)
        top = jnp.broadcast_to(top, own.shape)
        tops[c] = top
        exps = jnp.where(visible, jnp.exp2((own - top) * scale), 0.0)
        totals[c] = exps
        columns = slice(c * pair + HEAD_DIM, (c + 1) * pair)
        values = jnp.concatenate(
            [
                jnp.concatenate([grown[i, :, columns], grown[i + half, :, columns]], axis=0)
                for i in range(half)
            ],
            axis=1,
        )
        mixed_ref[c] = by_seat(mix(halves(exps), values))

    def mix_chunk(j, carry):
        part = pl.ds(pl.multiple_of(j * chunk, chunk), chunk)
        for c in range(kv_local):
            top = jnp.concatenate([tops[c]] * (chunk // HEAD_DIM), axis=1)
            exps = jnp.exp2((scores[c, j] - top) * scale)
            totals[c] = fold_lanes(exps, jnp.add, totals[c])
            mixed_ref[c] += mix(
                exps.astype(jnp.bfloat16), prompt[part, c * pair + HEAD_DIM : (c + 1) * pair]
            )
        return carry

    lax.fori_loop(0, chunks, mix_chunk, 0)
    weighted = jnp.zeros((base, HEAD_DIM), jnp.float32)
    for c in range(kv_local):
        mixed = mixed_ref[c] / jnp.sum(totals[c], axis=1, keepdims=True)
        for h in range(group):
            weighted = (
                weighted + mixed[h * base : (h + 1) * base] * head_ref[c * group + h][None, :]
            )
    row_ids = lax.broadcasted_iota(jnp.int32, (base, HEAD_DIM), 0)
    column = jnp.full((base, HEAD_DIM), -1, jnp.int32)
    for i in range(base):
        pltpu.make_async_copy(bias_hbm.at[pl.ds(0, HEAD_DIM)], bias_rows.at[i, 0], bias_sem.at[i]).wait()
        column = jnp.where(row_ids == i, token_ref[i // per_dev, i % per_dev] % HEAD_DIM, column)
    adds = lax.axis_index("tp") == 0
    lane_ids = lax.broadcasted_iota(jnp.int32, (base, HEAD_DIM), 1)
    bias = jnp.where(lane_ids == column, bias_rows[...].reshape(base, HEAD_DIM), 0.0)
    weighted = weighted + jnp.where(adds, bias, 0.0)
    extra[...] = jnp.zeros(extra.shape, jnp.float32)
    extra[:, base : base + per_dev] = jnp.where(adds, prior_ref[...], 0.0)
    padding = jnp.zeros((HEAD_DIM - base, HEAD_DIM), jnp.float32)
    square = jnp.concatenate([weighted, padding], axis=0)
    row = jnp.sum(square.T, axis=0, keepdims=True) + extra[...]
    share_ref[...] = jnp.broadcast_to(row[None], share_ref.shape)
    for home, copy in homes:
        pl.when(home)(copy.wait)


def attend(
    own_lengths,
    own_ancestors,
    queries,
    prompt_kv,
    gen_cache,
    tokens,
    twist_bias,
    new_kv,
    twist_vector,
    prior_weights,
    devices,
):
    steps, per_dev, width = queries.shape
    keys, kv_width = prompt_kv.shape
    rows = gen_cache.shape[1]
    kv_local = kv_width // (2 * HEAD_DIM)
    group = width // (kv_local * HEAD_DIM)
    score_rows = steps * per_dev * group
    chunk = min(KEY_CHUNK, keys)
    head_weights = twist_vector.reshape(kv_local * group, HEAD_DIM)
    smem = pl.BlockSpec(memory_space=pltpu.SMEM)
    vmem = pl.BlockSpec(memory_space=pltpu.VMEM)
    hbm = pl.BlockSpec(memory_space=pltpu.HBM)
    score_count = score_rows * kv_local * (keys + rows)
    return pl.pallas_call(
        functools.partial(attend_kernel, per_dev, group, kv_local, chunk),
        out_shape=[
            jax.ShapeDtypeStruct((devices, 1, HEAD_DIM), jnp.float32),
            jax.ShapeDtypeStruct(gen_cache.shape, jnp.bfloat16),
        ],
        in_specs=[smem, smem, vmem, hbm, hbm, smem, hbm, vmem, vmem, vmem],
        out_specs=[vmem, hbm],
        scratch_shapes=[
            pltpu.VMEM(prompt_kv.shape, jnp.bfloat16),
            pltpu.VMEM(gen_cache.shape, jnp.bfloat16),
            pltpu.VMEM((steps * per_dev, kv_width), jnp.float32),
            pltpu.VMEM((kv_local, keys // chunk, score_rows, chunk), jnp.float32),
            pltpu.VMEM((kv_local, score_rows, HEAD_DIM), jnp.float32),
            pltpu.VMEM((kv_local, score_rows, HEAD_DIM), jnp.float32),
            pltpu.VMEM((kv_local, score_rows, HEAD_DIM), jnp.float32),
            pltpu.VMEM((steps * per_dev, 1, HEAD_DIM), jnp.float32),
            pltpu.VMEM((1, HEAD_DIM), jnp.float32),
            pltpu.SemaphoreType.DMA((keys // chunk,)),
            pltpu.SemaphoreType.DMA((per_dev,)),
            pltpu.SemaphoreType.DMA((per_dev,)),
            pltpu.SemaphoreType.DMA((steps * per_dev,)),
        ],
        compiler_params=pltpu.CompilerParams(vmem_limit_bytes=VMEM_BYTES),
        cost_estimate=pl.CostEstimate(
            flops=4 * score_count * HEAD_DIM,
            bytes_accessed=2 * (prompt_kv.size + 2 * gen_cache.size),
            transcendentals=score_count,
        ),
        name="attend",
    )(
        own_lengths,
        own_ancestors,
        queries,
        in_hbm(prompt_kv),
        in_hbm(gen_cache),
        tokens,
        in_hbm(twist_bias),
        new_kv,
        head_weights,
        prior_weights[None],
    )


def finish_kernel(doms, tps, slot_ref, *refs):
    gots = refs[: len(ORDERS[0])]
    _, all_ref, out_ref, twist_ref, normal_ref, sums, sem = refs[len(gots) :]
    per_dev = out_ref.shape[0]
    for p in range(per_dev):
        slot = slot_ref[p]
        for k, got in enumerate(gots):
            copy = pltpu.make_async_copy(got.at[slot % PICKS], out_ref.at[p], sem.at[p])
            pl.when(slot // PICKS == k)(copy.start)
    for d in range(doms):
        row = all_ref[d * tps]
        for t in range(1, tps):
            row = row + all_ref[d * tps + t]
        sums[d : d + 1, :] = row
    step_0, step_1, prior = (
        slice(k * per_dev, (k + 1) * per_dev) for k in range(3)
    )
    totals = sums[...]
    log_weights = totals[:, prior] + totals[:, step_1] - totals[:, step_0]
    largest = jnp.max(log_weights, keepdims=True)
    log_total = largest + jnp.log(jnp.sum(jnp.exp(log_weights - largest), keepdims=True))
    mine = sums[pl.ds(lax.axis_index("dom"), 1), :]
    own = mine[:, prior] + mine[:, step_1] - mine[:, step_0]
    twist_ref[...] = jnp.concatenate([mine[:, step_0], mine[:, step_1]], axis=0)
    normal_ref[...] = own - log_total
    for p in range(per_dev):
        copy = pltpu.make_async_copy(gots[0].at[0], out_ref.at[p], sem.at[p])
        pl.when(slot_ref[p] >= 0)(copy.wait)


def finish(slots, gots, held, shares, doms, tps):
    per_dev = held.shape[0]
    count = len(gots)
    smem = pl.BlockSpec(memory_space=pltpu.SMEM)
    vmem = pl.BlockSpec(memory_space=pltpu.VMEM)
    hbm = pl.BlockSpec(memory_space=pl.ANY)
    return pl.pallas_call(
        functools.partial(finish_kernel, doms, tps),
        out_shape=[
            jax.ShapeDtypeStruct(held.shape, held.dtype),
            jax.ShapeDtypeStruct((2, per_dev), jnp.float32),
            jax.ShapeDtypeStruct((1, per_dev), jnp.float32),
        ],
        in_specs=[smem] + [vmem] * count + [hbm, vmem],
        out_specs=[hbm, vmem, vmem],
        input_output_aliases={1 + count: 0},
        scratch_shapes=[
            pltpu.VMEM((doms, HEAD_DIM), jnp.float32),
            pltpu.SemaphoreType.DMA((per_dev,)),
        ],
        compiler_params=pltpu.CompilerParams(vmem_limit_bytes=VMEM_BYTES),
        cost_estimate=pl.CostEstimate(
            flops=0, bytes_accessed=held.size, transcendentals=0
        ),
        name="finish",
    )(slots, *gots, held, shares)


def routes(doms, tps, steps):
    pairs = []
    for d in range(doms):
        for t in range(tps):
            target = d + steps[t % 2]
            if 0 <= target < doms:
                pairs.append((d * tps + t, target * tps + t))
    return pairs


def local(
    queries,
    new_kv,
    gen_cache,
    prompt_kv,
    lengths,
    ancestors,
    tokens,
    twist_vector,
    twist_bias,
    prior_weights,
):
    doms, tps = lax.axis_size("dom"), lax.axis_size("tp")
    per_dev = gen_cache.shape[0]
    step_pairs = list(zip(*ORDERS))
    everyone = ("dom", "tp")

    *sends, new_lengths, own_lengths, own_ancestors, slots = pack(
        lengths, ancestors, new_kv, gen_cache, doms, step_pairs
    )
    arrivals = [
        lax.ppermute(send, everyone, routes(doms, tps, steps))
        for send, steps in zip(sends, step_pairs)
    ]

    shares, resampled = attend(
        own_lengths,
        own_ancestors,
        queries,
        prompt_kv,
        gen_cache,
        tokens,
        twist_bias,
        new_kv,
        twist_vector,
        prior_weights,
        doms * tps,
    )
    shares = lax.all_to_all(shares, everyone, 0, 0, tiled=True)
    resampled, twist, normalized = finish(slots, arrivals, resampled, shares, doms, tps)
    return (twist, normalized.reshape(per_dev), resampled, new_lengths)


def solution(mesh):
    in_specs = (
        P(None, "dom", "tp"),
        P(None, "dom", "tp"),
        P("dom", None, "tp"),
        P(None, "tp"),
        P(),
        P(),
        P(None, "dom"),
        P("tp"),
        P(),
        P("dom"),
    )
    out_specs = (P(None, "dom"), P("dom"), P("dom", None, "tp"), P("dom"))
    return jax.shard_map(local, mesh=mesh, in_specs=in_specs, out_specs=out_specs, check_vma=False)
```

```python
import functools
import math

import jax
import jax.numpy as jnp
from jax import lax
from jax.experimental import pallas as pl
from jax.experimental.pallas import tpu as pltpu
from jax.sharding import PartitionSpec as P

HEAD_DIM = 128
SPAN = 2
PICKS = 2
TABLE_PARTS = 4
NEG_FILL = -1e30
LOG2_E = math.log2(math.e)
KEY_CHUNK = 1024
VMEM_BYTES = 44 * 1024 * 1024
ROW_TILE = 16
WINDOW = 2 * ROW_TILE

ORDERS = ((-2, 2, 1, -1), (1, -1, -2, 2))


def in_hbm(x):
    return pltpu.with_memory_space_constraint(x, pltpu.HBM)


def place_new_rows(cache, new_rows, length, slot, per_dev):
    rows, width = cache.shape
    first = pl.multiple_of(
        jnp.minimum(length // ROW_TILE * ROW_TILE, rows - WINDOW), ROW_TILE
    )
    row_ids = first + lax.broadcasted_iota(jnp.int32, (WINDOW, width), 0)
    old = cache[pl.ds(first, WINDOW), :].astype(jnp.float32)
    later = jnp.where(row_ids == length + 1, new_rows[pl.ds(per_dev + slot, 1), :], 0.0)
    later = jnp.where(row_ids == length, new_rows[pl.ds(slot, 1), :], later)
    cache[pl.ds(first, WINDOW), :] = jnp.where(row_ids < length, old, later).astype(
        jnp.bfloat16
    )

    def clear(tile, carry):
        start = pl.multiple_of(tile * ROW_TILE, ROW_TILE)
        cache[pl.ds(start, ROW_TILE), :] = jnp.zeros((ROW_TILE, width), jnp.bfloat16)
        return carry

    lax.fori_loop(first // ROW_TILE + WINDOW // ROW_TILE, rows // ROW_TILE, clear, 0)


def named_range(anc_ref, first, owner, per_dev):
    low, high = jnp.int32(per_dev), jnp.int32(-1)
    for j in range(per_dev):
        local = anc_ref[first + j] - owner * per_dev
        named = jnp.logical_and(local >= 0, local < per_dev)
        low = jnp.minimum(low, jnp.where(named, local, per_dev))
        high = jnp.maximum(high, jnp.where(named, local, -1))
    return low, high


def pack_kernel(per_dev, doms, step_pairs, len_hbm, anc_hbm, new_hbm, gen_hbm, *refs):
    sends = refs[: len(step_pairs)]
    table_hbm, table, len_ref, anc_ref, new_bf16, new_rows, list_sem, load_sem = refs[
        len(step_pairs) :
    ]
    new_at, own_at, anc_at, slot_at = (k * per_dev for k in range(TABLE_PARTS))
    lists = [
        pltpu.make_async_copy(anc_hbm, anc_ref, list_sem.at[0]),
        pltpu.make_async_copy(len_hbm, len_ref, list_sem.at[1]),
        pltpu.make_async_copy(new_hbm, new_bf16, list_sem.at[2]),
    ]
    for copy in lists:
        copy.start()
    me, odd = lax.axis_index("dom"), lax.axis_index("tp") % 2
    lists[0].wait()
    picks = []
    loads = []
    for k, (even_step, odd_step) in enumerate(step_pairs):
        reader = jnp.clip(me + jnp.where(odd == 1, odd_step, even_step), 0, doms - 1)
        low, high = named_range(anc_ref, reader * per_dev, me, per_dev)
        for i, pick in enumerate((jnp.minimum(low, per_dev - 1), jnp.maximum(high, 0))):
            target = sends[k].at[i]
            load = pltpu.make_async_copy(gen_hbm.at[pick], target, load_sem.at[len(loads)])
            load.start()
            picks.append((pick, target))
            loads.append(load)
    lists[1].wait()
    for j in range(per_dev):
        table[anc_at + j] = anc_ref[me * per_dev + j]
        table[new_at + j] = len_ref[anc_ref[me * per_dev + j]] + 2
        table[own_at + j] = len_ref[me * per_dev + j]
        table[slot_at + j] = -PICKS
    for k, (even_step, odd_step) in enumerate(step_pairs):
        source = me - jnp.where(odd == 1, odd_step, even_step)
        low, _ = named_range(anc_ref, me * per_dev, source, per_dev)
        for j in range(per_dev):
            local = anc_ref[me * per_dev + j] - source * per_dev
            named = jnp.logical_and(local >= 0, local < per_dev)
            slot = k * PICKS + jnp.where(local == low, 0, PICKS - 1)
            table[slot_at + j] = jnp.where(named, slot, table[slot_at + j])
    table_copy = pltpu.make_async_copy(table, table_hbm, list_sem.at[3])
    table_copy.start()
    lists[2].wait()
    new_rows[...] = new_bf16[...].astype(jnp.float32).reshape(new_rows.shape)
    for load, (pick, target) in zip(loads, picks):
        load.wait()
        place_new_rows(target, new_rows, len_ref[me * per_dev + pick], pick, per_dev)
    table_copy.wait()


def pack(lengths, ancestors, new_kv, gen_cache, doms, step_pairs):
    per_dev, rows, width = gen_cache.shape
    count = len(step_pairs)
    vmem = pl.BlockSpec(memory_space=pltpu.VMEM)
    hbm = pl.BlockSpec(memory_space=pltpu.HBM)
    block_bytes = PICKS * rows * width * 2
    return pl.pallas_call(
        functools.partial(pack_kernel, per_dev, doms, step_pairs),
        out_shape=[jax.ShapeDtypeStruct((PICKS, rows, width), jnp.bfloat16)] * count
        + [jax.ShapeDtypeStruct((TABLE_PARTS * per_dev,), jnp.int32)],
        in_specs=[hbm] * 4,
        out_specs=[vmem] * count + [hbm],
        scratch_shapes=[
            pltpu.SMEM((TABLE_PARTS * per_dev,), jnp.int32),
            pltpu.SMEM(lengths.shape, jnp.int32),
            pltpu.SMEM(ancestors.shape, jnp.int32),
            pltpu.VMEM(new_kv.shape, jnp.bfloat16),
            pltpu.VMEM((2 * per_dev, width), jnp.float32),
            pltpu.SemaphoreType.DMA((4,)),
            pltpu.SemaphoreType.DMA((count * PICKS,)),
        ],
        compiler_params=pltpu.CompilerParams(vmem_limit_bytes=VMEM_BYTES),
        cost_estimate=pl.CostEstimate(
            flops=0, bytes_accessed=2 * count * block_bytes, transcendentals=0
        ),
        name="pack_sends",
    )(*(in_hbm(x) for x in (lengths, ancestors, new_kv, gen_cache)))


def fold_lanes(block, combine, start):
    for first in range(0, block.shape[1], HEAD_DIM):
        start = combine(start, block[:, first : first + HEAD_DIM])
    return start


def attend_kernel(
    per_dev,
    group,
    kv_local,
    chunk,
    table_hbm,
    q_ref,
    prompt_hbm,
    gen_hbm,
    token_hbm,
    bias_hbm,
    new_ref,
    head_ref,
    prior_ref,
    share_ref,
    out_hbm,
    prompt,
    grown,
    new_rows,
    scores,
    tops,
    totals,
    mixed_ref,
    bias_rows,
    extra,
    table,
    token_ref,
    prompt_sem,
    gen_sem,
    out_sem,
    bias_sem,
    list_sem,
):
    me = lax.axis_index("dom")
    steps = q_ref.shape[0]
    rows, width = grown.shape[1:]
    chunks = prompt.shape[0] // chunk
    pair = 2 * HEAD_DIM
    scale = LOG2_E / math.sqrt(HEAD_DIM)
    base = steps * per_dev

    half = per_dev // 2
    per_chunk = per_dev // chunks

    def gen_load(p):
        return pltpu.make_async_copy(gen_hbm.at[p], grown.at[p], gen_sem.at[p])

    def prompt_load(j):
        part = pl.ds(pl.multiple_of(j * chunk, chunk), chunk)
        return pltpu.make_async_copy(prompt_hbm.at[part], prompt.at[part], prompt_sem.at[j])

    lists = [
        pltpu.make_async_copy(table_hbm, table, list_sem.at[0]),
        pltpu.make_async_copy(token_hbm, token_ref, list_sem.at[1]),
    ]
    for copy in lists:
        copy.start()
    for j in range(chunks):
        prompt_load(j).start()
        for i in range(per_chunk):
            gen_load(j * per_chunk + i).start()

    for copy in lists:
        copy.wait()
    len_ref, anc_ref = (table.at[pl.ds(k * per_dev, per_dev)] for k in (1, 2))
    for i in range(base):
        row = token_ref[i // per_dev, i % per_dev] // HEAD_DIM
        pltpu.make_async_copy(bias_hbm.at[pl.ds(pl.multiple_of(row * HEAD_DIM, HEAD_DIM), HEAD_DIM)], bias_rows.at[i, 0], bias_sem.at[i]).start()

    new_rows[...] = new_ref[...].astype(jnp.float32).reshape(base, width)
    row_ids = lax.broadcasted_iota(jnp.int32, (rows, width), 0)

    def patch(p):
        gen_load(p).wait()
        behind = row_ids - len_ref[p]
        tail = jnp.where(behind == 1, new_rows[pl.ds(per_dev + p, 1), :], 0.0)
        tail = jnp.where(behind == 0, new_rows[pl.ds(p, 1), :], tail)
        grown[p] = jnp.where(behind < 0, grown[p].astype(jnp.float32), tail).astype(
            jnp.bfloat16
        )

    q2 = q_ref[...].reshape(base, q_ref.shape[-1])
    queries = [
        jnp.concatenate(
            [q2[:, h * HEAD_DIM : (h + 1) * HEAD_DIM] for h in range(c * group, (c + 1) * group)],
            axis=0,
        )
        for c in range(kv_local)
    ]

    def score(query_rows, keys):
        return lax.dot_general(
            query_rows, keys, (((1,), (1,)), ((), ())), preferred_element_type=jnp.float32
        )

    def mix(probs, values):
        return jnp.dot(probs, values, preferred_element_type=jnp.float32)

    tops[...] = jnp.full(tops.shape, NEG_FILL, jnp.float32)

    def score_chunk(j, carry):
        prompt_load(j).wait()
        part = pl.ds(pl.multiple_of(j * chunk, chunk), chunk)
        for c in range(kv_local):
            block = score(queries[c], prompt[part, c * pair : c * pair + HEAD_DIM])
            scores[c, j] = block
            tops[c] = fold_lanes(block, jnp.maximum, tops[c])
        for i in range(per_chunk):
            patch(j * per_chunk + i)
        return carry

    lax.fori_loop(0, chunks, score_chunk, 0)

    homes = []
    for p in range(per_dev):
        local = anc_ref[p] - me * per_dev
        home = jnp.logical_and(local >= 0, local < per_dev)
        source = grown.at[jnp.clip(local, 0, per_dev - 1)]
        copy = pltpu.make_async_copy(source, out_hbm.at[p], out_sem.at[p])
        homes.append((home, copy))
        pl.when(home)(copy.start)

    row_ids = lax.broadcasted_iota(jnp.int32, (base, rows), 0)
    owner = row_ids % per_dev
    last = row_ids // per_dev
    for p in range(per_dev):
        last = last + jnp.where(owner == p, len_ref[p], 0)
    visible = lax.broadcasted_iota(jnp.int32, (base, rows), 1) <= last
    visible, lower, seat = (
        jnp.concatenate([part.astype(jnp.int32)] * group, axis=0)
        for part in (visible, owner < half, owner % half)
    )
    visible, lower = visible == 1, lower == 1

    def halves(block):
        block = block.astype(jnp.float32)
        parts = [jnp.where(lower, block, 0.0), jnp.where(lower, 0.0, block)]
        return jnp.concatenate(parts, axis=1).astype(jnp.bfloat16)

    def by_seat(blocks):
        chosen = blocks[:, :HEAD_DIM]
        for i in range(1, half):
            chosen = jnp.where(seat == i, blocks[:, i * HEAD_DIM : (i + 1) * HEAD_DIM], chosen)
        return chosen

    for c in range(kv_local):
        columns = slice(c * pair, c * pair + HEAD_DIM)
        keys = jnp.concatenate(
            [
                jnp.concatenate([grown[i, :, columns], grown[i + half, :, columns]], axis=1)
                for i in range(half)
            ],
            axis=0,
        )
        own = jnp.where(visible, by_seat(score(halves(queries[c]), keys)), NEG_FILL)
        top = jnp.max(jnp.maximum(tops[c], own), axis=1, keepdims=True)
        top = jnp.broadcast_to(top, own.shape)
        tops[c] = top
        exps = jnp.where(visible, jnp.exp2((own - top) * scale), 0.0)
        totals[c] = exps
        columns = slice(c * pair + HEAD_DIM, (c + 1) * pair)
        values = jnp.concatenate(
            [
                jnp.concatenate([grown[i, :, columns], grown[i + half, :, columns]], axis=0)
                for i in range(half)
            ],
            axis=1,
        )
        mixed_ref[c] = by_seat(mix(halves(exps), values))

    def mix_chunk(j, carry):
        part = pl.ds(pl.multiple_of(j * chunk, chunk), chunk)
        for c in range(kv_local):
            top = jnp.concatenate([tops[c]] * (chunk // HEAD_DIM), axis=1)
            exps = jnp.exp2((scores[c, j] - top) * scale)
            totals[c] = fold_lanes(exps, jnp.add, totals[c])
            mixed_ref[c] += mix(
                exps.astype(jnp.bfloat16), prompt[part, c * pair + HEAD_DIM : (c + 1) * pair]
            )
        return carry

    lax.fori_loop(0, chunks, mix_chunk, 0)
    weighted = jnp.zeros((base, HEAD_DIM), jnp.float32)
    for c in range(kv_local):
        mixed = mixed_ref[c] / jnp.sum(totals[c], axis=1, keepdims=True)
        for h in range(group):
            weighted = (
                weighted + mixed[h * base : (h + 1) * base] * head_ref[c * group + h][None, :]
            )
    row_ids = lax.broadcasted_iota(jnp.int32, (base, HEAD_DIM), 0)
    column = jnp.full((base, HEAD_DIM), -1, jnp.int32)
    for i in range(base):
        pltpu.make_async_copy(bias_hbm.at[pl.ds(0, HEAD_DIM)], bias_rows.at[i, 0], bias_sem.at[i]).wait()
        column = jnp.where(row_ids == i, token_ref[i // per_dev, i % per_dev] % HEAD_DIM, column)
    adds = lax.axis_index("tp") == 0
    lane_ids = lax.broadcasted_iota(jnp.int32, (base, HEAD_DIM), 1)
    bias = jnp.where(lane_ids == column, bias_rows[...].reshape(base, HEAD_DIM), 0.0)
    weighted = weighted + jnp.where(adds, bias, 0.0)
    extra[...] = jnp.zeros(extra.shape, jnp.float32)
    extra[:, base : base + per_dev] = jnp.where(adds, prior_ref[...], 0.0)
    padding = jnp.zeros((HEAD_DIM - base, HEAD_DIM), jnp.float32)
    square = jnp.concatenate([weighted, padding], axis=0)
    row = jnp.sum(square.T, axis=0, keepdims=True) + extra[...]
    share_ref[...] = jnp.broadcast_to(row[None], share_ref.shape)
    for home, copy in homes:
        pl.when(home)(copy.wait)


def attend(
    table,
    queries,
    prompt_kv,
    gen_cache,
    tokens,
    twist_bias,
    new_kv,
    twist_vector,
    prior_weights,
    devices,
):
    steps, per_dev, width = queries.shape
    keys, kv_width = prompt_kv.shape
    rows = gen_cache.shape[1]
    kv_local = kv_width // (2 * HEAD_DIM)
    group = width // (kv_local * HEAD_DIM)
    score_rows = steps * per_dev * group
    chunk = min(KEY_CHUNK, keys)
    head_weights = twist_vector.reshape(kv_local * group, HEAD_DIM)
    vmem = pl.BlockSpec(memory_space=pltpu.VMEM)
    hbm = pl.BlockSpec(memory_space=pltpu.HBM)
    score_count = score_rows * kv_local * (keys + rows)
    return pl.pallas_call(
        functools.partial(attend_kernel, per_dev, group, kv_local, chunk),
        out_shape=[
            jax.ShapeDtypeStruct((devices, 1, HEAD_DIM), jnp.float32),
            jax.ShapeDtypeStruct(gen_cache.shape, jnp.bfloat16),
        ],
        in_specs=[hbm, vmem, hbm, hbm, hbm, hbm, vmem, vmem, vmem],
        out_specs=[vmem, hbm],
        scratch_shapes=[
            pltpu.VMEM(prompt_kv.shape, jnp.bfloat16),
            pltpu.VMEM(gen_cache.shape, jnp.bfloat16),
            pltpu.VMEM((steps * per_dev, kv_width), jnp.float32),
            pltpu.VMEM((kv_local, keys // chunk, score_rows, chunk), jnp.float32),
            pltpu.VMEM((kv_local, score_rows, HEAD_DIM), jnp.float32),
            pltpu.VMEM((kv_local, score_rows, HEAD_DIM), jnp.float32),
            pltpu.VMEM((kv_local, score_rows, HEAD_DIM), jnp.float32),
            pltpu.VMEM((steps * per_dev, 1, HEAD_DIM), jnp.float32),
            pltpu.VMEM((1, HEAD_DIM), jnp.float32),
            pltpu.SMEM(table.shape, jnp.int32),
            pltpu.SMEM(tokens.shape, jnp.int32),
            pltpu.SemaphoreType.DMA((keys // chunk,)),
            pltpu.SemaphoreType.DMA((per_dev,)),
            pltpu.SemaphoreType.DMA((per_dev,)),
            pltpu.SemaphoreType.DMA((steps * per_dev,)),
            pltpu.SemaphoreType.DMA((2,)),
        ],
        compiler_params=pltpu.CompilerParams(vmem_limit_bytes=VMEM_BYTES),
        cost_estimate=pl.CostEstimate(
            flops=4 * score_count * HEAD_DIM,
            bytes_accessed=2 * (prompt_kv.size + 2 * gen_cache.size),
            transcendentals=score_count,
        ),
        name="attend",
    )(
        in_hbm(table),
        queries,
        in_hbm(prompt_kv),
        in_hbm(gen_cache),
        in_hbm(tokens),
        in_hbm(twist_bias),
        new_kv,
        head_weights,
        prior_weights[None],
    )


def finish_kernel(doms, tps, table_ref, *refs):
    gots = refs[: len(ORDERS[0])]
    _, all_ref, out_ref, twist_hbm, normal_hbm = refs[len(gots) : len(gots) + 5]
    table, sums, twist, normal, copy_sem, small_sem = refs[len(gots) + 5 :]
    per_dev = out_ref.shape[0]
    table_copy = pltpu.make_async_copy(table_ref, table, small_sem.at[0])
    table_copy.start()
    table_copy.wait()
    slots = [table[(TABLE_PARTS - 1) * per_dev + p] for p in range(per_dev)]
    for p, slot in enumerate(slots):
        for k, got in enumerate(gots):
            copy = pltpu.make_async_copy(got.at[slot % PICKS], out_ref.at[p], copy_sem.at[p])
            pl.when(slot // PICKS == k)(copy.start)
    for d in range(doms):
        row = all_ref[d * tps]
        for t in range(1, tps):
            row = row + all_ref[d * tps + t]
        sums[d : d + 1, :] = row
    step_0, step_1, prior = (
        slice(k * per_dev, (k + 1) * per_dev) for k in range(3)
    )
    totals = sums[...]
    log_weights = totals[:, prior] + totals[:, step_1] - totals[:, step_0]
    largest = jnp.max(log_weights, keepdims=True)
    log_total = largest + jnp.log(jnp.sum(jnp.exp(log_weights - largest), keepdims=True))
    mine = sums[pl.ds(lax.axis_index("dom"), 1), :]
    own = mine[:, prior] + mine[:, step_1] - mine[:, step_0]
    twist[...] = jnp.concatenate([mine[:, step_0], mine[:, step_1]], axis=0)
    normal[...] = own - log_total
    results = [
        pltpu.make_async_copy(twist, twist_hbm, small_sem.at[1]),
        pltpu.make_async_copy(normal, normal_hbm, small_sem.at[2]),
    ]
    for copy in results:
        copy.start()
    for p, slot in enumerate(slots):
        copy = pltpu.make_async_copy(gots[0].at[0], out_ref.at[p], copy_sem.at[p])
        pl.when(slot >= 0)(copy.wait)
    for copy in results:
        copy.wait()


def finish(table, gots, held, shares, doms, tps):
    per_dev = held.shape[0]
    count = len(gots)
    vmem = pl.BlockSpec(memory_space=pltpu.VMEM)
    hbm = pl.BlockSpec(memory_space=pl.ANY)
    return pl.pallas_call(
        functools.partial(finish_kernel, doms, tps),
        out_shape=[
            jax.ShapeDtypeStruct(held.shape, held.dtype),
            jax.ShapeDtypeStruct((2, per_dev), jnp.float32),
            jax.ShapeDtypeStruct((1, per_dev), jnp.float32),
        ],
        in_specs=[vmem] + [vmem] * count + [hbm, vmem],
        out_specs=[hbm, hbm, hbm],
        input_output_aliases={1 + count: 0},
        scratch_shapes=[
            pltpu.SMEM(table.shape, jnp.int32),
            pltpu.VMEM((doms, HEAD_DIM), jnp.float32),
            pltpu.VMEM((2, per_dev), jnp.float32),
            pltpu.VMEM((1, per_dev), jnp.float32),
            pltpu.SemaphoreType.DMA((per_dev,)),
            pltpu.SemaphoreType.DMA((3,)),
        ],
        compiler_params=pltpu.CompilerParams(vmem_limit_bytes=VMEM_BYTES),
        cost_estimate=pl.CostEstimate(
            flops=0, bytes_accessed=held.size, transcendentals=0
        ),
        name="finish",
    )(table, *gots, held, shares)


def routes(doms, tps, steps):
    pairs = []
    for d in range(doms):
        for t in range(tps):
            target = d + steps[t % 2]
            if 0 <= target < doms:
                pairs.append((d * tps + t, target * tps + t))
    return pairs


def local(
    queries,
    new_kv,
    gen_cache,
    prompt_kv,
    lengths,
    ancestors,
    tokens,
    twist_vector,
    twist_bias,
    prior_weights,
):
    doms, tps = lax.axis_size("dom"), lax.axis_size("tp")
    per_dev = gen_cache.shape[0]
    step_pairs = list(zip(*ORDERS))
    everyone = ("dom", "tp")

    *sends, table = pack(
        lengths, ancestors, new_kv, gen_cache, doms, step_pairs
    )
    arrivals = [
        lax.ppermute(send, everyone, routes(doms, tps, steps))
        for send, steps in zip(sends, step_pairs)
    ]

    shares, resampled = attend(
        table,
        queries,
        prompt_kv,
        gen_cache,
        tokens,
        twist_bias,
        new_kv,
        twist_vector,
        prior_weights,
        doms * tps,
    )
    shares = lax.all_to_all(shares, everyone, 0, 0, tiled=True)
    resampled, twist, normalized = finish(table, arrivals, resampled, shares, doms, tps)
    return (twist, normalized.reshape(per_dev), resampled, table[:per_dev])


def solution(mesh):
    in_specs = (
        P(None, "dom", "tp"),
        P(None, "dom", "tp"),
        P("dom", None, "tp"),
        P(None, "tp"),
        P(),
        P(),
        P(None, "dom"),
        P("tp"),
        P(),
        P("dom"),
    )
    out_specs = (P(None, "dom"), P("dom"), P("dom", None, "tp"), P("dom"))
    return jax.shard_map(local, mesh=mesh, in_specs=in_specs, out_specs=out_specs, check_vma=False)
```

```python
import functools
import math

import jax
import jax.numpy as jnp
from jax import lax
from jax.experimental import pallas as pl
from jax.experimental.pallas import tpu as pltpu
from jax.sharding import PartitionSpec as P

HEAD_DIM = 128
SPAN = 2
PICKS = 2
TABLE_PARTS = 4
NEG_FILL = -1e30
LOG2_E = math.log2(math.e)
KEY_CHUNK = 1024
VMEM_BYTES = 44 * 1024 * 1024
ROW_TILE = 16
WINDOW = 2 * ROW_TILE

ORDERS = ((-2, 2, 1, -1), (2, -2, -1, 1))


def in_hbm(x):
    return pltpu.with_memory_space_constraint(x, pltpu.HBM)


def place_new_rows(cache, new_rows, length, slot, per_dev):
    rows, width = cache.shape
    first = pl.multiple_of(
        jnp.minimum(length // ROW_TILE * ROW_TILE, rows - WINDOW), ROW_TILE
    )
    row_ids = first + lax.broadcasted_iota(jnp.int32, (WINDOW, width), 0)
    old = cache[pl.ds(first, WINDOW), :].astype(jnp.float32)
    later = jnp.where(row_ids == length + 1, new_rows[pl.ds(per_dev + slot, 1), :], 0.0)
    later = jnp.where(row_ids == length, new_rows[pl.ds(slot, 1), :], later)
    cache[pl.ds(first, WINDOW), :] = jnp.where(row_ids < length, old, later).astype(
        jnp.bfloat16
    )

    def clear(tile, carry):
        start = pl.multiple_of(tile * ROW_TILE, ROW_TILE)
        cache[pl.ds(start, ROW_TILE), :] = jnp.zeros((ROW_TILE, width), jnp.bfloat16)
        return carry

    lax.fori_loop(first // ROW_TILE + WINDOW // ROW_TILE, rows // ROW_TILE, clear, 0)


def named_range(anc_ref, first, owner, per_dev):
    low, high = jnp.int32(per_dev), jnp.int32(-1)
    for j in range(per_dev):
        local = anc_ref[first + j] - owner * per_dev
        named = jnp.logical_and(local >= 0, local < per_dev)
        low = jnp.minimum(low, jnp.where(named, local, per_dev))
        high = jnp.maximum(high, jnp.where(named, local, -1))
    return low, high


def pack_kernel(per_dev, doms, step_pairs, len_hbm, anc_hbm, new_hbm, gen_hbm, *refs):
    sends = refs[: len(step_pairs)]
    table_hbm, table, len_ref, anc_ref, new_bf16, new_rows, list_sem, load_sem = refs[
        len(step_pairs) :
    ]
    new_at, own_at, anc_at, slot_at = (k * per_dev for k in range(TABLE_PARTS))
    lists = [
        pltpu.make_async_copy(anc_hbm, anc_ref, list_sem.at[0]),
        pltpu.make_async_copy(len_hbm, len_ref, list_sem.at[1]),
        pltpu.make_async_copy(new_hbm, new_bf16, list_sem.at[2]),
    ]
    for copy in lists:
        copy.start()
    me, odd = lax.axis_index("dom"), lax.axis_index("tp") % 2
    lists[0].wait()
    picks = []
    loads = []
    for k, (even_step, odd_step) in enumerate(step_pairs):
        reader = jnp.clip(me + jnp.where(odd == 1, odd_step, even_step), 0, doms - 1)
        low, high = named_range(anc_ref, reader * per_dev, me, per_dev)
        for i, pick in enumerate((jnp.minimum(low, per_dev - 1), jnp.maximum(high, 0))):
            target = sends[k].at[i]
            load = pltpu.make_async_copy(gen_hbm.at[pick], target, load_sem.at[len(loads)])
            load.start()
            picks.append((pick, target))
            loads.append(load)
    lists[1].wait()
    for j in range(per_dev):
        table[anc_at + j] = anc_ref[me * per_dev + j]
        table[new_at + j] = len_ref[anc_ref[me * per_dev + j]] + 2
        table[own_at + j] = len_ref[me * per_dev + j]
        table[slot_at + j] = -PICKS
    for k, (even_step, odd_step) in enumerate(step_pairs):
        source = me - jnp.where(odd == 1, odd_step, even_step)
        low, _ = named_range(anc_ref, me * per_dev, source, per_dev)
        for j in range(per_dev):
            local = anc_ref[me * per_dev + j] - source * per_dev
            named = jnp.logical_and(local >= 0, local < per_dev)
            slot = k * PICKS + jnp.where(local == low, 0, PICKS - 1)
            table[slot_at + j] = jnp.where(named, slot, table[slot_at + j])
    table_copy = pltpu.make_async_copy(table, table_hbm, list_sem.at[3])
    table_copy.start()
    lists[2].wait()
    new_rows[...] = new_bf16[...].astype(jnp.float32).reshape(new_rows.shape)
    for load, (pick, target) in zip(loads, picks):
        load.wait()
        place_new_rows(target, new_rows, len_ref[me * per_dev + pick], pick, per_dev)
    table_copy.wait()


def pack(lengths, ancestors, new_kv, gen_cache, doms, step_pairs):
    per_dev, rows, width = gen_cache.shape
    count = len(step_pairs)
    vmem = pl.BlockSpec(memory_space=pltpu.VMEM)
    hbm = pl.BlockSpec(memory_space=pltpu.HBM)
    block_bytes = PICKS * rows * width * 2
    return pl.pallas_call(
        functools.partial(pack_kernel, per_dev, doms, step_pairs),
        out_shape=[jax.ShapeDtypeStruct((PICKS, rows, width), jnp.bfloat16)] * count
        + [jax.ShapeDtypeStruct((TABLE_PARTS * per_dev,), jnp.int32)],
        in_specs=[hbm] * 4,
        out_specs=[vmem] * count + [hbm],
        scratch_shapes=[
            pltpu.SMEM((TABLE_PARTS * per_dev,), jnp.int32),
            pltpu.SMEM(lengths.shape, jnp.int32),
            pltpu.SMEM(ancestors.shape, jnp.int32),
            pltpu.VMEM(new_kv.shape, jnp.bfloat16),
            pltpu.VMEM((2 * per_dev, width), jnp.float32),
            pltpu.SemaphoreType.DMA((4,)),
            pltpu.SemaphoreType.DMA((count * PICKS,)),
        ],
        compiler_params=pltpu.CompilerParams(vmem_limit_bytes=VMEM_BYTES),
        cost_estimate=pl.CostEstimate(
            flops=0, bytes_accessed=2 * count * block_bytes, transcendentals=0
        ),
        name="pack_sends",
    )(*(in_hbm(x) for x in (lengths, ancestors, new_kv, gen_cache)))


def fold_lanes(block, combine, start):
    for first in range(0, block.shape[1], HEAD_DIM):
        start = combine(start, block[:, first : first + HEAD_DIM])
    return start


def attend_kernel(
    per_dev,
    group,
    kv_local,
    chunk,
    table_hbm,
    q_ref,
    prompt_hbm,
    gen_hbm,
    token_hbm,
    bias_hbm,
    new_ref,
    head_ref,
    prior_ref,
    share_ref,
    out_hbm,
    prompt,
    grown,
    new_rows,
    scores,
    tops,
    totals,
    mixed_ref,
    bias_rows,
    extra,
    table,
    token_ref,
    prompt_sem,
    gen_sem,
    out_sem,
    bias_sem,
    list_sem,
):
    me = lax.axis_index("dom")
    steps = q_ref.shape[0]
    rows, width = grown.shape[1:]
    chunks = prompt.shape[0] // chunk
    pair = 2 * HEAD_DIM
    scale = LOG2_E / math.sqrt(HEAD_DIM)
    base = steps * per_dev

    half = per_dev // 2
    per_chunk = per_dev // chunks

    def gen_load(p):
        return pltpu.make_async_copy(gen_hbm.at[p], grown.at[p], gen_sem.at[p])

    def prompt_load(j):
        part = pl.ds(pl.multiple_of(j * chunk, chunk), chunk)
        return pltpu.make_async_copy(prompt_hbm.at[part], prompt.at[part], prompt_sem.at[j])

    lists = [
        pltpu.make_async_copy(table_hbm, table, list_sem.at[0]),
        pltpu.make_async_copy(token_hbm, token_ref, list_sem.at[1]),
    ]
    for copy in lists:
        copy.start()
    for j in range(chunks):
        prompt_load(j).start()
        for i in range(per_chunk):
            gen_load(j * per_chunk + i).start()

    for copy in lists:
        copy.wait()
    len_ref, anc_ref = (table.at[pl.ds(k * per_dev, per_dev)] for k in (1, 2))
    for i in range(base):
        row = token_ref[i // per_dev, i % per_dev] // HEAD_DIM
        pltpu.make_async_copy(bias_hbm.at[pl.ds(pl.multiple_of(row * HEAD_DIM, HEAD_DIM), HEAD_DIM)], bias_rows.at[i, 0], bias_sem.at[i]).start()

    new_rows[...] = new_ref[...].astype(jnp.float32).reshape(base, width)
    row_ids = lax.broadcasted_iota(jnp.int32, (rows, width), 0)

    def patch(p):
        gen_load(p).wait()
        behind = row_ids - len_ref[p]
        tail = jnp.where(behind == 1, new_rows[pl.ds(per_dev + p, 1), :], 0.0)
        tail = jnp.where(behind == 0, new_rows[pl.ds(p, 1), :], tail)
        grown[p] = jnp.where(behind < 0, grown[p].astype(jnp.float32), tail).astype(
            jnp.bfloat16
        )

    q2 = q_ref[...].reshape(base, q_ref.shape[-1])
    queries = [
        jnp.concatenate(
            [q2[:, h * HEAD_DIM : (h + 1) * HEAD_DIM] for h in range(c * group, (c + 1) * group)],
            axis=0,
        )
        for c in range(kv_local)
    ]

    def score(query_rows, keys):
        return lax.dot_general(
            query_rows, keys, (((1,), (1,)), ((), ())), preferred_element_type=jnp.float32
        )

    def mix(probs, values):
        return jnp.dot(probs, values, preferred_element_type=jnp.float32)

    tops[...] = jnp.full(tops.shape, NEG_FILL, jnp.float32)

    def score_chunk(j, carry):
        prompt_load(j).wait()
        part = pl.ds(pl.multiple_of(j * chunk, chunk), chunk)
        for c in range(kv_local):
            block = score(queries[c], prompt[part, c * pair : c * pair + HEAD_DIM])
            scores[c, j] = block
            tops[c] = fold_lanes(block, jnp.maximum, tops[c])
        for i in range(per_chunk):
            patch(j * per_chunk + i)
        return carry

    lax.fori_loop(0, chunks, score_chunk, 0)

    homes = []
    for p in range(per_dev):
        local = anc_ref[p] - me * per_dev
        home = jnp.logical_and(local >= 0, local < per_dev)
        source = grown.at[jnp.clip(local, 0, per_dev - 1)]
        copy = pltpu.make_async_copy(source, out_hbm.at[p], out_sem.at[p])
        homes.append((home, copy))
        pl.when(home)(copy.start)

    row_ids = lax.broadcasted_iota(jnp.int32, (base, rows), 0)
    owner = row_ids % per_dev
    last = row_ids // per_dev
    for p in range(per_dev):
        last = last + jnp.where(owner == p, len_ref[p], 0)
    visible = lax.broadcasted_iota(jnp.int32, (base, rows), 1) <= last
    visible, lower, seat = (
        jnp.concatenate([part.astype(jnp.int32)] * group, axis=0)
        for part in (visible, owner < half, owner % half)
    )
    visible, lower = visible == 1, lower == 1

    def halves(block):
        block = block.astype(jnp.float32)
        parts = [jnp.where(lower, block, 0.0), jnp.where(lower, 0.0, block)]
        return jnp.concatenate(parts, axis=1).astype(jnp.bfloat16)

    def by_seat(blocks):
        chosen = blocks[:, :HEAD_DIM]
        for i in range(1, half):
            chosen = jnp.where(seat == i, blocks[:, i * HEAD_DIM : (i + 1) * HEAD_DIM], chosen)
        return chosen

    for c in range(kv_local):
        columns = slice(c * pair, c * pair + HEAD_DIM)
        keys = jnp.concatenate(
            [
                jnp.concatenate([grown[i, :, columns], grown[i + half, :, columns]], axis=1)
                for i in range(half)
            ],
            axis=0,
        )
        own = jnp.where(visible, by_seat(score(halves(queries[c]), keys)), NEG_FILL)
        top = jnp.max(jnp.maximum(tops[c], own), axis=1, keepdims=True)
        top = jnp.broadcast_to(top, own.shape)
        tops[c] = top
        exps = jnp.where(visible, jnp.exp2((own - top) * scale), 0.0)
        totals[c] = exps
        columns = slice(c * pair + HEAD_DIM, (c + 1) * pair)
        values = jnp.concatenate(
            [
                jnp.concatenate([grown[i, :, columns], grown[i + half, :, columns]], axis=0)
                for i in range(half)
            ],
            axis=1,
        )
        mixed_ref[c] = by_seat(mix(halves(exps), values))

    def mix_chunk(j, carry):
        part = pl.ds(pl.multiple_of(j * chunk, chunk), chunk)
        for c in range(kv_local):
            top = jnp.concatenate([tops[c]] * (chunk // HEAD_DIM), axis=1)
            exps = jnp.exp2((scores[c, j] - top) * scale)
            totals[c] = fold_lanes(exps, jnp.add, totals[c])
            mixed_ref[c] += mix(
                exps.astype(jnp.bfloat16), prompt[part, c * pair + HEAD_DIM : (c + 1) * pair]
            )
        return carry

    lax.fori_loop(0, chunks, mix_chunk, 0)
    weighted = jnp.zeros((base, HEAD_DIM), jnp.float32)
    for c in range(kv_local):
        mixed = mixed_ref[c] / jnp.sum(totals[c], axis=1, keepdims=True)
        for h in range(group):
            weighted = (
                weighted + mixed[h * base : (h + 1) * base] * head_ref[c * group + h][None, :]
            )
    row_ids = lax.broadcasted_iota(jnp.int32, (base, HEAD_DIM), 0)
    column = jnp.full((base, HEAD_DIM), -1, jnp.int32)
    for i in range(base):
        pltpu.make_async_copy(bias_hbm.at[pl.ds(0, HEAD_DIM)], bias_rows.at[i, 0], bias_sem.at[i]).wait()
        column = jnp.where(row_ids == i, token_ref[i // per_dev, i % per_dev] % HEAD_DIM, column)
    adds = lax.axis_index("tp") == 0
    lane_ids = lax.broadcasted_iota(jnp.int32, (base, HEAD_DIM), 1)
    bias = jnp.where(lane_ids == column, bias_rows[...].reshape(base, HEAD_DIM), 0.0)
    weighted = weighted + jnp.where(adds, bias, 0.0)
    extra[...] = jnp.zeros(extra.shape, jnp.float32)
    extra[:, base : base + per_dev] = jnp.where(adds, prior_ref[...], 0.0)
    padding = jnp.zeros((HEAD_DIM - base, HEAD_DIM), jnp.float32)
    square = jnp.concatenate([weighted, padding], axis=0)
    row = jnp.sum(square.T, axis=0, keepdims=True) + extra[...]
    share_ref[...] = jnp.broadcast_to(row[None], share_ref.shape)
    for home, copy in homes:
        pl.when(home)(copy.wait)


def attend(
    table,
    queries,
    prompt_kv,
    gen_cache,
    tokens,
    twist_bias,
    new_kv,
    twist_vector,
    prior_weights,
    devices,
):
    steps, per_dev, width = queries.shape
    keys, kv_width = prompt_kv.shape
    rows = gen_cache.shape[1]
    kv_local = kv_width // (2 * HEAD_DIM)
    group = width // (kv_local * HEAD_DIM)
    score_rows = steps * per_dev * group
    chunk = min(KEY_CHUNK, keys)
    head_weights = twist_vector.reshape(kv_local * group, HEAD_DIM)
    vmem = pl.BlockSpec(memory_space=pltpu.VMEM)
    hbm = pl.BlockSpec(memory_space=pltpu.HBM)
    score_count = score_rows * kv_local * (keys + rows)
    return pl.pallas_call(
        functools.partial(attend_kernel, per_dev, group, kv_local, chunk),
        out_shape=[
            jax.ShapeDtypeStruct((devices, 1, HEAD_DIM), jnp.float32),
            jax.ShapeDtypeStruct(gen_cache.shape, jnp.bfloat16),
        ],
        in_specs=[hbm, vmem, hbm, hbm, hbm, hbm, vmem, vmem, vmem],
        out_specs=[vmem, hbm],
        scratch_shapes=[
            pltpu.VMEM(prompt_kv.shape, jnp.bfloat16),
            pltpu.VMEM(gen_cache.shape, jnp.bfloat16),
            pltpu.VMEM((steps * per_dev, kv_width), jnp.float32),
            pltpu.VMEM((kv_local, keys // chunk, score_rows, chunk), jnp.float32),
            pltpu.VMEM((kv_local, score_rows, HEAD_DIM), jnp.float32),
            pltpu.VMEM((kv_local, score_rows, HEAD_DIM), jnp.float32),
            pltpu.VMEM((kv_local, score_rows, HEAD_DIM), jnp.float32),
            pltpu.VMEM((steps * per_dev, 1, HEAD_DIM), jnp.float32),
            pltpu.VMEM((1, HEAD_DIM), jnp.float32),
            pltpu.SMEM(table.shape, jnp.int32),
            pltpu.SMEM(tokens.shape, jnp.int32),
            pltpu.SemaphoreType.DMA((keys // chunk,)),
            pltpu.SemaphoreType.DMA((per_dev,)),
            pltpu.SemaphoreType.DMA((per_dev,)),
            pltpu.SemaphoreType.DMA((steps * per_dev,)),
            pltpu.SemaphoreType.DMA((2,)),
        ],
        compiler_params=pltpu.CompilerParams(vmem_limit_bytes=VMEM_BYTES),
        cost_estimate=pl.CostEstimate(
            flops=4 * score_count * HEAD_DIM,
            bytes_accessed=2 * (prompt_kv.size + 2 * gen_cache.size),
            transcendentals=score_count,
        ),
        name="attend",
    )(
        in_hbm(table),
        queries,
        in_hbm(prompt_kv),
        in_hbm(gen_cache),
        in_hbm(tokens),
        in_hbm(twist_bias),
        new_kv,
        head_weights,
        prior_weights[None],
    )


def finish_kernel(doms, tps, table_ref, *refs):
    gots = refs[: len(ORDERS[0])]
    _, all_ref, out_ref, twist_hbm, normal_hbm = refs[len(gots) : len(gots) + 5]
    table, sums, twist, normal, copy_sem, small_sem = refs[len(gots) + 5 :]
    per_dev = out_ref.shape[0]
    table_copy = pltpu.make_async_copy(table_ref, table, small_sem.at[0])
    table_copy.start()
    table_copy.wait()
    slots = [table[(TABLE_PARTS - 1) * per_dev + p] for p in range(per_dev)]
    for p, slot in enumerate(slots):
        for k, got in enumerate(gots):
            copy = pltpu.make_async_copy(got.at[slot % PICKS], out_ref.at[p], copy_sem.at[p])
            pl.when(slot // PICKS == k)(copy.start)
    for d in range(doms):
        row = all_ref[d * tps]
        for t in range(1, tps):
            row = row + all_ref[d * tps + t]
        sums[d : d + 1, :] = row
    step_0, step_1, prior = (
        slice(k * per_dev, (k + 1) * per_dev) for k in range(3)
    )
    totals = sums[...]
    log_weights = totals[:, prior] + totals[:, step_1] - totals[:, step_0]
    largest = jnp.max(log_weights, keepdims=True)
    log_total = largest + jnp.log(jnp.sum(jnp.exp(log_weights - largest), keepdims=True))
    mine = sums[pl.ds(lax.axis_index("dom"), 1), :]
    own = mine[:, prior] + mine[:, step_1] - mine[:, step_0]
    twist[...] = jnp.concatenate([mine[:, step_0], mine[:, step_1]], axis=0)
    normal[...] = own - log_total
    results = [
        pltpu.make_async_copy(twist, twist_hbm, small_sem.at[1]),
        pltpu.make_async_copy(normal, normal_hbm, small_sem.at[2]),
    ]
    for copy in results:
        copy.start()
    for p, slot in enumerate(slots):
        copy = pltpu.make_async_copy(gots[0].at[0], out_ref.at[p], copy_sem.at[p])
        pl.when(slot >= 0)(copy.wait)
    for copy in results:
        copy.wait()


def finish(table, gots, held, shares, doms, tps):
    per_dev = held.shape[0]
    count = len(gots)
    vmem = pl.BlockSpec(memory_space=pltpu.VMEM)
    hbm = pl.BlockSpec(memory_space=pl.ANY)
    return pl.pallas_call(
        functools.partial(finish_kernel, doms, tps),
        out_shape=[
            jax.ShapeDtypeStruct(held.shape, held.dtype),
            jax.ShapeDtypeStruct((2, per_dev), jnp.float32),
            jax.ShapeDtypeStruct((1, per_dev), jnp.float32),
        ],
        in_specs=[vmem] + [vmem] * count + [hbm, vmem],
        out_specs=[hbm, hbm, hbm],
        input_output_aliases={1 + count: 0},
        scratch_shapes=[
            pltpu.SMEM(table.shape, jnp.int32),
            pltpu.VMEM((doms, HEAD_DIM), jnp.float32),
            pltpu.VMEM((2, per_dev), jnp.float32),
            pltpu.VMEM((1, per_dev), jnp.float32),
            pltpu.SemaphoreType.DMA((per_dev,)),
            pltpu.SemaphoreType.DMA((3,)),
        ],
        compiler_params=pltpu.CompilerParams(vmem_limit_bytes=VMEM_BYTES),
        cost_estimate=pl.CostEstimate(
            flops=0, bytes_accessed=held.size, transcendentals=0
        ),
        name="finish",
    )(table, *gots, held, shares)


def routes(doms, tps, steps):
    pairs = []
    for d in range(doms):
        for t in range(tps):
            target = d + steps[t % 2]
            if 0 <= target < doms:
                pairs.append((d * tps + t, target * tps + t))
    return pairs


def local(
    queries,
    new_kv,
    gen_cache,
    prompt_kv,
    lengths,
    ancestors,
    tokens,
    twist_vector,
    twist_bias,
    prior_weights,
):
    doms, tps = lax.axis_size("dom"), lax.axis_size("tp")
    per_dev = gen_cache.shape[0]
    step_pairs = list(zip(*ORDERS))
    everyone = ("dom", "tp")

    *sends, table = pack(
        lengths, ancestors, new_kv, gen_cache, doms, step_pairs
    )
    arrivals = [
        lax.ppermute(send, everyone, routes(doms, tps, steps))
        for send, steps in zip(sends, step_pairs)
    ]

    shares, resampled = attend(
        table,
        queries,
        prompt_kv,
        gen_cache,
        tokens,
        twist_bias,
        new_kv,
        twist_vector,
        prior_weights,
        doms * tps,
    )
    shares = lax.all_to_all(shares, everyone, 0, 0, tiled=True)
    resampled, twist, normalized = finish(table, arrivals, resampled, shares, doms, tps)
    return (twist, normalized.reshape(per_dev), resampled, table[:per_dev])


def solution(mesh):
    in_specs = (
        P(None, "dom", "tp"),
        P(None, "dom", "tp"),
        P("dom", None, "tp"),
        P(None, "tp"),
        P(),
        P(),
        P(None, "dom"),
        P("tp"),
        P(),
        P("dom"),
    )
    out_specs = (P(None, "dom"), P("dom"), P("dom", None, "tp"), P("dom"))
    return jax.shard_map(local, mesh=mesh, in_specs=in_specs, out_specs=out_specs, check_vma=False)
```

```python
import functools
import math

import jax
import jax.numpy as jnp
from jax import lax
from jax.experimental import pallas as pl
from jax.experimental.pallas import tpu as pltpu
from jax.sharding import PartitionSpec as P

HEAD_DIM = 128
SPAN = 2
PICKS = 2
TABLE_PARTS = 4
AHEAD = 2
NEG_FILL = -1e30
LOG2_E = math.log2(math.e)
KEY_CHUNK = 512
VMEM_BYTES = 44 * 1024 * 1024
ROW_TILE = 16
WINDOW = 2 * ROW_TILE

ORDERS = ((-2, 2, 1, -1), (2, -2, -1, 1))


def in_hbm(x):
    return pltpu.with_memory_space_constraint(x, pltpu.HBM)


def place_new_rows(cache, new_rows, length, slot, per_dev):
    rows, width = cache.shape
    first = pl.multiple_of(
        jnp.minimum(length // ROW_TILE * ROW_TILE, rows - WINDOW), ROW_TILE
    )
    row_ids = first + lax.broadcasted_iota(jnp.int32, (WINDOW, width), 0)
    old = cache[pl.ds(first, WINDOW), :].astype(jnp.float32)
    later = jnp.where(row_ids == length + 1, new_rows[pl.ds(per_dev + slot, 1), :], 0.0)
    later = jnp.where(row_ids == length, new_rows[pl.ds(slot, 1), :], later)
    cache[pl.ds(first, WINDOW), :] = jnp.where(row_ids < length, old, later).astype(
        jnp.bfloat16
    )

    def clear(tile, carry):
        start = pl.multiple_of(tile * ROW_TILE, ROW_TILE)
        cache[pl.ds(start, ROW_TILE), :] = jnp.zeros((ROW_TILE, width), jnp.bfloat16)
        return carry

    lax.fori_loop(first // ROW_TILE + WINDOW // ROW_TILE, rows // ROW_TILE, clear, 0)


def named_range(anc_ref, first, owner, per_dev):
    low, high = jnp.int32(per_dev), jnp.int32(-1)
    for j in range(per_dev):
        local = anc_ref[first + j] - owner * per_dev
        named = jnp.logical_and(local >= 0, local < per_dev)
        low = jnp.minimum(low, jnp.where(named, local, per_dev))
        high = jnp.maximum(high, jnp.where(named, local, -1))
    return low, high


def pack_kernel(per_dev, doms, step_pairs, len_hbm, anc_hbm, new_hbm, gen_hbm, *refs):
    sends = refs[: len(step_pairs)]
    table_hbm, table, len_ref, anc_ref, new_bf16, new_rows, list_sem, load_sem = refs[
        len(step_pairs) :
    ]
    new_at, own_at, anc_at, slot_at = (k * per_dev for k in range(TABLE_PARTS))
    lists = [
        pltpu.make_async_copy(anc_hbm, anc_ref, list_sem.at[0]),
        pltpu.make_async_copy(len_hbm, len_ref, list_sem.at[1]),
        pltpu.make_async_copy(new_hbm, new_bf16, list_sem.at[2]),
    ]
    for copy in lists:
        copy.start()
    me, odd = lax.axis_index("dom"), lax.axis_index("tp") % 2
    lists[0].wait()
    picks = []
    loads = []
    for k, (even_step, odd_step) in enumerate(step_pairs):
        reader = jnp.clip(me + jnp.where(odd == 1, odd_step, even_step), 0, doms - 1)
        low, high = named_range(anc_ref, reader * per_dev, me, per_dev)
        for i, pick in enumerate((jnp.minimum(low, per_dev - 1), jnp.maximum(high, 0))):
            target = sends[k].at[i]
            load = pltpu.make_async_copy(gen_hbm.at[pick], target, load_sem.at[len(loads)])
            load.start()
            picks.append((pick, target))
            loads.append(load)
    lists[1].wait()
    for j in range(per_dev):
        table[anc_at + j] = anc_ref[me * per_dev + j]
        table[new_at + j] = len_ref[anc_ref[me * per_dev + j]] + 2
        table[own_at + j] = len_ref[me * per_dev + j]
        table[slot_at + j] = -PICKS
    for k, (even_step, odd_step) in enumerate(step_pairs):
        source = me - jnp.where(odd == 1, odd_step, even_step)
        low, _ = named_range(anc_ref, me * per_dev, source, per_dev)
        for j in range(per_dev):
            local = anc_ref[me * per_dev + j] - source * per_dev
            named = jnp.logical_and(local >= 0, local < per_dev)
            slot = k * PICKS + jnp.where(local == low, 0, PICKS - 1)
            table[slot_at + j] = jnp.where(named, slot, table[slot_at + j])
    table_copy = pltpu.make_async_copy(table, table_hbm, list_sem.at[3])
    table_copy.start()
    lists[2].wait()
    new_rows[...] = new_bf16[...].astype(jnp.float32).reshape(new_rows.shape)
    for load, (pick, target) in zip(loads, picks):
        load.wait()
        place_new_rows(target, new_rows, len_ref[me * per_dev + pick], pick, per_dev)
    table_copy.wait()


def pack(lengths, ancestors, new_kv, gen_cache, doms, step_pairs):
    per_dev, rows, width = gen_cache.shape
    count = len(step_pairs)
    vmem = pl.BlockSpec(memory_space=pltpu.VMEM)
    hbm = pl.BlockSpec(memory_space=pltpu.HBM)
    block_bytes = PICKS * rows * width * 2
    return pl.pallas_call(
        functools.partial(pack_kernel, per_dev, doms, step_pairs),
        out_shape=[jax.ShapeDtypeStruct((PICKS, rows, width), jnp.bfloat16)] * count
        + [jax.ShapeDtypeStruct((TABLE_PARTS * per_dev,), jnp.int32)],
        in_specs=[hbm] * 4,
        out_specs=[vmem] * count + [hbm],
        scratch_shapes=[
            pltpu.SMEM((TABLE_PARTS * per_dev,), jnp.int32),
            pltpu.SMEM(lengths.shape, jnp.int32),
            pltpu.SMEM(ancestors.shape, jnp.int32),
            pltpu.VMEM(new_kv.shape, jnp.bfloat16),
            pltpu.VMEM((2 * per_dev, width), jnp.float32),
            pltpu.SemaphoreType.DMA((4,)),
            pltpu.SemaphoreType.DMA((count * PICKS,)),
        ],
        compiler_params=pltpu.CompilerParams(vmem_limit_bytes=VMEM_BYTES),
        cost_estimate=pl.CostEstimate(
            flops=0, bytes_accessed=2 * count * block_bytes, transcendentals=0
        ),
        name="pack_sends",
    )(*(in_hbm(x) for x in (lengths, ancestors, new_kv, gen_cache)))


def fold_lanes(block, combine, start):
    for first in range(0, block.shape[1], HEAD_DIM):
        start = combine(start, block[:, first : first + HEAD_DIM])
    return start


def attend_kernel(
    per_dev,
    group,
    kv_local,
    chunk,
    table_hbm,
    q_ref,
    prompt_hbm,
    gen_hbm,
    token_hbm,
    bias_hbm,
    new_ref,
    head_ref,
    prior_ref,
    share_ref,
    out_hbm,
    prompt,
    grown,
    new_rows,
    scores,
    tops,
    totals,
    mixed_ref,
    bias_rows,
    extra,
    table,
    token_ref,
    prompt_sem,
    gen_sem,
    out_sem,
    bias_sem,
    list_sem,
):
    me = lax.axis_index("dom")
    steps = q_ref.shape[0]
    rows, width = grown.shape[1:]
    chunks = prompt.shape[0] // chunk
    pair = 2 * HEAD_DIM
    scale = LOG2_E / math.sqrt(HEAD_DIM)
    base = steps * per_dev

    half = per_dev // 2
    per_chunk = per_dev // chunks

    def gen_load(p):
        return pltpu.make_async_copy(gen_hbm.at[p], grown.at[p], gen_sem.at[p])

    def prompt_load(j):
        part = pl.ds(pl.multiple_of(j * chunk, chunk), chunk)
        return pltpu.make_async_copy(prompt_hbm.at[part], prompt.at[part], prompt_sem.at[j])

    lists = [
        pltpu.make_async_copy(table_hbm, table, list_sem.at[0]),
        pltpu.make_async_copy(token_hbm, token_ref, list_sem.at[1]),
    ]
    for copy in lists:
        copy.start()
    def start_loads(j):
        prompt_load(j).start()
        for i in range(per_chunk):
            gen_load(j * per_chunk + i).start()

    for j in range(AHEAD):
        start_loads(j)

    for copy in lists:
        copy.wait()
    len_ref, anc_ref = (table.at[pl.ds(k * per_dev, per_dev)] for k in (1, 2))
    for i in range(base):
        row = token_ref[i // per_dev, i % per_dev] // HEAD_DIM
        pltpu.make_async_copy(bias_hbm.at[pl.ds(pl.multiple_of(row * HEAD_DIM, HEAD_DIM), HEAD_DIM)], bias_rows.at[i, 0], bias_sem.at[i]).start()

    new_rows[...] = new_ref[...].astype(jnp.float32).reshape(base, width)
    row_ids = lax.broadcasted_iota(jnp.int32, (rows, width), 0)

    def patch(p):
        gen_load(p).wait()
        behind = row_ids - len_ref[p]
        tail = jnp.where(behind == 1, new_rows[pl.ds(per_dev + p, 1), :], 0.0)
        tail = jnp.where(behind == 0, new_rows[pl.ds(p, 1), :], tail)
        grown[p] = jnp.where(behind < 0, grown[p].astype(jnp.float32), tail).astype(
            jnp.bfloat16
        )

    q2 = q_ref[...].reshape(base, q_ref.shape[-1])
    queries = [
        jnp.concatenate(
            [q2[:, h * HEAD_DIM : (h + 1) * HEAD_DIM] for h in range(c * group, (c + 1) * group)],
            axis=0,
        )
        for c in range(kv_local)
    ]

    def score(query_rows, keys):
        return lax.dot_general(
            query_rows, keys, (((1,), (1,)), ((), ())), preferred_element_type=jnp.float32
        )

    def mix(probs, values):
        return jnp.dot(probs, values, preferred_element_type=jnp.float32)

    tops[...] = jnp.full(tops.shape, NEG_FILL, jnp.float32)

    def score_chunk(j, carry):
        prompt_load(j).wait()
        pl.when(j + AHEAD < chunks)(functools.partial(start_loads, j + AHEAD))
        part = pl.ds(pl.multiple_of(j * chunk, chunk), chunk)
        for c in range(kv_local):
            block = score(queries[c], prompt[part, c * pair : c * pair + HEAD_DIM])
            scores[c, j] = block
            tops[c] = fold_lanes(block, jnp.maximum, tops[c])
        for i in range(per_chunk):
            patch(j * per_chunk + i)
        return carry

    lax.fori_loop(0, chunks, score_chunk, 0)

    homes = []
    for p in range(per_dev):
        local = anc_ref[p] - me * per_dev
        home = jnp.logical_and(local >= 0, local < per_dev)
        source = grown.at[jnp.clip(local, 0, per_dev - 1)]
        copy = pltpu.make_async_copy(source, out_hbm.at[p], out_sem.at[p])
        homes.append((home, copy))
        pl.when(home)(copy.start)

    row_ids = lax.broadcasted_iota(jnp.int32, (base, rows), 0)
    owner = row_ids % per_dev
    last = row_ids // per_dev
    for p in range(per_dev):
        last = last + jnp.where(owner == p, len_ref[p], 0)
    visible = lax.broadcasted_iota(jnp.int32, (base, rows), 1) <= last
    visible, lower, seat = (
        jnp.concatenate([part.astype(jnp.int32)] * group, axis=0)
        for part in (visible, owner < half, owner % half)
    )
    visible, lower = visible == 1, lower == 1

    def halves(block):
        block = block.astype(jnp.float32)
        parts = [jnp.where(lower, block, 0.0), jnp.where(lower, 0.0, block)]
        return jnp.concatenate(parts, axis=1).astype(jnp.bfloat16)

    def by_seat(blocks):
        chosen = blocks[:, :HEAD_DIM]
        for i in range(1, half):
            chosen = jnp.where(seat == i, blocks[:, i * HEAD_DIM : (i + 1) * HEAD_DIM], chosen)
        return chosen

    for c in range(kv_local):
        columns = slice(c * pair, c * pair + HEAD_DIM)
        keys = jnp.concatenate(
            [
                jnp.concatenate([grown[i, :, columns], grown[i + half, :, columns]], axis=1)
                for i in range(half)
            ],
            axis=0,
        )
        own = jnp.where(visible, by_seat(score(halves(queries[c]), keys)), NEG_FILL)
        top = jnp.max(jnp.maximum(tops[c], own), axis=1, keepdims=True)
        top = jnp.broadcast_to(top, own.shape)
        tops[c] = top
        exps = jnp.where(visible, jnp.exp2((own - top) * scale), 0.0)
        totals[c] = exps
        columns = slice(c * pair + HEAD_DIM, (c + 1) * pair)
        values = jnp.concatenate(
            [
                jnp.concatenate([grown[i, :, columns], grown[i + half, :, columns]], axis=0)
                for i in range(half)
            ],
            axis=1,
        )
        mixed_ref[c] = by_seat(mix(halves(exps), values))

    def mix_chunks(step, carry):
        for c in range(kv_local):
            top = jnp.concatenate([tops[c]] * (chunk // HEAD_DIM), axis=1)
            total, mixed = totals[c], mixed_ref[c]
            for i in range(AHEAD):
                j = step * AHEAD + i
                part = pl.ds(pl.multiple_of(j * chunk, chunk), chunk)
                exps = jnp.exp2((scores[c, j] - top) * scale)
                total = fold_lanes(exps, jnp.add, total)
                mixed = mixed + mix(
                    exps.astype(jnp.bfloat16), prompt[part, c * pair + HEAD_DIM : (c + 1) * pair]
                )
            totals[c] = total
            mixed_ref[c] = mixed
        return carry

    lax.fori_loop(0, chunks // AHEAD, mix_chunks, 0)
    weighted = jnp.zeros((base, HEAD_DIM), jnp.float32)
    for c in range(kv_local):
        mixed = mixed_ref[c] / jnp.sum(totals[c], axis=1, keepdims=True)
        for h in range(group):
            weighted = (
                weighted + mixed[h * base : (h + 1) * base] * head_ref[c * group + h][None, :]
            )
    row_ids = lax.broadcasted_iota(jnp.int32, (base, HEAD_DIM), 0)
    column = jnp.full((base, HEAD_DIM), -1, jnp.int32)
    for i in range(base):
        pltpu.make_async_copy(bias_hbm.at[pl.ds(0, HEAD_DIM)], bias_rows.at[i, 0], bias_sem.at[i]).wait()
        column = jnp.where(row_ids == i, token_ref[i // per_dev, i % per_dev] % HEAD_DIM, column)
    adds = lax.axis_index("tp") == 0
    lane_ids = lax.broadcasted_iota(jnp.int32, (base, HEAD_DIM), 1)
    bias = jnp.where(lane_ids == column, bias_rows[...].reshape(base, HEAD_DIM), 0.0)
    weighted = weighted + jnp.where(adds, bias, 0.0)
    extra[...] = jnp.zeros(extra.shape, jnp.float32)
    extra[:, base : base + per_dev] = jnp.where(adds, prior_ref[...], 0.0)
    padding = jnp.zeros((HEAD_DIM - base, HEAD_DIM), jnp.float32)
    square = jnp.concatenate([weighted, padding], axis=0)
    row = jnp.sum(square.T, axis=0, keepdims=True) + extra[...]
    share_ref[...] = jnp.broadcast_to(row[None], share_ref.shape)
    for home, copy in homes:
        pl.when(home)(copy.wait)


def attend(
    table,
    queries,
    prompt_kv,
    gen_cache,
    tokens,
    twist_bias,
    new_kv,
    twist_vector,
    prior_weights,
    devices,
):
    steps, per_dev, width = queries.shape
    keys, kv_width = prompt_kv.shape
    rows = gen_cache.shape[1]
    kv_local = kv_width // (2 * HEAD_DIM)
    group = width // (kv_local * HEAD_DIM)
    score_rows = steps * per_dev * group
    chunk = min(KEY_CHUNK, keys)
    head_weights = twist_vector.reshape(kv_local * group, HEAD_DIM)
    vmem = pl.BlockSpec(memory_space=pltpu.VMEM)
    hbm = pl.BlockSpec(memory_space=pltpu.HBM)
    score_count = score_rows * kv_local * (keys + rows)
    return pl.pallas_call(
        functools.partial(attend_kernel, per_dev, group, kv_local, chunk),
        out_shape=[
            jax.ShapeDtypeStruct((devices, 1, HEAD_DIM), jnp.float32),
            jax.ShapeDtypeStruct(gen_cache.shape, jnp.bfloat16),
        ],
        in_specs=[hbm, vmem, hbm, hbm, hbm, hbm, vmem, vmem, vmem],
        out_specs=[vmem, hbm],
        scratch_shapes=[
            pltpu.VMEM(prompt_kv.shape, jnp.bfloat16),
            pltpu.VMEM(gen_cache.shape, jnp.bfloat16),
            pltpu.VMEM((steps * per_dev, kv_width), jnp.float32),
            pltpu.VMEM((kv_local, keys // chunk, score_rows, chunk), jnp.float32),
            pltpu.VMEM((kv_local, score_rows, HEAD_DIM), jnp.float32),
            pltpu.VMEM((kv_local, score_rows, HEAD_DIM), jnp.float32),
            pltpu.VMEM((kv_local, score_rows, HEAD_DIM), jnp.float32),
            pltpu.VMEM((steps * per_dev, 1, HEAD_DIM), jnp.float32),
            pltpu.VMEM((1, HEAD_DIM), jnp.float32),
            pltpu.SMEM(table.shape, jnp.int32),
            pltpu.SMEM(tokens.shape, jnp.int32),
            pltpu.SemaphoreType.DMA((keys // chunk,)),
            pltpu.SemaphoreType.DMA((per_dev,)),
            pltpu.SemaphoreType.DMA((per_dev,)),
            pltpu.SemaphoreType.DMA((steps * per_dev,)),
            pltpu.SemaphoreType.DMA((2,)),
        ],
        compiler_params=pltpu.CompilerParams(vmem_limit_bytes=VMEM_BYTES),
        cost_estimate=pl.CostEstimate(
            flops=4 * score_count * HEAD_DIM,
            bytes_accessed=2 * (prompt_kv.size + 2 * gen_cache.size),
            transcendentals=score_count,
        ),
        name="attend",
    )(
        in_hbm(table),
        queries,
        in_hbm(prompt_kv),
        in_hbm(gen_cache),
        in_hbm(tokens),
        in_hbm(twist_bias),
        new_kv,
        head_weights,
        prior_weights[None],
    )


def finish_kernel(doms, tps, table_ref, *refs):
    gots = refs[: len(ORDERS[0])]
    _, all_ref, out_ref, twist_hbm, normal_hbm = refs[len(gots) : len(gots) + 5]
    table, sums, twist, normal, copy_sem, small_sem = refs[len(gots) + 5 :]
    per_dev = out_ref.shape[0]
    table_copy = pltpu.make_async_copy(table_ref, table, small_sem.at[0])
    table_copy.start()
    table_copy.wait()
    slots = [table[(TABLE_PARTS - 1) * per_dev + p] for p in range(per_dev)]
    for p, slot in enumerate(slots):
        for k, got in enumerate(gots):
            copy = pltpu.make_async_copy(got.at[slot % PICKS], out_ref.at[p], copy_sem.at[p])
            pl.when(slot // PICKS == k)(copy.start)
    for d in range(doms):
        row = all_ref[d * tps]
        for t in range(1, tps):
            row = row + all_ref[d * tps + t]
        sums[d : d + 1, :] = row
    step_0, step_1, prior = (
        slice(k * per_dev, (k + 1) * per_dev) for k in range(3)
    )
    totals = sums[...]
    log_weights = totals[:, prior] + totals[:, step_1] - totals[:, step_0]
    largest = jnp.max(log_weights, keepdims=True)
    log_total = largest + jnp.log(jnp.sum(jnp.exp(log_weights - largest), keepdims=True))
    mine = sums[pl.ds(lax.axis_index("dom"), 1), :]
    own = mine[:, prior] + mine[:, step_1] - mine[:, step_0]
    twist[...] = jnp.concatenate([mine[:, step_0], mine[:, step_1]], axis=0)
    normal[...] = own - log_total
    results = [
        pltpu.make_async_copy(twist, twist_hbm, small_sem.at[1]),
        pltpu.make_async_copy(normal, normal_hbm, small_sem.at[2]),
    ]
    for copy in results:
        copy.start()
    for p, slot in enumerate(slots):
        copy = pltpu.make_async_copy(gots[0].at[0], out_ref.at[p], copy_sem.at[p])
        pl.when(slot >= 0)(copy.wait)
    for copy in results:
        copy.wait()


def finish(table, gots, held, shares, doms, tps):
    per_dev = held.shape[0]
    count = len(gots)
    vmem = pl.BlockSpec(memory_space=pltpu.VMEM)
    hbm = pl.BlockSpec(memory_space=pl.ANY)
    return pl.pallas_call(
        functools.partial(finish_kernel, doms, tps),
        out_shape=[
            jax.ShapeDtypeStruct(held.shape, held.dtype),
            jax.ShapeDtypeStruct((2, per_dev), jnp.float32),
            jax.ShapeDtypeStruct((1, per_dev), jnp.float32),
        ],
        in_specs=[vmem] + [vmem] * count + [hbm, vmem],
        out_specs=[hbm, hbm, hbm],
        input_output_aliases={1 + count: 0},
        scratch_shapes=[
            pltpu.SMEM(table.shape, jnp.int32),
            pltpu.VMEM((doms, HEAD_DIM), jnp.float32),
            pltpu.VMEM((2, per_dev), jnp.float32),
            pltpu.VMEM((1, per_dev), jnp.float32),
            pltpu.SemaphoreType.DMA((per_dev,)),
            pltpu.SemaphoreType.DMA((3,)),
        ],
        compiler_params=pltpu.CompilerParams(vmem_limit_bytes=VMEM_BYTES),
        cost_estimate=pl.CostEstimate(
            flops=0, bytes_accessed=held.size, transcendentals=0
        ),
        name="finish",
    )(table, *gots, held, shares)


def routes(doms, tps, steps):
    pairs = []
    for d in range(doms):
        for t in range(tps):
            target = d + steps[t % 2]
            if 0 <= target < doms:
                pairs.append((d * tps + t, target * tps + t))
    return pairs


def local(
    queries,
    new_kv,
    gen_cache,
    prompt_kv,
    lengths,
    ancestors,
    tokens,
    twist_vector,
    twist_bias,
    prior_weights,
):
    doms, tps = lax.axis_size("dom"), lax.axis_size("tp")
    per_dev = gen_cache.shape[0]
    step_pairs = list(zip(*ORDERS))
    everyone = ("dom", "tp")

    *sends, table = pack(
        lengths, ancestors, new_kv, gen_cache, doms, step_pairs
    )
    arrivals = [
        lax.ppermute(send, everyone, routes(doms, tps, steps))
        for send, steps in zip(sends, step_pairs)
    ]

    shares, resampled = attend(
        table,
        queries,
        prompt_kv,
        gen_cache,
        tokens,
        twist_bias,
        new_kv,
        twist_vector,
        prior_weights,
        doms * tps,
    )
    shares = lax.all_to_all(shares, everyone, 0, 0, tiled=True)
    resampled, twist, normalized = finish(table, arrivals, resampled, shares, doms, tps)
    return (twist, normalized.reshape(per_dev), resampled, table[:per_dev])


def solution(mesh):
    in_specs = (
        P(None, "dom", "tp"),
        P(None, "dom", "tp"),
        P("dom", None, "tp"),
        P(None, "tp"),
        P(),
        P(),
        P(None, "dom"),
        P("tp"),
        P(),
        P("dom"),
    )
    out_specs = (P(None, "dom"), P("dom"), P("dom", None, "tp"), P("dom"))
    return jax.shard_map(local, mesh=mesh, in_specs=in_specs, out_specs=out_specs, check_vma=False)
```

```python
import functools
import math

import jax
import jax.numpy as jnp
from jax import lax
from jax.experimental import pallas as pl
from jax.experimental.pallas import tpu as pltpu
from jax.sharding import PartitionSpec as P

HEAD_DIM = 128
SPAN = 2
PICKS = 2
TABLE_PARTS = 4
AHEAD = 2
NEG_FILL = -1e30
LOG2_E = math.log2(math.e)
KEY_CHUNK = 512
VMEM_BYTES = 44 * 1024 * 1024
ROW_TILE = 16
WINDOW = 2 * ROW_TILE

ROUNDS = ((2, 0), (2, 2), (1, 0), (1, 1))


def is_first(device, distance, offset):
    return (device + distance * 2 - offset) % (2 * distance) < distance


def pairs(doms, distance, offset):
    return [
        [d, (d + distance) % doms] for d in range(doms) if is_first(d, distance, offset)
    ]


def partner(me, doms, distance, offset):
    step = jnp.where(is_first(me, distance, offset), distance, doms - distance)
    return (me + step) % doms


def in_hbm(x):
    return pltpu.with_memory_space_constraint(x, pltpu.HBM)


def place_new_rows(cache, new_rows, length, slot, per_dev):
    rows, width = cache.shape
    first = pl.multiple_of(
        jnp.minimum(length // ROW_TILE * ROW_TILE, rows - WINDOW), ROW_TILE
    )
    row_ids = first + lax.broadcasted_iota(jnp.int32, (WINDOW, width), 0)
    old = cache[pl.ds(first, WINDOW), :].astype(jnp.float32)
    later = jnp.where(row_ids == length + 1, new_rows[pl.ds(per_dev + slot, 1), :], 0.0)
    later = jnp.where(row_ids == length, new_rows[pl.ds(slot, 1), :], later)
    cache[pl.ds(first, WINDOW), :] = jnp.where(row_ids < length, old, later).astype(
        jnp.bfloat16
    )

    def clear(tile, carry):
        start = pl.multiple_of(tile * ROW_TILE, ROW_TILE)
        cache[pl.ds(start, ROW_TILE), :] = jnp.zeros((ROW_TILE, width), jnp.bfloat16)
        return carry

    lax.fori_loop(first // ROW_TILE + WINDOW // ROW_TILE, rows // ROW_TILE, clear, 0)


def named_range(anc_ref, first, owner, per_dev):
    low, high = jnp.int32(per_dev), jnp.int32(-1)
    for j in range(per_dev):
        local = anc_ref[first + j] - owner * per_dev
        named = jnp.logical_and(local >= 0, local < per_dev)
        low = jnp.minimum(low, jnp.where(named, local, per_dev))
        high = jnp.maximum(high, jnp.where(named, local, -1))
    return low, high


def pack_kernel(per_dev, doms, len_hbm, anc_hbm, new_hbm, gen_hbm, *refs):
    sends = refs[: len(ROUNDS)]
    table_hbm, table, len_ref, anc_ref, new_bf16, new_rows, list_sem, load_sem = refs[
        len(ROUNDS) :
    ]
    new_at, own_at, anc_at, slot_at = (k * per_dev for k in range(TABLE_PARTS))
    lists = [
        pltpu.make_async_copy(anc_hbm, anc_ref, list_sem.at[0]),
        pltpu.make_async_copy(len_hbm, len_ref, list_sem.at[1]),
        pltpu.make_async_copy(new_hbm, new_bf16, list_sem.at[2]),
    ]
    for copy in lists:
        copy.start()
    me = lax.axis_index("dom")
    lists[0].wait()
    picks = []
    loads = []
    for k, pairing in enumerate(ROUNDS):
        reader = partner(me, doms, *pairing)
        low, high = named_range(anc_ref, reader * per_dev, me, per_dev)
        for i, pick in enumerate((jnp.minimum(low, per_dev - 1), jnp.maximum(high, 0))):
            target = sends[k].at[i]
            load = pltpu.make_async_copy(gen_hbm.at[pick], target, load_sem.at[len(loads)])
            load.start()
            picks.append((pick, target))
            loads.append(load)
    lists[1].wait()
    for j in range(per_dev):
        table[anc_at + j] = anc_ref[me * per_dev + j]
        table[new_at + j] = len_ref[anc_ref[me * per_dev + j]] + 2
        table[own_at + j] = len_ref[me * per_dev + j]
        table[slot_at + j] = -PICKS
    for k, pairing in enumerate(ROUNDS):
        source = partner(me, doms, *pairing)
        low, _ = named_range(anc_ref, me * per_dev, source, per_dev)
        for j in range(per_dev):
            local = anc_ref[me * per_dev + j] - source * per_dev
            named = jnp.logical_and(local >= 0, local < per_dev)
            slot = k * PICKS + jnp.where(local == low, 0, PICKS - 1)
            table[slot_at + j] = jnp.where(named, slot, table[slot_at + j])
    table_copy = pltpu.make_async_copy(table, table_hbm, list_sem.at[3])
    table_copy.start()
    lists[2].wait()
    new_rows[...] = new_bf16[...].astype(jnp.float32).reshape(new_rows.shape)
    for load, (pick, target) in zip(loads, picks):
        load.wait()
        place_new_rows(target, new_rows, len_ref[me * per_dev + pick], pick, per_dev)
    table_copy.wait()


def pack(lengths, ancestors, new_kv, gen_cache, doms):
    per_dev, rows, width = gen_cache.shape
    count = len(ROUNDS)
    vmem = pl.BlockSpec(memory_space=pltpu.VMEM)
    hbm = pl.BlockSpec(memory_space=pltpu.HBM)
    block_bytes = PICKS * rows * width * 2
    return pl.pallas_call(
        functools.partial(pack_kernel, per_dev, doms),
        out_shape=[jax.ShapeDtypeStruct((PICKS, rows, width), jnp.bfloat16)] * count
        + [jax.ShapeDtypeStruct((TABLE_PARTS * per_dev,), jnp.int32)],
        in_specs=[hbm] * 4,
        out_specs=[vmem] * count + [hbm],
        scratch_shapes=[
            pltpu.SMEM((TABLE_PARTS * per_dev,), jnp.int32),
            pltpu.SMEM(lengths.shape, jnp.int32),
            pltpu.SMEM(ancestors.shape, jnp.int32),
            pltpu.VMEM(new_kv.shape, jnp.bfloat16),
            pltpu.VMEM((2 * per_dev, width), jnp.float32),
            pltpu.SemaphoreType.DMA((4,)),
            pltpu.SemaphoreType.DMA((count * PICKS,)),
        ],
        compiler_params=pltpu.CompilerParams(vmem_limit_bytes=VMEM_BYTES),
        cost_estimate=pl.CostEstimate(
            flops=0, bytes_accessed=2 * count * block_bytes, transcendentals=0
        ),
        name="pack_sends",
    )(*(in_hbm(x) for x in (lengths, ancestors, new_kv, gen_cache)))


def fold_lanes(block, combine, start):
    for first in range(0, block.shape[1], HEAD_DIM):
        start = combine(start, block[:, first : first + HEAD_DIM])
    return start


def attend_kernel(
    per_dev,
    group,
    kv_local,
    chunk,
    table_hbm,
    q_ref,
    prompt_hbm,
    gen_hbm,
    token_hbm,
    bias_hbm,
    new_ref,
    head_ref,
    prior_ref,
    share_ref,
    out_hbm,
    prompt,
    grown,
    new_rows,
    scores,
    tops,
    totals,
    mixed_ref,
    bias_rows,
    extra,
    table,
    token_ref,
    prompt_sem,
    gen_sem,
    out_sem,
    bias_sem,
    list_sem,
):
    me = lax.axis_index("dom")
    steps = q_ref.shape[0]
    rows, width = grown.shape[1:]
    chunks = prompt.shape[0] // chunk
    pair = 2 * HEAD_DIM
    scale = LOG2_E / math.sqrt(HEAD_DIM)
    base = steps * per_dev

    half = per_dev // 2
    per_chunk = per_dev // chunks

    def gen_load(p):
        return pltpu.make_async_copy(gen_hbm.at[p], grown.at[p], gen_sem.at[p])

    def prompt_load(j):
        part = pl.ds(pl.multiple_of(j * chunk, chunk), chunk)
        return pltpu.make_async_copy(prompt_hbm.at[part], prompt.at[part], prompt_sem.at[j])

    lists = [
        pltpu.make_async_copy(table_hbm, table, list_sem.at[0]),
        pltpu.make_async_copy(token_hbm, token_ref, list_sem.at[1]),
    ]
    for copy in lists:
        copy.start()
    def start_loads(j):
        prompt_load(j).start()
        for i in range(per_chunk):
            gen_load(j * per_chunk + i).start()

    for j in range(AHEAD):
        start_loads(j)

    for copy in lists:
        copy.wait()
    len_ref, anc_ref = (table.at[pl.ds(k * per_dev, per_dev)] for k in (1, 2))
    for i in range(base):
        row = token_ref[i // per_dev, i % per_dev] // HEAD_DIM
        pltpu.make_async_copy(bias_hbm.at[pl.ds(pl.multiple_of(row * HEAD_DIM, HEAD_DIM), HEAD_DIM)], bias_rows.at[i, 0], bias_sem.at[i]).start()

    new_rows[...] = new_ref[...].astype(jnp.float32).reshape(base, width)
    row_ids = lax.broadcasted_iota(jnp.int32, (rows, width), 0)

    def patch(p):
        gen_load(p).wait()
        behind = row_ids - len_ref[p]
        tail = jnp.where(behind == 1, new_rows[pl.ds(per_dev + p, 1), :], 0.0)
        tail = jnp.where(behind == 0, new_rows[pl.ds(p, 1), :], tail)
        grown[p] = jnp.where(behind < 0, grown[p].astype(jnp.float32), tail).astype(
            jnp.bfloat16
        )

    q2 = q_ref[...].reshape(base, q_ref.shape[-1])
    queries = [
        jnp.concatenate(
            [q2[:, h * HEAD_DIM : (h + 1) * HEAD_DIM] for h in range(c * group, (c + 1) * group)],
            axis=0,
        )
        for c in range(kv_local)
    ]

    def score(query_rows, keys):
        return lax.dot_general(
            query_rows, keys, (((1,), (1,)), ((), ())), preferred_element_type=jnp.float32
        )

    def mix(probs, values):
        return jnp.dot(probs, values, preferred_element_type=jnp.float32)

    tops[...] = jnp.full(tops.shape, NEG_FILL, jnp.float32)

    def score_chunk(j, carry):
        prompt_load(j).wait()
        pl.when(j + AHEAD < chunks)(functools.partial(start_loads, j + AHEAD))
        part = pl.ds(pl.multiple_of(j * chunk, chunk), chunk)
        for c in range(kv_local):
            block = score(queries[c], prompt[part, c * pair : c * pair + HEAD_DIM])
            scores[c, j] = block
            tops[c] = fold_lanes(block, jnp.maximum, tops[c])
        for i in range(per_chunk):
            patch(j * per_chunk + i)
        return carry

    lax.fori_loop(0, chunks, score_chunk, 0)

    homes = []
    for p in range(per_dev):
        local = anc_ref[p] - me * per_dev
        home = jnp.logical_and(local >= 0, local < per_dev)
        source = grown.at[jnp.clip(local, 0, per_dev - 1)]
        copy = pltpu.make_async_copy(source, out_hbm.at[p], out_sem.at[p])
        homes.append((home, copy))
        pl.when(home)(copy.start)

    row_ids = lax.broadcasted_iota(jnp.int32, (base, rows), 0)
    owner = row_ids % per_dev
    last = row_ids // per_dev
    for p in range(per_dev):
        last = last + jnp.where(owner == p, len_ref[p], 0)
    visible = lax.broadcasted_iota(jnp.int32, (base, rows), 1) <= last
    visible, lower, seat = (
        jnp.concatenate([part.astype(jnp.int32)] * group, axis=0)
        for part in (visible, owner < half, owner % half)
    )
    visible, lower = visible == 1, lower == 1

    def halves(block):
        block = block.astype(jnp.float32)
        parts = [jnp.where(lower, block, 0.0), jnp.where(lower, 0.0, block)]
        return jnp.concatenate(parts, axis=1).astype(jnp.bfloat16)

    def by_seat(blocks):
        chosen = blocks[:, :HEAD_DIM]
        for i in range(1, half):
            chosen = jnp.where(seat == i, blocks[:, i * HEAD_DIM : (i + 1) * HEAD_DIM], chosen)
        return chosen

    for c in range(kv_local):
        columns = slice(c * pair, c * pair + HEAD_DIM)
        keys = jnp.concatenate(
            [
                jnp.concatenate([grown[i, :, columns], grown[i + half, :, columns]], axis=1)
                for i in range(half)
            ],
            axis=0,
        )
        own = jnp.where(visible, by_seat(score(halves(queries[c]), keys)), NEG_FILL)
        top = jnp.max(jnp.maximum(tops[c], own), axis=1, keepdims=True)
        top = jnp.broadcast_to(top, own.shape)
        tops[c] = top
        exps = jnp.where(visible, jnp.exp2((own - top) * scale), 0.0)
        totals[c] = exps
        columns = slice(c * pair + HEAD_DIM, (c + 1) * pair)
        values = jnp.concatenate(
            [
                jnp.concatenate([grown[i, :, columns], grown[i + half, :, columns]], axis=0)
                for i in range(half)
            ],
            axis=1,
        )
        mixed_ref[c] = by_seat(mix(halves(exps), values))

    def mix_chunks(step, carry):
        for c in range(kv_local):
            top = jnp.concatenate([tops[c]] * (chunk // HEAD_DIM), axis=1)
            total, mixed = totals[c], mixed_ref[c]
            for i in range(AHEAD):
                j = step * AHEAD + i
                part = pl.ds(pl.multiple_of(j * chunk, chunk), chunk)
                exps = jnp.exp2((scores[c, j] - top) * scale)
                total = fold_lanes(exps, jnp.add, total)
                mixed = mixed + mix(
                    exps.astype(jnp.bfloat16), prompt[part, c * pair + HEAD_DIM : (c + 1) * pair]
                )
            totals[c] = total
            mixed_ref[c] = mixed
        return carry

    lax.fori_loop(0, chunks // AHEAD, mix_chunks, 0)
    weighted = jnp.zeros((base, HEAD_DIM), jnp.float32)
    for c in range(kv_local):
        mixed = mixed_ref[c] / jnp.sum(totals[c], axis=1, keepdims=True)
        for h in range(group):
            weighted = (
                weighted + mixed[h * base : (h + 1) * base] * head_ref[c * group + h][None, :]
            )
    row_ids = lax.broadcasted_iota(jnp.int32, (base, HEAD_DIM), 0)
    column = jnp.full((base, HEAD_DIM), -1, jnp.int32)
    for i in range(base):
        pltpu.make_async_copy(bias_hbm.at[pl.ds(0, HEAD_DIM)], bias_rows.at[i, 0], bias_sem.at[i]).wait()
        column = jnp.where(row_ids == i, token_ref[i // per_dev, i % per_dev] % HEAD_DIM, column)
    adds = lax.axis_index("tp") == 0
    lane_ids = lax.broadcasted_iota(jnp.int32, (base, HEAD_DIM), 1)
    bias = jnp.where(lane_ids == column, bias_rows[...].reshape(base, HEAD_DIM), 0.0)
    weighted = weighted + jnp.where(adds, bias, 0.0)
    extra[...] = jnp.zeros(extra.shape, jnp.float32)
    extra[:, base : base + per_dev] = jnp.where(adds, prior_ref[...], 0.0)
    padding = jnp.zeros((HEAD_DIM - base, HEAD_DIM), jnp.float32)
    square = jnp.concatenate([weighted, padding], axis=0)
    row = jnp.sum(square.T, axis=0, keepdims=True) + extra[...]
    share_ref[...] = jnp.broadcast_to(row[None], share_ref.shape)
    for home, copy in homes:
        pl.when(home)(copy.wait)


def attend(
    table,
    queries,
    prompt_kv,
    gen_cache,
    tokens,
    twist_bias,
    new_kv,
    twist_vector,
    prior_weights,
    devices,
):
    steps, per_dev, width = queries.shape
    keys, kv_width = prompt_kv.shape
    rows = gen_cache.shape[1]
    kv_local = kv_width // (2 * HEAD_DIM)
    group = width // (kv_local * HEAD_DIM)
    score_rows = steps * per_dev * group
    chunk = min(KEY_CHUNK, keys)
    head_weights = twist_vector.reshape(kv_local * group, HEAD_DIM)
    vmem = pl.BlockSpec(memory_space=pltpu.VMEM)
    hbm = pl.BlockSpec(memory_space=pltpu.HBM)
    score_count = score_rows * kv_local * (keys + rows)
    return pl.pallas_call(
        functools.partial(attend_kernel, per_dev, group, kv_local, chunk),
        out_shape=[
            jax.ShapeDtypeStruct((devices, 1, HEAD_DIM), jnp.float32),
            jax.ShapeDtypeStruct(gen_cache.shape, jnp.bfloat16),
        ],
        in_specs=[hbm, vmem, hbm, hbm, hbm, hbm, vmem, vmem, vmem],
        out_specs=[vmem, hbm],
        scratch_shapes=[
            pltpu.VMEM(prompt_kv.shape, jnp.bfloat16),
            pltpu.VMEM(gen_cache.shape, jnp.bfloat16),
            pltpu.VMEM((steps * per_dev, kv_width), jnp.float32),
            pltpu.VMEM((kv_local, keys // chunk, score_rows, chunk), jnp.float32),
            pltpu.VMEM((kv_local, score_rows, HEAD_DIM), jnp.float32),
            pltpu.VMEM((kv_local, score_rows, HEAD_DIM), jnp.float32),
            pltpu.VMEM((kv_local, score_rows, HEAD_DIM), jnp.float32),
            pltpu.VMEM((steps * per_dev, 1, HEAD_DIM), jnp.float32),
            pltpu.VMEM((1, HEAD_DIM), jnp.float32),
            pltpu.SMEM(table.shape, jnp.int32),
            pltpu.SMEM(tokens.shape, jnp.int32),
            pltpu.SemaphoreType.DMA((keys // chunk,)),
            pltpu.SemaphoreType.DMA((per_dev,)),
            pltpu.SemaphoreType.DMA((per_dev,)),
            pltpu.SemaphoreType.DMA((steps * per_dev,)),
            pltpu.SemaphoreType.DMA((2,)),
        ],
        compiler_params=pltpu.CompilerParams(vmem_limit_bytes=VMEM_BYTES),
        cost_estimate=pl.CostEstimate(
            flops=4 * score_count * HEAD_DIM,
            bytes_accessed=2 * (prompt_kv.size + 2 * gen_cache.size),
            transcendentals=score_count,
        ),
        name="attend",
    )(
        in_hbm(table),
        queries,
        in_hbm(prompt_kv),
        in_hbm(gen_cache),
        in_hbm(tokens),
        in_hbm(twist_bias),
        new_kv,
        head_weights,
        prior_weights[None],
    )


def finish_kernel(doms, tps, table_ref, *refs):
    gots = refs[: len(ROUNDS)]
    _, all_ref, out_ref, twist_hbm, normal_hbm = refs[len(gots) : len(gots) + 5]
    arrived, table, sums, twist, normal, load_sem, copy_sem, small_sem = refs[len(gots) + 5 :]
    per_dev = out_ref.shape[0]
    me = lax.axis_index("dom")
    loads = []
    for k, got in enumerate(gots):
        theirs = jnp.where(is_first(me, *ROUNDS[k]), 1, 0)
        loads.append(pltpu.make_async_copy(got.at[theirs], arrived.at[k], load_sem.at[k]))
        loads[-1].start()
    table_copy = pltpu.make_async_copy(table_ref, table, small_sem.at[0])
    table_copy.start()
    table_copy.wait()
    slots = [table[(TABLE_PARTS - 1) * per_dev + p] for p in range(per_dev)]
    for k, load in enumerate(loads):
        load.wait()
        for p, slot in enumerate(slots):
            copy = pltpu.make_async_copy(
                arrived.at[k, slot % PICKS], out_ref.at[p], copy_sem.at[p]
            )
            pl.when(slot // PICKS == k)(copy.start)
    for d in range(doms):
        row = all_ref[d * tps]
        for t in range(1, tps):
            row = row + all_ref[d * tps + t]
        sums[d : d + 1, :] = row
    step_0, step_1, prior = (
        slice(k * per_dev, (k + 1) * per_dev) for k in range(3)
    )
    totals = sums[...]
    log_weights = totals[:, prior] + totals[:, step_1] - totals[:, step_0]
    largest = jnp.max(log_weights, keepdims=True)
    log_total = largest + jnp.log(jnp.sum(jnp.exp(log_weights - largest), keepdims=True))
    mine = sums[pl.ds(lax.axis_index("dom"), 1), :]
    own = mine[:, prior] + mine[:, step_1] - mine[:, step_0]
    twist[...] = jnp.concatenate([mine[:, step_0], mine[:, step_1]], axis=0)
    normal[...] = own - log_total
    results = [
        pltpu.make_async_copy(twist, twist_hbm, small_sem.at[1]),
        pltpu.make_async_copy(normal, normal_hbm, small_sem.at[2]),
    ]
    for copy in results:
        copy.start()
    for p, slot in enumerate(slots):
        copy = pltpu.make_async_copy(arrived.at[0, 0], out_ref.at[p], copy_sem.at[p])
        pl.when(slot >= 0)(copy.wait)
    for copy in results:
        copy.wait()


def finish(table, gots, held, shares, doms, tps):
    per_dev = held.shape[0]
    count = len(gots)
    vmem = pl.BlockSpec(memory_space=pltpu.VMEM)
    hbm = pl.BlockSpec(memory_space=pl.ANY)
    return pl.pallas_call(
        functools.partial(finish_kernel, doms, tps),
        out_shape=[
            jax.ShapeDtypeStruct(held.shape, held.dtype),
            jax.ShapeDtypeStruct((2, per_dev), jnp.float32),
            jax.ShapeDtypeStruct((1, per_dev), jnp.float32),
        ],
        in_specs=[vmem] + [hbm] * count + [hbm, vmem],
        out_specs=[hbm, hbm, hbm],
        input_output_aliases={1 + count: 0},
        scratch_shapes=[
            pltpu.VMEM((count, *gots[0].shape[1:]), jnp.bfloat16),
            pltpu.SMEM(table.shape, jnp.int32),
            pltpu.VMEM((doms, HEAD_DIM), jnp.float32),
            pltpu.VMEM((2, per_dev), jnp.float32),
            pltpu.VMEM((1, per_dev), jnp.float32),
            pltpu.SemaphoreType.DMA((count,)),
            pltpu.SemaphoreType.DMA((per_dev,)),
            pltpu.SemaphoreType.DMA((3,)),
        ],
        compiler_params=pltpu.CompilerParams(vmem_limit_bytes=VMEM_BYTES),
        cost_estimate=pl.CostEstimate(
            flops=0, bytes_accessed=held.size, transcendentals=0
        ),
        name="finish",
    )(table, *(in_hbm(got) for got in gots), held, shares)


def local(
    queries,
    new_kv,
    gen_cache,
    prompt_kv,
    lengths,
    ancestors,
    tokens,
    twist_vector,
    twist_bias,
    prior_weights,
):
    doms, tps = lax.axis_size("dom"), lax.axis_size("tp")
    per_dev = gen_cache.shape[0]
    everyone = ("dom", "tp")

    *sends, table = pack(lengths, ancestors, new_kv, gen_cache, doms)
    arrivals = [
        lax.all_gather(send, "dom", axis_index_groups=pairs(doms, *pairing))
        for send, pairing in zip(sends, ROUNDS)
    ]

    shares, resampled = attend(
        table,
        queries,
        prompt_kv,
        gen_cache,
        tokens,
        twist_bias,
        new_kv,
        twist_vector,
        prior_weights,
        doms * tps,
    )
    shares = lax.all_to_all(shares, everyone, 0, 0, tiled=True)
    resampled, twist, normalized = finish(table, arrivals, resampled, shares, doms, tps)
    return (twist, normalized.reshape(per_dev), resampled, table[:per_dev])


def solution(mesh):
    in_specs = (
        P(None, "dom", "tp"),
        P(None, "dom", "tp"),
        P("dom", None, "tp"),
        P(None, "tp"),
        P(),
        P(),
        P(None, "dom"),
        P("tp"),
        P(),
        P("dom"),
    )
    out_specs = (P(None, "dom"), P("dom"), P("dom", None, "tp"), P("dom"))
    return jax.shard_map(local, mesh=mesh, in_specs=in_specs, out_specs=out_specs, check_vma=False)
```

```python
import functools
import math

import jax
import jax.numpy as jnp
from jax import lax
from jax.experimental import pallas as pl
from jax.experimental.pallas import tpu as pltpu
from jax.sharding import PartitionSpec as P

HEAD_DIM = 128
SPAN = 2
PICKS = 2
TABLE_PARTS = 4
AHEAD = 2
NEG_FILL = -1e30
LOG2_E = math.log2(math.e)
KEY_CHUNK = 512
VMEM_BYTES = 44 * 1024 * 1024
ROW_TILE = 16
WINDOW = 2 * ROW_TILE

ROUNDS = ((2, 0), (2, 2), (1, 0), (1, 1))


def is_first(device, distance, offset):
    return (device + distance * 2 - offset) % (2 * distance) < distance


def pairs(doms, distance, offset):
    return [
        [d, (d + distance) % doms] for d in range(doms) if is_first(d, distance, offset)
    ]


def swaps(doms, tps, distance, offset):
    routes = []
    for first, second in pairs(doms, distance, offset):
        if second - first == distance:
            for t in range(tps):
                ends = (first * tps + t, second * tps + t)
                routes += [ends, ends[::-1]]
    return routes


def partner(me, doms, distance, offset):
    step = jnp.where(is_first(me, distance, offset), distance, doms - distance)
    return (me + step) % doms


def in_hbm(x):
    return pltpu.with_memory_space_constraint(x, pltpu.HBM)


def place_new_rows(cache, new_rows, length, slot, per_dev):
    rows, width = cache.shape
    first = pl.multiple_of(
        jnp.minimum(length // ROW_TILE * ROW_TILE, rows - WINDOW), ROW_TILE
    )
    row_ids = first + lax.broadcasted_iota(jnp.int32, (WINDOW, width), 0)
    old = cache[pl.ds(first, WINDOW), :].astype(jnp.float32)
    later = jnp.where(row_ids == length + 1, new_rows[pl.ds(per_dev + slot, 1), :], 0.0)
    later = jnp.where(row_ids == length, new_rows[pl.ds(slot, 1), :], later)
    cache[pl.ds(first, WINDOW), :] = jnp.where(row_ids < length, old, later).astype(
        jnp.bfloat16
    )

    def clear(tile, carry):
        start = pl.multiple_of(tile * ROW_TILE, ROW_TILE)
        cache[pl.ds(start, ROW_TILE), :] = jnp.zeros((ROW_TILE, width), jnp.bfloat16)
        return carry

    lax.fori_loop(first // ROW_TILE + WINDOW // ROW_TILE, rows // ROW_TILE, clear, 0)


def named_range(anc_ref, first, owner, per_dev):
    low, high = jnp.int32(per_dev), jnp.int32(-1)
    for j in range(per_dev):
        local = anc_ref[first + j] - owner * per_dev
        named = jnp.logical_and(local >= 0, local < per_dev)
        low = jnp.minimum(low, jnp.where(named, local, per_dev))
        high = jnp.maximum(high, jnp.where(named, local, -1))
    return low, high


def pack_kernel(per_dev, doms, len_hbm, anc_hbm, new_hbm, gen_hbm, *refs):
    sends = refs[: len(ROUNDS)]
    table_hbm, table, len_ref, anc_ref, new_bf16, new_rows, held, list_sem, load_sem = refs[
        len(ROUNDS) :
    ]
    new_at, own_at, anc_at, slot_at = (k * per_dev for k in range(TABLE_PARTS))
    lists = [
        pltpu.make_async_copy(anc_hbm, anc_ref, list_sem.at[0]),
        pltpu.make_async_copy(len_hbm, len_ref, list_sem.at[1]),
        pltpu.make_async_copy(new_hbm, new_bf16, list_sem.at[2]),
    ]
    for copy in lists:
        copy.start()
    me = lax.axis_index("dom")
    lists[0].wait()
    picks = []
    loads = []
    for k, pairing in enumerate(ROUNDS):
        reader = partner(me, doms, *pairing)
        low, high = named_range(anc_ref, reader * per_dev, me, per_dev)
        for i, pick in enumerate((jnp.minimum(low, per_dev - 1), jnp.maximum(high, 0))):
            target = held.at[i] if k == 0 else sends[k].at[i]
            load = pltpu.make_async_copy(gen_hbm.at[pick], target, load_sem.at[len(loads)])
            load.start()
            picks.append((pick, target))
            loads.append(load)
    lists[1].wait()
    for j in range(per_dev):
        table[anc_at + j] = anc_ref[me * per_dev + j]
        table[new_at + j] = len_ref[anc_ref[me * per_dev + j]] + 2
        table[own_at + j] = len_ref[me * per_dev + j]
        table[slot_at + j] = -PICKS
    for k, pairing in enumerate(ROUNDS):
        source = partner(me, doms, *pairing)
        low, _ = named_range(anc_ref, me * per_dev, source, per_dev)
        for j in range(per_dev):
            local = anc_ref[me * per_dev + j] - source * per_dev
            named = jnp.logical_and(local >= 0, local < per_dev)
            slot = k * PICKS + jnp.where(local == low, 0, PICKS - 1)
            table[slot_at + j] = jnp.where(named, slot, table[slot_at + j])
    table_copy = pltpu.make_async_copy(table, table_hbm, list_sem.at[3])
    table_copy.start()
    lists[2].wait()
    new_rows[...] = new_bf16[...].astype(jnp.float32).reshape(new_rows.shape)
    first_send = pltpu.make_async_copy(held, sends[0], list_sem.at[4])
    for k, (load, (pick, target)) in enumerate(zip(loads, picks)):
        load.wait()
        place_new_rows(target, new_rows, len_ref[me * per_dev + pick], pick, per_dev)
        if k == PICKS - 1:
            first_send.start()
    table_copy.wait()
    first_send.wait()


def pack(lengths, ancestors, new_kv, gen_cache, doms):
    per_dev, rows, width = gen_cache.shape
    count = len(ROUNDS)
    vmem = pl.BlockSpec(memory_space=pltpu.VMEM)
    hbm = pl.BlockSpec(memory_space=pltpu.HBM)
    block_bytes = PICKS * rows * width * 2
    return pl.pallas_call(
        functools.partial(pack_kernel, per_dev, doms),
        out_shape=[jax.ShapeDtypeStruct((PICKS, rows, width), jnp.bfloat16)] * count
        + [jax.ShapeDtypeStruct((TABLE_PARTS * per_dev,), jnp.int32)],
        in_specs=[hbm] * 4,
        out_specs=[hbm] + [vmem] * (count - 1) + [hbm],
        scratch_shapes=[
            pltpu.SMEM((TABLE_PARTS * per_dev,), jnp.int32),
            pltpu.SMEM(lengths.shape, jnp.int32),
            pltpu.SMEM(ancestors.shape, jnp.int32),
            pltpu.VMEM(new_kv.shape, jnp.bfloat16),
            pltpu.VMEM((2 * per_dev, width), jnp.float32),
            pltpu.VMEM((PICKS, rows, width), jnp.bfloat16),
            pltpu.SemaphoreType.DMA((5,)),
            pltpu.SemaphoreType.DMA((count * PICKS,)),
        ],
        compiler_params=pltpu.CompilerParams(vmem_limit_bytes=VMEM_BYTES),
        cost_estimate=pl.CostEstimate(
            flops=0, bytes_accessed=2 * count * block_bytes, transcendentals=0
        ),
        name="pack_sends",
    )(*(in_hbm(x) for x in (lengths, ancestors, new_kv, gen_cache)))


def fold_lanes(block, combine, start):
    for first in range(0, block.shape[1], HEAD_DIM):
        start = combine(start, block[:, first : first + HEAD_DIM])
    return start


def attend_kernel(
    per_dev,
    group,
    kv_local,
    chunk,
    table_hbm,
    q_ref,
    prompt_hbm,
    gen_hbm,
    token_hbm,
    bias_hbm,
    new_ref,
    head_ref,
    prior_ref,
    share_ref,
    out_hbm,
    prompt,
    grown,
    new_rows,
    scores,
    tops,
    totals,
    mixed_ref,
    bias_rows,
    extra,
    table,
    token_ref,
    prompt_sem,
    gen_sem,
    out_sem,
    bias_sem,
    list_sem,
):
    me = lax.axis_index("dom")
    steps = q_ref.shape[0]
    rows, width = grown.shape[1:]
    chunks = prompt.shape[0] // chunk
    pair = 2 * HEAD_DIM
    scale = LOG2_E / math.sqrt(HEAD_DIM)
    base = steps * per_dev

    half = per_dev // 2
    per_chunk = per_dev // chunks

    def gen_load(p):
        return pltpu.make_async_copy(gen_hbm.at[p], grown.at[p], gen_sem.at[p])

    def prompt_load(j):
        part = pl.ds(pl.multiple_of(j * chunk, chunk), chunk)
        return pltpu.make_async_copy(prompt_hbm.at[part], prompt.at[part], prompt_sem.at[j])

    lists = [
        pltpu.make_async_copy(table_hbm, table, list_sem.at[0]),
        pltpu.make_async_copy(token_hbm, token_ref, list_sem.at[1]),
    ]
    for copy in lists:
        copy.start()
    def start_loads(j):
        prompt_load(j).start()
        for i in range(per_chunk):
            gen_load(j * per_chunk + i).start()

    for j in range(AHEAD):
        start_loads(j)

    for copy in lists:
        copy.wait()
    len_ref, anc_ref = (table.at[pl.ds(k * per_dev, per_dev)] for k in (1, 2))
    for i in range(base):
        row = token_ref[i // per_dev, i % per_dev] // HEAD_DIM
        pltpu.make_async_copy(bias_hbm.at[pl.ds(pl.multiple_of(row * HEAD_DIM, HEAD_DIM), HEAD_DIM)], bias_rows.at[i, 0], bias_sem.at[i]).start()

    new_rows[...] = new_ref[...].astype(jnp.float32).reshape(base, width)
    row_ids = lax.broadcasted_iota(jnp.int32, (rows, width), 0)

    def patch(p):
        gen_load(p).wait()
        behind = row_ids - len_ref[p]
        tail = jnp.where(behind == 1, new_rows[pl.ds(per_dev + p, 1), :], 0.0)
        tail = jnp.where(behind == 0, new_rows[pl.ds(p, 1), :], tail)
        grown[p] = jnp.where(behind < 0, grown[p].astype(jnp.float32), tail).astype(
            jnp.bfloat16
        )

    q2 = q_ref[...].reshape(base, q_ref.shape[-1])
    queries = [
        jnp.concatenate(
            [q2[:, h * HEAD_DIM : (h + 1) * HEAD_DIM] for h in range(c * group, (c + 1) * group)],
            axis=0,
        )
        for c in range(kv_local)
    ]

    def score(query_rows, keys):
        return lax.dot_general(
            query_rows, keys, (((1,), (1,)), ((), ())), preferred_element_type=jnp.float32
        )

    def mix(probs, values):
        return jnp.dot(probs, values, preferred_element_type=jnp.float32)

    tops[...] = jnp.full(tops.shape, NEG_FILL, jnp.float32)

    def score_chunk(j, carry):
        prompt_load(j).wait()
        pl.when(j + AHEAD < chunks)(functools.partial(start_loads, j + AHEAD))
        part = pl.ds(pl.multiple_of(j * chunk, chunk), chunk)
        for c in range(kv_local):
            block = score(queries[c], prompt[part, c * pair : c * pair + HEAD_DIM])
            scores[c, j] = block
            tops[c] = fold_lanes(block, jnp.maximum, tops[c])
        for i in range(per_chunk):
            patch(j * per_chunk + i)
        return carry

    lax.fori_loop(0, chunks, score_chunk, 0)

    homes = []
    for p in range(per_dev):
        local = anc_ref[p] - me * per_dev
        home = jnp.logical_and(local >= 0, local < per_dev)
        source = grown.at[jnp.clip(local, 0, per_dev - 1)]
        copy = pltpu.make_async_copy(source, out_hbm.at[p], out_sem.at[p])
        homes.append((home, copy))
        pl.when(home)(copy.start)

    row_ids = lax.broadcasted_iota(jnp.int32, (base, rows), 0)
    owner = row_ids % per_dev
    last = row_ids // per_dev
    for p in range(per_dev):
        last = last + jnp.where(owner == p, len_ref[p], 0)
    visible = lax.broadcasted_iota(jnp.int32, (base, rows), 1) <= last
    visible, lower, seat = (
        jnp.concatenate([part.astype(jnp.int32)] * group, axis=0)
        for part in (visible, owner < half, owner % half)
    )
    visible, lower = visible == 1, lower == 1

    def halves(block):
        block = block.astype(jnp.float32)
        parts = [jnp.where(lower, block, 0.0), jnp.where(lower, 0.0, block)]
        return jnp.concatenate(parts, axis=1).astype(jnp.bfloat16)

    def by_seat(blocks):
        chosen = blocks[:, :HEAD_DIM]
        for i in range(1, half):
            chosen = jnp.where(seat == i, blocks[:, i * HEAD_DIM : (i + 1) * HEAD_DIM], chosen)
        return chosen

    for c in range(kv_local):
        columns = slice(c * pair, c * pair + HEAD_DIM)
        keys = jnp.concatenate(
            [
                jnp.concatenate([grown[i, :, columns], grown[i + half, :, columns]], axis=1)
                for i in range(half)
            ],
            axis=0,
        )
        own = jnp.where(visible, by_seat(score(halves(queries[c]), keys)), NEG_FILL)
        top = jnp.max(jnp.maximum(tops[c], own), axis=1, keepdims=True)
        top = jnp.broadcast_to(top, own.shape)
        tops[c] = top
        exps = jnp.where(visible, jnp.exp2((own - top) * scale), 0.0)
        totals[c] = exps
        columns = slice(c * pair + HEAD_DIM, (c + 1) * pair)
        values = jnp.concatenate(
            [
                jnp.concatenate([grown[i, :, columns], grown[i + half, :, columns]], axis=0)
                for i in range(half)
            ],
            axis=1,
        )
        mixed_ref[c] = by_seat(mix(halves(exps), values))

    def mix_chunks(step, carry):
        for c in range(kv_local):
            top = jnp.concatenate([tops[c]] * (chunk // HEAD_DIM), axis=1)
            total, mixed = totals[c], mixed_ref[c]
            for i in range(AHEAD):
                j = step * AHEAD + i
                part = pl.ds(pl.multiple_of(j * chunk, chunk), chunk)
                exps = jnp.exp2((scores[c, j] - top) * scale)
                total = fold_lanes(exps, jnp.add, total)
                mixed = mixed + mix(
                    exps.astype(jnp.bfloat16), prompt[part, c * pair + HEAD_DIM : (c + 1) * pair]
                )
            totals[c] = total
            mixed_ref[c] = mixed
        return carry

    lax.fori_loop(0, chunks // AHEAD, mix_chunks, 0)
    weighted = jnp.zeros((base, HEAD_DIM), jnp.float32)
    for c in range(kv_local):
        mixed = mixed_ref[c] / jnp.sum(totals[c], axis=1, keepdims=True)
        for h in range(group):
            weighted = (
                weighted + mixed[h * base : (h + 1) * base] * head_ref[c * group + h][None, :]
            )
    row_ids = lax.broadcasted_iota(jnp.int32, (base, HEAD_DIM), 0)
    column = jnp.full((base, HEAD_DIM), -1, jnp.int32)
    for i in range(base):
        pltpu.make_async_copy(bias_hbm.at[pl.ds(0, HEAD_DIM)], bias_rows.at[i, 0], bias_sem.at[i]).wait()
        column = jnp.where(row_ids == i, token_ref[i // per_dev, i % per_dev] % HEAD_DIM, column)
    adds = lax.axis_index("tp") == 0
    lane_ids = lax.broadcasted_iota(jnp.int32, (base, HEAD_DIM), 1)
    bias = jnp.where(lane_ids == column, bias_rows[...].reshape(base, HEAD_DIM), 0.0)
    weighted = weighted + jnp.where(adds, bias, 0.0)
    extra[...] = jnp.zeros(extra.shape, jnp.float32)
    extra[:, base : base + per_dev] = jnp.where(adds, prior_ref[...], 0.0)
    padding = jnp.zeros((HEAD_DIM - base, HEAD_DIM), jnp.float32)
    square = jnp.concatenate([weighted, padding], axis=0)
    row = jnp.sum(square.T, axis=0, keepdims=True) + extra[...]
    share_ref[...] = jnp.broadcast_to(row[None], share_ref.shape)
    for home, copy in homes:
        pl.when(home)(copy.wait)


def attend(
    table,
    queries,
    prompt_kv,
    gen_cache,
    tokens,
    twist_bias,
    new_kv,
    twist_vector,
    prior_weights,
    devices,
):
    steps, per_dev, width = queries.shape
    keys, kv_width = prompt_kv.shape
    rows = gen_cache.shape[1]
    kv_local = kv_width // (2 * HEAD_DIM)
    group = width // (kv_local * HEAD_DIM)
    score_rows = steps * per_dev * group
    chunk = min(KEY_CHUNK, keys)
    head_weights = twist_vector.reshape(kv_local * group, HEAD_DIM)
    vmem = pl.BlockSpec(memory_space=pltpu.VMEM)
    hbm = pl.BlockSpec(memory_space=pltpu.HBM)
    score_count = score_rows * kv_local * (keys + rows)
    return pl.pallas_call(
        functools.partial(attend_kernel, per_dev, group, kv_local, chunk),
        out_shape=[
            jax.ShapeDtypeStruct((devices, 1, HEAD_DIM), jnp.float32),
            jax.ShapeDtypeStruct(gen_cache.shape, jnp.bfloat16),
        ],
        in_specs=[hbm, vmem, hbm, hbm, hbm, hbm, vmem, vmem, vmem],
        out_specs=[vmem, hbm],
        scratch_shapes=[
            pltpu.VMEM(prompt_kv.shape, jnp.bfloat16),
            pltpu.VMEM(gen_cache.shape, jnp.bfloat16),
            pltpu.VMEM((steps * per_dev, kv_width), jnp.float32),
            pltpu.VMEM((kv_local, keys // chunk, score_rows, chunk), jnp.float32),
            pltpu.VMEM((kv_local, score_rows, HEAD_DIM), jnp.float32),
            pltpu.VMEM((kv_local, score_rows, HEAD_DIM), jnp.float32),
            pltpu.VMEM((kv_local, score_rows, HEAD_DIM), jnp.float32),
            pltpu.VMEM((steps * per_dev, 1, HEAD_DIM), jnp.float32),
            pltpu.VMEM((1, HEAD_DIM), jnp.float32),
            pltpu.SMEM(table.shape, jnp.int32),
            pltpu.SMEM(tokens.shape, jnp.int32),
            pltpu.SemaphoreType.DMA((keys // chunk,)),
            pltpu.SemaphoreType.DMA((per_dev,)),
            pltpu.SemaphoreType.DMA((per_dev,)),
            pltpu.SemaphoreType.DMA((steps * per_dev,)),
            pltpu.SemaphoreType.DMA((2,)),
        ],
        compiler_params=pltpu.CompilerParams(vmem_limit_bytes=VMEM_BYTES),
        cost_estimate=pl.CostEstimate(
            flops=4 * score_count * HEAD_DIM,
            bytes_accessed=2 * (prompt_kv.size + 2 * gen_cache.size),
            transcendentals=score_count,
        ),
        name="attend",
    )(
        in_hbm(table),
        queries,
        in_hbm(prompt_kv),
        in_hbm(gen_cache),
        in_hbm(tokens),
        in_hbm(twist_bias),
        new_kv,
        head_weights,
        prior_weights[None],
    )


def finish_kernel(doms, tps, table_ref, *refs):
    gots = refs[: len(ROUNDS)]
    _, all_ref, out_ref, twist_hbm, normal_hbm = refs[len(gots) : len(gots) + 5]
    arrived, table, sums, twist, normal, load_sem, copy_sem, small_sem = refs[len(gots) + 5 :]
    per_dev = out_ref.shape[0]
    theirs = jnp.where(is_first(lax.axis_index("dom"), *ROUNDS[0]), 1, 0)
    load = pltpu.make_async_copy(gots[0].at[theirs], arrived, load_sem)
    load.start()
    table_copy = pltpu.make_async_copy(table_ref, table, small_sem.at[0])
    table_copy.start()
    table_copy.wait()
    slots = [table[(TABLE_PARTS - 1) * per_dev + p] for p in range(per_dev)]
    for p, slot in enumerate(slots):
        for k in range(1, len(gots)):
            copy = pltpu.make_async_copy(gots[k].at[slot % PICKS], out_ref.at[p], copy_sem.at[p])
            pl.when(slot // PICKS == k)(copy.start)
    load.wait()
    for p, slot in enumerate(slots):
        copy = pltpu.make_async_copy(arrived.at[slot % PICKS], out_ref.at[p], copy_sem.at[p])
        pl.when(slot // PICKS == 0)(copy.start)
    for d in range(doms):
        row = all_ref[d * tps]
        for t in range(1, tps):
            row = row + all_ref[d * tps + t]
        sums[d : d + 1, :] = row
    step_0, step_1, prior = (
        slice(k * per_dev, (k + 1) * per_dev) for k in range(3)
    )
    totals = sums[...]
    log_weights = totals[:, prior] + totals[:, step_1] - totals[:, step_0]
    largest = jnp.max(log_weights, keepdims=True)
    log_total = largest + jnp.log(jnp.sum(jnp.exp(log_weights - largest), keepdims=True))
    mine = sums[pl.ds(lax.axis_index("dom"), 1), :]
    own = mine[:, prior] + mine[:, step_1] - mine[:, step_0]
    twist[...] = jnp.concatenate([mine[:, step_0], mine[:, step_1]], axis=0)
    normal[...] = own - log_total
    results = [
        pltpu.make_async_copy(twist, twist_hbm, small_sem.at[1]),
        pltpu.make_async_copy(normal, normal_hbm, small_sem.at[2]),
    ]
    for copy in results:
        copy.start()
    for p, slot in enumerate(slots):
        copy = pltpu.make_async_copy(arrived.at[0], out_ref.at[p], copy_sem.at[p])
        pl.when(slot >= 0)(copy.wait)
    for copy in results:
        copy.wait()


def finish(table, gots, held, shares, doms, tps):
    per_dev = held.shape[0]
    count = len(gots)
    vmem = pl.BlockSpec(memory_space=pltpu.VMEM)
    hbm = pl.BlockSpec(memory_space=pl.ANY)
    return pl.pallas_call(
        functools.partial(finish_kernel, doms, tps),
        out_shape=[
            jax.ShapeDtypeStruct(held.shape, held.dtype),
            jax.ShapeDtypeStruct((2, per_dev), jnp.float32),
            jax.ShapeDtypeStruct((1, per_dev), jnp.float32),
        ],
        in_specs=[vmem, hbm] + [vmem] * (count - 1) + [hbm, vmem],
        out_specs=[hbm, hbm, hbm],
        input_output_aliases={1 + count: 0},
        scratch_shapes=[
            pltpu.VMEM(gots[0].shape[1:], jnp.bfloat16),
            pltpu.SMEM(table.shape, jnp.int32),
            pltpu.VMEM((doms, HEAD_DIM), jnp.float32),
            pltpu.VMEM((2, per_dev), jnp.float32),
            pltpu.VMEM((1, per_dev), jnp.float32),
            pltpu.SemaphoreType.DMA,
            pltpu.SemaphoreType.DMA((per_dev,)),
            pltpu.SemaphoreType.DMA((3,)),
        ],
        compiler_params=pltpu.CompilerParams(vmem_limit_bytes=VMEM_BYTES),
        cost_estimate=pl.CostEstimate(
            flops=0, bytes_accessed=held.size, transcendentals=0
        ),
        name="finish",
    )(table, in_hbm(gots[0]), *gots[1:], held, shares)


def local(
    queries,
    new_kv,
    gen_cache,
    prompt_kv,
    lengths,
    ancestors,
    tokens,
    twist_vector,
    twist_bias,
    prior_weights,
):
    doms, tps = lax.axis_size("dom"), lax.axis_size("tp")
    per_dev = gen_cache.shape[0]
    everyone = ("dom", "tp")

    *sends, table = pack(lengths, ancestors, new_kv, gen_cache, doms)
    arrivals = [lax.all_gather(sends[0], "dom", axis_index_groups=pairs(doms, *ROUNDS[0]))]
    for send, pairing in zip(sends[1:], ROUNDS[1:]):
        arrivals.append(lax.ppermute(send, everyone, swaps(doms, tps, *pairing)))

    shares, resampled = attend(
        table,
        queries,
        prompt_kv,
        gen_cache,
        tokens,
        twist_bias,
        new_kv,
        twist_vector,
        prior_weights,
        doms * tps,
    )
    shares = lax.all_to_all(shares, everyone, 0, 0, tiled=True)
    resampled, twist, normalized = finish(table, arrivals, resampled, shares, doms, tps)
    return (twist, normalized.reshape(per_dev), resampled, table[:per_dev])


def solution(mesh):
    in_specs = (
        P(None, "dom", "tp"),
        P(None, "dom", "tp"),
        P("dom", None, "tp"),
        P(None, "tp"),
        P(),
        P(),
        P(None, "dom"),
        P("tp"),
        P(),
        P("dom"),
    )
    out_specs = (P(None, "dom"), P("dom"), P("dom", None, "tp"), P("dom"))
    return jax.shard_map(local, mesh=mesh, in_specs=in_specs, out_specs=out_specs, check_vma=False)
```

```python
import functools
import math

import jax
import jax.numpy as jnp
from jax import lax
from jax.experimental import pallas as pl
from jax.experimental.pallas import tpu as pltpu
from jax.sharding import PartitionSpec as P

HEAD_DIM = 128
SPAN = 2
PICKS = 2
TABLE_PARTS = 4
AHEAD = 2
NEG_FILL = -1e30
LOG2_E = math.log2(math.e)
KEY_CHUNK = 512
VMEM_BYTES = 44 * 1024 * 1024
ROW_TILE = 16
WINDOW = 2 * ROW_TILE

ROUNDS = ((2, 0), (2, 2), (1, 0), (1, 1))


def is_first(device, distance, offset):
    return (device + distance * 2 - offset) % (2 * distance) < distance


def pairs(doms, distance, offset):
    return [
        [d, (d + distance) % doms] for d in range(doms) if is_first(d, distance, offset)
    ]


def swaps(doms, tps, distance, offset):
    routes = []
    for first, second in pairs(doms, distance, offset):
        if second - first == distance:
            for t in range(tps):
                ends = (first * tps + t, second * tps + t)
                routes += [ends, ends[::-1]]
    return routes


def partner(me, doms, distance, offset):
    step = jnp.where(is_first(me, distance, offset), distance, doms - distance)
    return (me + step) % doms


def in_hbm(x):
    return pltpu.with_memory_space_constraint(x, pltpu.HBM)


def place_new_rows(cache, new_rows, length, slot, per_dev):
    rows, width = cache.shape
    first = pl.multiple_of(
        jnp.minimum(length // ROW_TILE * ROW_TILE, rows - WINDOW), ROW_TILE
    )
    row_ids = first + lax.broadcasted_iota(jnp.int32, (WINDOW, width), 0)
    old = cache[pl.ds(first, WINDOW), :].astype(jnp.float32)
    later = jnp.where(row_ids == length + 1, new_rows[pl.ds(per_dev + slot, 1), :], 0.0)
    later = jnp.where(row_ids == length, new_rows[pl.ds(slot, 1), :], later)
    cache[pl.ds(first, WINDOW), :] = jnp.where(row_ids < length, old, later).astype(
        jnp.bfloat16
    )

    def clear(tile, carry):
        start = pl.multiple_of(tile * ROW_TILE, ROW_TILE)
        cache[pl.ds(start, ROW_TILE), :] = jnp.zeros((ROW_TILE, width), jnp.bfloat16)
        return carry

    lax.fori_loop(first // ROW_TILE + WINDOW // ROW_TILE, rows // ROW_TILE, clear, 0)


def named_range(anc_ref, first, owner, per_dev):
    low, high = jnp.int32(per_dev), jnp.int32(-1)
    for j in range(per_dev):
        local = anc_ref[first + j] - owner * per_dev
        named = jnp.logical_and(local >= 0, local < per_dev)
        low = jnp.minimum(low, jnp.where(named, local, per_dev))
        high = jnp.maximum(high, jnp.where(named, local, -1))
    return low, high


def pack_kernel(per_dev, doms, len_hbm, anc_hbm, new_hbm, gen_hbm, *refs):
    sends = refs[: len(ROUNDS)]
    table_hbm, table, len_ref, anc_ref, new_bf16, new_rows, list_sem, load_sem = refs[
        len(ROUNDS) :
    ]
    new_at, own_at, anc_at, slot_at = (k * per_dev for k in range(TABLE_PARTS))
    lists = [
        pltpu.make_async_copy(anc_hbm, anc_ref, list_sem.at[0]),
        pltpu.make_async_copy(len_hbm, len_ref, list_sem.at[1]),
        pltpu.make_async_copy(new_hbm, new_bf16, list_sem.at[2]),
    ]
    for copy in lists:
        copy.start()
    me = lax.axis_index("dom")
    lists[0].wait()
    picks = []
    loads = []
    for k, pairing in enumerate(ROUNDS):
        reader = partner(me, doms, *pairing)
        low, high = named_range(anc_ref, reader * per_dev, me, per_dev)
        for i, pick in enumerate((jnp.minimum(low, per_dev - 1), jnp.maximum(high, 0))):
            target = sends[k].at[i]
            load = pltpu.make_async_copy(gen_hbm.at[pick], target, load_sem.at[len(loads)])
            load.start()
            picks.append((pick, target))
            loads.append(load)
    lists[1].wait()
    for j in range(per_dev):
        table[anc_at + j] = anc_ref[me * per_dev + j]
        table[new_at + j] = len_ref[anc_ref[me * per_dev + j]] + 2
        table[own_at + j] = len_ref[me * per_dev + j]
        table[slot_at + j] = -PICKS
    for k, pairing in enumerate(ROUNDS):
        source = partner(me, doms, *pairing)
        low, _ = named_range(anc_ref, me * per_dev, source, per_dev)
        for j in range(per_dev):
            local = anc_ref[me * per_dev + j] - source * per_dev
            named = jnp.logical_and(local >= 0, local < per_dev)
            slot = k * PICKS + jnp.where(local == low, 0, PICKS - 1)
            table[slot_at + j] = jnp.where(named, slot, table[slot_at + j])
    table_copy = pltpu.make_async_copy(table, table_hbm, list_sem.at[3])
    table_copy.start()
    lists[2].wait()
    new_rows[...] = new_bf16[...].astype(jnp.float32).reshape(new_rows.shape)
    for load, (pick, target) in zip(loads, picks):
        load.wait()
        place_new_rows(target, new_rows, len_ref[me * per_dev + pick], pick, per_dev)
    table_copy.wait()


def pack(lengths, ancestors, new_kv, gen_cache, doms):
    per_dev, rows, width = gen_cache.shape
    count = len(ROUNDS)
    vmem = pl.BlockSpec(memory_space=pltpu.VMEM)
    hbm = pl.BlockSpec(memory_space=pltpu.HBM)
    block_bytes = PICKS * rows * width * 2
    return pl.pallas_call(
        functools.partial(pack_kernel, per_dev, doms),
        out_shape=[jax.ShapeDtypeStruct((PICKS, rows, width), jnp.bfloat16)] * count
        + [jax.ShapeDtypeStruct((TABLE_PARTS * per_dev,), jnp.int32)],
        in_specs=[hbm] * 4,
        out_specs=[vmem] * count + [hbm],
        scratch_shapes=[
            pltpu.SMEM((TABLE_PARTS * per_dev,), jnp.int32),
            pltpu.SMEM(lengths.shape, jnp.int32),
            pltpu.SMEM(ancestors.shape, jnp.int32),
            pltpu.VMEM(new_kv.shape, jnp.bfloat16),
            pltpu.VMEM((2 * per_dev, width), jnp.float32),
            pltpu.SemaphoreType.DMA((4,)),
            pltpu.SemaphoreType.DMA((count * PICKS,)),
        ],
        compiler_params=pltpu.CompilerParams(vmem_limit_bytes=VMEM_BYTES),
        cost_estimate=pl.CostEstimate(
            flops=0, bytes_accessed=2 * count * block_bytes, transcendentals=0
        ),
        name="pack_sends",
    )(*(in_hbm(x) for x in (lengths, ancestors, new_kv, gen_cache)))


def fold_lanes(block, combine, start):
    for first in range(0, block.shape[1], HEAD_DIM):
        start = combine(start, block[:, first : first + HEAD_DIM])
    return start


def attend_kernel(
    per_dev,
    group,
    kv_local,
    chunk,
    table_hbm,
    q_ref,
    prompt_hbm,
    gen_hbm,
    token_hbm,
    bias_hbm,
    new_ref,
    head_ref,
    prior_ref,
    share_ref,
    out_hbm,
    prompt,
    grown,
    new_rows,
    scores,
    tops,
    totals,
    mixed_ref,
    bias_rows,
    extra,
    table,
    token_ref,
    prompt_sem,
    gen_sem,
    out_sem,
    bias_sem,
    list_sem,
):
    me = lax.axis_index("dom")
    steps = q_ref.shape[0]
    rows, width = grown.shape[1:]
    chunks = prompt.shape[0] // chunk
    pair = 2 * HEAD_DIM
    scale = LOG2_E / math.sqrt(HEAD_DIM)
    base = steps * per_dev

    half = per_dev // 2
    per_chunk = per_dev // chunks

    def gen_load(p):
        return pltpu.make_async_copy(gen_hbm.at[p], grown.at[p], gen_sem.at[p])

    def prompt_load(j):
        part = pl.ds(pl.multiple_of(j * chunk, chunk), chunk)
        return pltpu.make_async_copy(prompt_hbm.at[part], prompt.at[part], prompt_sem.at[j])

    lists = [
        pltpu.make_async_copy(table_hbm, table, list_sem.at[0]),
        pltpu.make_async_copy(token_hbm, token_ref, list_sem.at[1]),
    ]
    for copy in lists:
        copy.start()
    def start_loads(j):
        prompt_load(j).start()
        for i in range(per_chunk):
            gen_load(j * per_chunk + i).start()

    for j in range(AHEAD):
        start_loads(j)

    for copy in lists:
        copy.wait()
    len_ref, anc_ref = (table.at[pl.ds(k * per_dev, per_dev)] for k in (1, 2))
    for i in range(base):
        row = token_ref[i // per_dev, i % per_dev] // HEAD_DIM
        pltpu.make_async_copy(bias_hbm.at[pl.ds(pl.multiple_of(row * HEAD_DIM, HEAD_DIM), HEAD_DIM)], bias_rows.at[i, 0], bias_sem.at[i]).start()

    new_rows[...] = new_ref[...].astype(jnp.float32).reshape(base, width)
    row_ids = lax.broadcasted_iota(jnp.int32, (rows, width), 0)

    def patch(p):
        gen_load(p).wait()
        behind = row_ids - len_ref[p]
        tail = jnp.where(behind == 1, new_rows[pl.ds(per_dev + p, 1), :], 0.0)
        tail = jnp.where(behind == 0, new_rows[pl.ds(p, 1), :], tail)
        grown[p] = jnp.where(behind < 0, grown[p].astype(jnp.float32), tail).astype(
            jnp.bfloat16
        )

    q2 = q_ref[...].reshape(base, q_ref.shape[-1])
    queries = [
        jnp.concatenate(
            [q2[:, h * HEAD_DIM : (h + 1) * HEAD_DIM] for h in range(c * group, (c + 1) * group)],
            axis=0,
        )
        for c in range(kv_local)
    ]

    def score(query_rows, keys):
        return lax.dot_general(
            query_rows, keys, (((1,), (1,)), ((), ())), preferred_element_type=jnp.float32
        )

    def mix(probs, values):
        return jnp.dot(probs, values, preferred_element_type=jnp.float32)

    tops[...] = jnp.full(tops.shape, NEG_FILL, jnp.float32)

    def score_chunk(j, carry):
        prompt_load(j).wait()
        pl.when(j + AHEAD < chunks)(functools.partial(start_loads, j + AHEAD))
        part = pl.ds(pl.multiple_of(j * chunk, chunk), chunk)
        for c in range(kv_local):
            block = score(queries[c], prompt[part, c * pair : c * pair + HEAD_DIM])
            scores[c, j] = block
            tops[c] = fold_lanes(block, jnp.maximum, tops[c])
        for i in range(per_chunk):
            patch(j * per_chunk + i)
        return carry

    lax.fori_loop(0, chunks, score_chunk, 0)

    homes = []
    for p in range(per_dev):
        local = anc_ref[p] - me * per_dev
        home = jnp.logical_and(local >= 0, local < per_dev)
        source = grown.at[jnp.clip(local, 0, per_dev - 1)]
        copy = pltpu.make_async_copy(source, out_hbm.at[p], out_sem.at[p])
        homes.append((home, copy))
        pl.when(home)(copy.start)

    row_ids = lax.broadcasted_iota(jnp.int32, (base, rows), 0)
    owner = row_ids % per_dev
    last = row_ids // per_dev
    for p in range(per_dev):
        last = last + jnp.where(owner == p, len_ref[p], 0)
    visible = lax.broadcasted_iota(jnp.int32, (base, rows), 1) <= last
    visible, lower, seat = (
        jnp.concatenate([part.astype(jnp.int32)] * group, axis=0)
        for part in (visible, owner < half, owner % half)
    )
    visible, lower = visible == 1, lower == 1

    def halves(block):
        block = block.astype(jnp.float32)
        parts = [jnp.where(lower, block, 0.0), jnp.where(lower, 0.0, block)]
        return jnp.concatenate(parts, axis=1).astype(jnp.bfloat16)

    def by_seat(blocks):
        chosen = blocks[:, :HEAD_DIM]
        for i in range(1, half):
            chosen = jnp.where(seat == i, blocks[:, i * HEAD_DIM : (i + 1) * HEAD_DIM], chosen)
        return chosen

    for c in range(kv_local):
        columns = slice(c * pair, c * pair + HEAD_DIM)
        keys = jnp.concatenate(
            [
                jnp.concatenate([grown[i, :, columns], grown[i + half, :, columns]], axis=1)
                for i in range(half)
            ],
            axis=0,
        )
        own = jnp.where(visible, by_seat(score(halves(queries[c]), keys)), NEG_FILL)
        top = jnp.max(jnp.maximum(tops[c], own), axis=1, keepdims=True)
        top = jnp.broadcast_to(top, own.shape)
        tops[c] = top
        exps = jnp.where(visible, jnp.exp2((own - top) * scale), 0.0)
        totals[c] = exps
        columns = slice(c * pair + HEAD_DIM, (c + 1) * pair)
        values = jnp.concatenate(
            [
                jnp.concatenate([grown[i, :, columns], grown[i + half, :, columns]], axis=0)
                for i in range(half)
            ],
            axis=1,
        )
        mixed_ref[c] = by_seat(mix(halves(exps), values))

    def mix_chunks(step, carry):
        for c in range(kv_local):
            top = jnp.concatenate([tops[c]] * (chunk // HEAD_DIM), axis=1)
            total, mixed = totals[c], mixed_ref[c]
            for i in range(AHEAD):
                j = step * AHEAD + i
                part = pl.ds(pl.multiple_of(j * chunk, chunk), chunk)
                exps = jnp.exp2((scores[c, j] - top) * scale)
                total = fold_lanes(exps, jnp.add, total)
                mixed = mixed + mix(
                    exps.astype(jnp.bfloat16), prompt[part, c * pair + HEAD_DIM : (c + 1) * pair]
                )
            totals[c] = total
            mixed_ref[c] = mixed
        return carry

    lax.fori_loop(0, chunks // AHEAD, mix_chunks, 0)
    weighted = jnp.zeros((base, HEAD_DIM), jnp.float32)
    for c in range(kv_local):
        mixed = mixed_ref[c] / jnp.sum(totals[c], axis=1, keepdims=True)
        for h in range(group):
            weighted = (
                weighted + mixed[h * base : (h + 1) * base] * head_ref[c * group + h][None, :]
            )
    row_ids = lax.broadcasted_iota(jnp.int32, (base, HEAD_DIM), 0)
    column = jnp.full((base, HEAD_DIM), -1, jnp.int32)
    for i in range(base):
        pltpu.make_async_copy(bias_hbm.at[pl.ds(0, HEAD_DIM)], bias_rows.at[i, 0], bias_sem.at[i]).wait()
        column = jnp.where(row_ids == i, token_ref[i // per_dev, i % per_dev] % HEAD_DIM, column)
    adds = lax.axis_index("tp") == 0
    lane_ids = lax.broadcasted_iota(jnp.int32, (base, HEAD_DIM), 1)
    bias = jnp.where(lane_ids == column, bias_rows[...].reshape(base, HEAD_DIM), 0.0)
    weighted = weighted + jnp.where(adds, bias, 0.0)
    extra[...] = jnp.zeros(extra.shape, jnp.float32)
    extra[:, base : base + per_dev] = jnp.where(adds, prior_ref[...], 0.0)
    padding = jnp.zeros((HEAD_DIM - base, HEAD_DIM), jnp.float32)
    square = jnp.concatenate([weighted, padding], axis=0)
    row = jnp.sum(square.T, axis=0, keepdims=True) + extra[...]
    share_ref[...] = jnp.broadcast_to(row[None], share_ref.shape)
    for home, copy in homes:
        pl.when(home)(copy.wait)


def attend(
    table,
    queries,
    prompt_kv,
    gen_cache,
    tokens,
    twist_bias,
    new_kv,
    twist_vector,
    prior_weights,
    devices,
):
    steps, per_dev, width = queries.shape
    keys, kv_width = prompt_kv.shape
    rows = gen_cache.shape[1]
    kv_local = kv_width // (2 * HEAD_DIM)
    group = width // (kv_local * HEAD_DIM)
    score_rows = steps * per_dev * group
    chunk = min(KEY_CHUNK, keys)
    head_weights = twist_vector.reshape(kv_local * group, HEAD_DIM)
    vmem = pl.BlockSpec(memory_space=pltpu.VMEM)
    hbm = pl.BlockSpec(memory_space=pltpu.HBM)
    score_count = score_rows * kv_local * (keys + rows)
    return pl.pallas_call(
        functools.partial(attend_kernel, per_dev, group, kv_local, chunk),
        out_shape=[
            jax.ShapeDtypeStruct((devices, 1, HEAD_DIM), jnp.float32),
            jax.ShapeDtypeStruct(gen_cache.shape, jnp.bfloat16),
        ],
        in_specs=[hbm, vmem, hbm, hbm, hbm, hbm, vmem, vmem, vmem],
        out_specs=[vmem, hbm],
        scratch_shapes=[
            pltpu.VMEM(prompt_kv.shape, jnp.bfloat16),
            pltpu.VMEM(gen_cache.shape, jnp.bfloat16),
            pltpu.VMEM((steps * per_dev, kv_width), jnp.float32),
            pltpu.VMEM((kv_local, keys // chunk, score_rows, chunk), jnp.float32),
            pltpu.VMEM((kv_local, score_rows, HEAD_DIM), jnp.float32),
            pltpu.VMEM((kv_local, score_rows, HEAD_DIM), jnp.float32),
            pltpu.VMEM((kv_local, score_rows, HEAD_DIM), jnp.float32),
            pltpu.VMEM((steps * per_dev, 1, HEAD_DIM), jnp.float32),
            pltpu.VMEM((1, HEAD_DIM), jnp.float32),
            pltpu.SMEM(table.shape, jnp.int32),
            pltpu.SMEM(tokens.shape, jnp.int32),
            pltpu.SemaphoreType.DMA((keys // chunk,)),
            pltpu.SemaphoreType.DMA((per_dev,)),
            pltpu.SemaphoreType.DMA((per_dev,)),
            pltpu.SemaphoreType.DMA((steps * per_dev,)),
            pltpu.SemaphoreType.DMA((2,)),
        ],
        compiler_params=pltpu.CompilerParams(vmem_limit_bytes=VMEM_BYTES),
        cost_estimate=pl.CostEstimate(
            flops=4 * score_count * HEAD_DIM,
            bytes_accessed=2 * (prompt_kv.size + 2 * gen_cache.size),
            transcendentals=score_count,
        ),
        name="attend",
    )(
        in_hbm(table),
        queries,
        in_hbm(prompt_kv),
        in_hbm(gen_cache),
        in_hbm(tokens),
        in_hbm(twist_bias),
        new_kv,
        head_weights,
        prior_weights[None],
    )


def finish_kernel(doms, tps, table_ref, *refs):
    gots = refs[: len(ROUNDS)]
    _, all_ref, out_ref, twist_hbm, normal_hbm = refs[len(gots) : len(gots) + 5]
    table, sums, twist, normal, copy_sem, small_sem = refs[len(gots) + 5 :]
    per_dev = out_ref.shape[0]
    table_copy = pltpu.make_async_copy(table_ref, table, small_sem.at[0])
    table_copy.start()
    table_copy.wait()
    slots = [table[(TABLE_PARTS - 1) * per_dev + p] for p in range(per_dev)]
    for p, slot in enumerate(slots):
        for k, got in enumerate(gots):
            copy = pltpu.make_async_copy(got.at[slot % PICKS], out_ref.at[p], copy_sem.at[p])
            pl.when(slot // PICKS == k)(copy.start)
    for d in range(doms):
        row = all_ref[d * tps]
        for t in range(1, tps):
            row = row + all_ref[d * tps + t]
        sums[d : d + 1, :] = row
    step_0, step_1, prior = (
        slice(k * per_dev, (k + 1) * per_dev) for k in range(3)
    )
    totals = sums[...]
    log_weights = totals[:, prior] + totals[:, step_1] - totals[:, step_0]
    largest = jnp.max(log_weights, keepdims=True)
    log_total = largest + jnp.log(jnp.sum(jnp.exp(log_weights - largest), keepdims=True))
    mine = sums[pl.ds(lax.axis_index("dom"), 1), :]
    own = mine[:, prior] + mine[:, step_1] - mine[:, step_0]
    twist[...] = jnp.concatenate([mine[:, step_0], mine[:, step_1]], axis=0)
    normal[...] = own - log_total
    results = [
        pltpu.make_async_copy(twist, twist_hbm, small_sem.at[1]),
        pltpu.make_async_copy(normal, normal_hbm, small_sem.at[2]),
    ]
    for copy in results:
        copy.start()
    for p, slot in enumerate(slots):
        copy = pltpu.make_async_copy(gots[0].at[0], out_ref.at[p], copy_sem.at[p])
        pl.when(slot >= 0)(copy.wait)
    for copy in results:
        copy.wait()


def finish(table, gots, held, shares, doms, tps):
    per_dev = held.shape[0]
    count = len(gots)
    vmem = pl.BlockSpec(memory_space=pltpu.VMEM)
    hbm = pl.BlockSpec(memory_space=pl.ANY)
    return pl.pallas_call(
        functools.partial(finish_kernel, doms, tps),
        out_shape=[
            jax.ShapeDtypeStruct(held.shape, held.dtype),
            jax.ShapeDtypeStruct((2, per_dev), jnp.float32),
            jax.ShapeDtypeStruct((1, per_dev), jnp.float32),
        ],
        in_specs=[vmem] + [vmem] * count + [hbm, vmem],
        out_specs=[hbm, hbm, hbm],
        input_output_aliases={1 + count: 0},
        scratch_shapes=[
            pltpu.SMEM(table.shape, jnp.int32),
            pltpu.VMEM((doms, HEAD_DIM), jnp.float32),
            pltpu.VMEM((2, per_dev), jnp.float32),
            pltpu.VMEM((1, per_dev), jnp.float32),
            pltpu.SemaphoreType.DMA((per_dev,)),
            pltpu.SemaphoreType.DMA((3,)),
        ],
        compiler_params=pltpu.CompilerParams(vmem_limit_bytes=VMEM_BYTES),
        cost_estimate=pl.CostEstimate(
            flops=0, bytes_accessed=held.size, transcendentals=0
        ),
        name="finish",
    )(table, *gots, held, shares)


def local(
    queries,
    new_kv,
    gen_cache,
    prompt_kv,
    lengths,
    ancestors,
    tokens,
    twist_vector,
    twist_bias,
    prior_weights,
):
    doms, tps = lax.axis_size("dom"), lax.axis_size("tp")
    per_dev = gen_cache.shape[0]
    everyone = ("dom", "tp")

    *sends, table = pack(lengths, ancestors, new_kv, gen_cache, doms)
    arrivals = [
        lax.ppermute(send, everyone, swaps(doms, tps, *pairing))
        for send, pairing in zip(sends, ROUNDS)
    ]

    shares, resampled = attend(
        table,
        queries,
        prompt_kv,
        gen_cache,
        tokens,
        twist_bias,
        new_kv,
        twist_vector,
        prior_weights,
        doms * tps,
    )
    shares = lax.all_to_all(shares, everyone, 0, 0, tiled=True)
    resampled, twist, normalized = finish(table, arrivals, resampled, shares, doms, tps)
    return (twist, normalized.reshape(per_dev), resampled, table[:per_dev])


def solution(mesh):
    in_specs = (
        P(None, "dom", "tp"),
        P(None, "dom", "tp"),
        P("dom", None, "tp"),
        P(None, "tp"),
        P(),
        P(),
        P(None, "dom"),
        P("tp"),
        P(),
        P("dom"),
    )
    out_specs = (P(None, "dom"), P("dom"), P("dom", None, "tp"), P("dom"))
    return jax.shard_map(local, mesh=mesh, in_specs=in_specs, out_specs=out_specs, check_vma=False)
```

```python
import functools
import math

import jax
import jax.numpy as jnp
from jax import lax
from jax.experimental import pallas as pl
from jax.experimental.pallas import tpu as pltpu
from jax.sharding import PartitionSpec as P

HEAD_DIM = 128
SPAN = 2
PICKS = 2
TABLE_PARTS = 4
AHEAD = 2
NEG_FILL = -1e30
LOG2_E = math.log2(math.e)
KEY_CHUNK = 512
VMEM_BYTES = 44 * 1024 * 1024
ROW_TILE = 16
WINDOW = 2 * ROW_TILE

ROUNDS = ((2, 0), (2, 2), (1, 1), (1, 0))


def is_first(device, distance, offset):
    return (device + distance * 2 - offset) % (2 * distance) < distance


def pairs(doms, distance, offset):
    return [
        [d, (d + distance) % doms] for d in range(doms) if is_first(d, distance, offset)
    ]


def swaps(doms, tps, distance, offset):
    routes = []
    for first, second in pairs(doms, distance, offset):
        if second - first == distance:
            for t in range(tps):
                ends = (first * tps + t, second * tps + t)
                routes += [ends, ends[::-1]]
    return routes


def partner(me, doms, distance, offset):
    step = jnp.where(is_first(me, distance, offset), distance, doms - distance)
    return (me + step) % doms


def in_hbm(x):
    return pltpu.with_memory_space_constraint(x, pltpu.HBM)


def place_new_rows(cache, new_rows, length, slot, per_dev):
    rows, width = cache.shape
    first = pl.multiple_of(
        jnp.minimum(length // ROW_TILE * ROW_TILE, rows - WINDOW), ROW_TILE
    )
    row_ids = first + lax.broadcasted_iota(jnp.int32, (WINDOW, width), 0)
    old = cache[pl.ds(first, WINDOW), :].astype(jnp.float32)
    later = jnp.where(row_ids == length + 1, new_rows[pl.ds(per_dev + slot, 1), :], 0.0)
    later = jnp.where(row_ids == length, new_rows[pl.ds(slot, 1), :], later)
    cache[pl.ds(first, WINDOW), :] = jnp.where(row_ids < length, old, later).astype(
        jnp.bfloat16
    )

    def clear(tile, carry):
        start = pl.multiple_of(tile * ROW_TILE, ROW_TILE)
        cache[pl.ds(start, ROW_TILE), :] = jnp.zeros((ROW_TILE, width), jnp.bfloat16)
        return carry

    lax.fori_loop(first // ROW_TILE + WINDOW // ROW_TILE, rows // ROW_TILE, clear, 0)


def named_range(anc_ref, first, owner, per_dev):
    low, high = jnp.int32(per_dev), jnp.int32(-1)
    for j in range(per_dev):
        local = anc_ref[first + j] - owner * per_dev
        named = jnp.logical_and(local >= 0, local < per_dev)
        low = jnp.minimum(low, jnp.where(named, local, per_dev))
        high = jnp.maximum(high, jnp.where(named, local, -1))
    return low, high


def pack_kernel(per_dev, doms, len_hbm, anc_hbm, new_hbm, gen_hbm, *refs):
    sends = refs[: len(ROUNDS)]
    table_hbm, table, len_ref, anc_ref, new_bf16, new_rows, list_sem, load_sem = refs[
        len(ROUNDS) :
    ]
    new_at, own_at, anc_at, slot_at = (k * per_dev for k in range(TABLE_PARTS))
    lists = [
        pltpu.make_async_copy(anc_hbm, anc_ref, list_sem.at[0]),
        pltpu.make_async_copy(len_hbm, len_ref, list_sem.at[1]),
        pltpu.make_async_copy(new_hbm, new_bf16, list_sem.at[2]),
    ]
    for copy in lists:
        copy.start()
    me = lax.axis_index("dom")
    lists[0].wait()
    picks = []
    loads = []
    for k, pairing in enumerate(ROUNDS):
        reader = partner(me, doms, *pairing)
        low, high = named_range(anc_ref, reader * per_dev, me, per_dev)
        for i, pick in enumerate((jnp.minimum(low, per_dev - 1), jnp.maximum(high, 0))):
            target = sends[k].at[i]
            load = pltpu.make_async_copy(gen_hbm.at[pick], target, load_sem.at[len(loads)])
            load.start()
            picks.append((pick, target))
            loads.append(load)
    lists[1].wait()
    for j in range(per_dev):
        table[anc_at + j] = anc_ref[me * per_dev + j]
        table[new_at + j] = len_ref[anc_ref[me * per_dev + j]] + 2
        table[own_at + j] = len_ref[me * per_dev + j]
        table[slot_at + j] = -PICKS
    for k, pairing in enumerate(ROUNDS):
        source = partner(me, doms, *pairing)
        low, _ = named_range(anc_ref, me * per_dev, source, per_dev)
        for j in range(per_dev):
            local = anc_ref[me * per_dev + j] - source * per_dev
            named = jnp.logical_and(local >= 0, local < per_dev)
            slot = k * PICKS + jnp.where(local == low, 0, PICKS - 1)
            table[slot_at + j] = jnp.where(named, slot, table[slot_at + j])
    table_copy = pltpu.make_async_copy(table, table_hbm, list_sem.at[3])
    table_copy.start()
    lists[2].wait()
    new_rows[...] = new_bf16[...].astype(jnp.float32).reshape(new_rows.shape)
    for load, (pick, target) in zip(loads, picks):
        load.wait()
        place_new_rows(target, new_rows, len_ref[me * per_dev + pick], pick, per_dev)
    table_copy.wait()


def pack(lengths, ancestors, new_kv, gen_cache, doms):
    per_dev, rows, width = gen_cache.shape
    count = len(ROUNDS)
    vmem = pl.BlockSpec(memory_space=pltpu.VMEM)
    hbm = pl.BlockSpec(memory_space=pltpu.HBM)
    block_bytes = PICKS * rows * width * 2
    return pl.pallas_call(
        functools.partial(pack_kernel, per_dev, doms),
        out_shape=[jax.ShapeDtypeStruct((PICKS, rows, width), jnp.bfloat16)] * count
        + [jax.ShapeDtypeStruct((TABLE_PARTS * per_dev,), jnp.int32)],
        in_specs=[hbm] * 4,
        out_specs=[vmem] * count + [hbm],
        scratch_shapes=[
            pltpu.SMEM((TABLE_PARTS * per_dev,), jnp.int32),
            pltpu.SMEM(lengths.shape, jnp.int32),
            pltpu.SMEM(ancestors.shape, jnp.int32),
            pltpu.VMEM(new_kv.shape, jnp.bfloat16),
            pltpu.VMEM((2 * per_dev, width), jnp.float32),
            pltpu.SemaphoreType.DMA((4,)),
            pltpu.SemaphoreType.DMA((count * PICKS,)),
        ],
        compiler_params=pltpu.CompilerParams(vmem_limit_bytes=VMEM_BYTES),
        cost_estimate=pl.CostEstimate(
            flops=0, bytes_accessed=2 * count * block_bytes, transcendentals=0
        ),
        name="pack_sends",
    )(*(in_hbm(x) for x in (lengths, ancestors, new_kv, gen_cache)))


def fold_lanes(block, combine, start):
    for first in range(0, block.shape[1], HEAD_DIM):
        start = combine(start, block[:, first : first + HEAD_DIM])
    return start


def attend_kernel(
    per_dev,
    group,
    kv_local,
    chunk,
    table_hbm,
    q_ref,
    prompt_hbm,
    gen_hbm,
    token_hbm,
    bias_hbm,
    new_ref,
    head_ref,
    prior_ref,
    share_ref,
    out_hbm,
    prompt,
    grown,
    new_rows,
    scores,
    tops,
    totals,
    mixed_ref,
    bias_rows,
    extra,
    table,
    token_ref,
    prompt_sem,
    gen_sem,
    out_sem,
    bias_sem,
    list_sem,
):
    me = lax.axis_index("dom")
    steps = q_ref.shape[0]
    rows, width = grown.shape[1:]
    chunks = prompt.shape[0] // chunk
    pair = 2 * HEAD_DIM
    scale = LOG2_E / math.sqrt(HEAD_DIM)
    base = steps * per_dev

    half = per_dev // 2
    per_chunk = per_dev // chunks

    def gen_load(p):
        return pltpu.make_async_copy(gen_hbm.at[p], grown.at[p], gen_sem.at[p])

    def prompt_load(j):
        part = pl.ds(pl.multiple_of(j * chunk, chunk), chunk)
        return pltpu.make_async_copy(prompt_hbm.at[part], prompt.at[part], prompt_sem.at[j])

    lists = [
        pltpu.make_async_copy(table_hbm, table, list_sem.at[0]),
        pltpu.make_async_copy(token_hbm, token_ref, list_sem.at[1]),
    ]
    for copy in lists:
        copy.start()
    def start_loads(j):
        prompt_load(j).start()
        for i in range(per_chunk):
            gen_load(j * per_chunk + i).start()

    for j in range(AHEAD):
        start_loads(j)

    for copy in lists:
        copy.wait()
    len_ref, anc_ref = (table.at[pl.ds(k * per_dev, per_dev)] for k in (1, 2))
    for i in range(base):
        row = token_ref[i // per_dev, i % per_dev] // HEAD_DIM
        pltpu.make_async_copy(bias_hbm.at[pl.ds(pl.multiple_of(row * HEAD_DIM, HEAD_DIM), HEAD_DIM)], bias_rows.at[i, 0], bias_sem.at[i]).start()

    new_rows[...] = new_ref[...].astype(jnp.float32).reshape(base, width)
    row_ids = lax.broadcasted_iota(jnp.int32, (rows, width), 0)

    def patch(p):
        gen_load(p).wait()
        behind = row_ids - len_ref[p]
        tail = jnp.where(behind == 1, new_rows[pl.ds(per_dev + p, 1), :], 0.0)
        tail = jnp.where(behind == 0, new_rows[pl.ds(p, 1), :], tail)
        grown[p] = jnp.where(behind < 0, grown[p].astype(jnp.float32), tail).astype(
            jnp.bfloat16
        )

    q2 = q_ref[...].reshape(base, q_ref.shape[-1])
    queries = [
        jnp.concatenate(
            [q2[:, h * HEAD_DIM : (h + 1) * HEAD_DIM] for h in range(c * group, (c + 1) * group)],
            axis=0,
        )
        for c in range(kv_local)
    ]

    def score(query_rows, keys):
        return lax.dot_general(
            query_rows, keys, (((1,), (1,)), ((), ())), preferred_element_type=jnp.float32
        )

    def mix(probs, values):
        return jnp.dot(probs, values, preferred_element_type=jnp.float32)

    tops[...] = jnp.full(tops.shape, NEG_FILL, jnp.float32)

    def score_chunk(j, carry):
        prompt_load(j).wait()
        pl.when(j + AHEAD < chunks)(functools.partial(start_loads, j + AHEAD))
        part = pl.ds(pl.multiple_of(j * chunk, chunk), chunk)
        for c in range(kv_local):
            block = score(queries[c], prompt[part, c * pair : c * pair + HEAD_DIM])
            scores[c, j] = block
            tops[c] = fold_lanes(block, jnp.maximum, tops[c])
        for i in range(per_chunk):
            patch(j * per_chunk + i)
        return carry

    lax.fori_loop(0, chunks, score_chunk, 0)

    homes = []
    for p in range(per_dev):
        local = anc_ref[p] - me * per_dev
        home = jnp.logical_and(local >= 0, local < per_dev)
        source = grown.at[jnp.clip(local, 0, per_dev - 1)]
        copy = pltpu.make_async_copy(source, out_hbm.at[p], out_sem.at[p])
        homes.append((home, copy))
        pl.when(home)(copy.start)

    row_ids = lax.broadcasted_iota(jnp.int32, (base, rows), 0)
    owner = row_ids % per_dev
    last = row_ids // per_dev
    for p in range(per_dev):
        last = last + jnp.where(owner == p, len_ref[p], 0)
    visible = lax.broadcasted_iota(jnp.int32, (base, rows), 1) <= last
    visible, lower, seat = (
        jnp.concatenate([part.astype(jnp.int32)] * group, axis=0)
        for part in (visible, owner < half, owner % half)
    )
    visible, lower = visible == 1, lower == 1

    def halves(block):
        block = block.astype(jnp.float32)
        parts = [jnp.where(lower, block, 0.0), jnp.where(lower, 0.0, block)]
        return jnp.concatenate(parts, axis=1).astype(jnp.bfloat16)

    def by_seat(blocks):
        chosen = blocks[:, :HEAD_DIM]
        for i in range(1, half):
            chosen = jnp.where(seat == i, blocks[:, i * HEAD_DIM : (i + 1) * HEAD_DIM], chosen)
        return chosen

    for c in range(kv_local):
        columns = slice(c * pair, c * pair + HEAD_DIM)
        keys = jnp.concatenate(
            [
                jnp.concatenate([grown[i, :, columns], grown[i + half, :, columns]], axis=1)
                for i in range(half)
            ],
            axis=0,
        )
        own = jnp.where(visible, by_seat(score(halves(queries[c]), keys)), NEG_FILL)
        top = jnp.max(jnp.maximum(tops[c], own), axis=1, keepdims=True)
        top = jnp.broadcast_to(top, own.shape)
        tops[c] = top
        exps = jnp.where(visible, jnp.exp2((own - top) * scale), 0.0)
        totals[c] = exps
        columns = slice(c * pair + HEAD_DIM, (c + 1) * pair)
        values = jnp.concatenate(
            [
                jnp.concatenate([grown[i, :, columns], grown[i + half, :, columns]], axis=0)
                for i in range(half)
            ],
            axis=1,
        )
        mixed_ref[c] = by_seat(mix(halves(exps), values))

    def mix_chunks(step, carry):
        for c in range(kv_local):
            top = jnp.concatenate([tops[c]] * (chunk // HEAD_DIM), axis=1)
            total, mixed = totals[c], mixed_ref[c]
            for i in range(AHEAD):
                j = step * AHEAD + i
                part = pl.ds(pl.multiple_of(j * chunk, chunk), chunk)
                exps = jnp.exp2((scores[c, j] - top) * scale)
                total = fold_lanes(exps, jnp.add, total)
                mixed = mixed + mix(
                    exps.astype(jnp.bfloat16), prompt[part, c * pair + HEAD_DIM : (c + 1) * pair]
                )
            totals[c] = total
            mixed_ref[c] = mixed
        return carry

    lax.fori_loop(0, chunks // AHEAD, mix_chunks, 0)
    weighted = jnp.zeros((base, HEAD_DIM), jnp.float32)
    for c in range(kv_local):
        mixed = mixed_ref[c] / jnp.sum(totals[c], axis=1, keepdims=True)
        for h in range(group):
            weighted = (
                weighted + mixed[h * base : (h + 1) * base] * head_ref[c * group + h][None, :]
            )
    row_ids = lax.broadcasted_iota(jnp.int32, (base, HEAD_DIM), 0)
    column = jnp.full((base, HEAD_DIM), -1, jnp.int32)
    for i in range(base):
        pltpu.make_async_copy(bias_hbm.at[pl.ds(0, HEAD_DIM)], bias_rows.at[i, 0], bias_sem.at[i]).wait()
        column = jnp.where(row_ids == i, token_ref[i // per_dev, i % per_dev] % HEAD_DIM, column)
    adds = lax.axis_index("tp") == 0
    lane_ids = lax.broadcasted_iota(jnp.int32, (base, HEAD_DIM), 1)
    bias = jnp.where(lane_ids == column, bias_rows[...].reshape(base, HEAD_DIM), 0.0)
    weighted = weighted + jnp.where(adds, bias, 0.0)
    extra[...] = jnp.zeros(extra.shape, jnp.float32)
    extra[:, base : base + per_dev] = jnp.where(adds, prior_ref[...], 0.0)
    padding = jnp.zeros((HEAD_DIM - base, HEAD_DIM), jnp.float32)
    square = jnp.concatenate([weighted, padding], axis=0)
    row = jnp.sum(square.T, axis=0, keepdims=True) + extra[...]
    share_ref[...] = jnp.broadcast_to(row[None], share_ref.shape)
    for home, copy in homes:
        pl.when(home)(copy.wait)


def attend(
    table,
    queries,
    prompt_kv,
    gen_cache,
    tokens,
    twist_bias,
    new_kv,
    twist_vector,
    prior_weights,
    devices,
):
    steps, per_dev, width = queries.shape
    keys, kv_width = prompt_kv.shape
    rows = gen_cache.shape[1]
    kv_local = kv_width // (2 * HEAD_DIM)
    group = width // (kv_local * HEAD_DIM)
    score_rows = steps * per_dev * group
    chunk = min(KEY_CHUNK, keys)
    head_weights = twist_vector.reshape(kv_local * group, HEAD_DIM)
    vmem = pl.BlockSpec(memory_space=pltpu.VMEM)
    hbm = pl.BlockSpec(memory_space=pltpu.HBM)
    score_count = score_rows * kv_local * (keys + rows)
    return pl.pallas_call(
        functools.partial(attend_kernel, per_dev, group, kv_local, chunk),
        out_shape=[
            jax.ShapeDtypeStruct((devices, 1, HEAD_DIM), jnp.float32),
            jax.ShapeDtypeStruct(gen_cache.shape, jnp.bfloat16),
        ],
        in_specs=[hbm, vmem, hbm, hbm, hbm, hbm, vmem, vmem, vmem],
        out_specs=[vmem, hbm],
        scratch_shapes=[
            pltpu.VMEM(prompt_kv.shape, jnp.bfloat16),
            pltpu.VMEM(gen_cache.shape, jnp.bfloat16),
            pltpu.VMEM((steps * per_dev, kv_width), jnp.float32),
            pltpu.VMEM((kv_local, keys // chunk, score_rows, chunk), jnp.float32),
            pltpu.VMEM((kv_local, score_rows, HEAD_DIM), jnp.float32),
            pltpu.VMEM((kv_local, score_rows, HEAD_DIM), jnp.float32),
            pltpu.VMEM((kv_local, score_rows, HEAD_DIM), jnp.float32),
            pltpu.VMEM((steps * per_dev, 1, HEAD_DIM), jnp.float32),
            pltpu.VMEM((1, HEAD_DIM), jnp.float32),
            pltpu.SMEM(table.shape, jnp.int32),
            pltpu.SMEM(tokens.shape, jnp.int32),
            pltpu.SemaphoreType.DMA((keys // chunk,)),
            pltpu.SemaphoreType.DMA((per_dev,)),
            pltpu.SemaphoreType.DMA((per_dev,)),
            pltpu.SemaphoreType.DMA((steps * per_dev,)),
            pltpu.SemaphoreType.DMA((2,)),
        ],
        compiler_params=pltpu.CompilerParams(vmem_limit_bytes=VMEM_BYTES),
        cost_estimate=pl.CostEstimate(
            flops=4 * score_count * HEAD_DIM,
            bytes_accessed=2 * (prompt_kv.size + 2 * gen_cache.size),
            transcendentals=score_count,
        ),
        name="attend",
    )(
        in_hbm(table),
        queries,
        in_hbm(prompt_kv),
        in_hbm(gen_cache),
        in_hbm(tokens),
        in_hbm(twist_bias),
        new_kv,
        head_weights,
        prior_weights[None],
    )


def finish_kernel(doms, tps, table_ref, *refs):
    gots = refs[: len(ROUNDS)]
    _, all_ref, out_ref, twist_hbm, normal_hbm = refs[len(gots) : len(gots) + 5]
    table, sums, twist, normal, copy_sem, small_sem = refs[len(gots) + 5 :]
    per_dev = out_ref.shape[0]
    table_copy = pltpu.make_async_copy(table_ref, table, small_sem.at[0])
    table_copy.start()
    table_copy.wait()
    slots = [table[(TABLE_PARTS - 1) * per_dev + p] for p in range(per_dev)]
    for p, slot in enumerate(slots):
        for k, got in enumerate(gots):
            copy = pltpu.make_async_copy(got.at[slot % PICKS], out_ref.at[p], copy_sem.at[p])
            pl.when(slot // PICKS == k)(copy.start)
    for d in range(doms):
        row = all_ref[d * tps]
        for t in range(1, tps):
            row = row + all_ref[d * tps + t]
        sums[d : d + 1, :] = row
    step_0, step_1, prior = (
        slice(k * per_dev, (k + 1) * per_dev) for k in range(3)
    )
    totals = sums[...]
    log_weights = totals[:, prior] + totals[:, step_1] - totals[:, step_0]
    largest = jnp.max(log_weights, keepdims=True)
    log_total = largest + jnp.log(jnp.sum(jnp.exp(log_weights - largest), keepdims=True))
    mine = sums[pl.ds(lax.axis_index("dom"), 1), :]
    own = mine[:, prior] + mine[:, step_1] - mine[:, step_0]
    twist[...] = jnp.concatenate([mine[:, step_0], mine[:, step_1]], axis=0)
    normal[...] = own - log_total
    results = [
        pltpu.make_async_copy(twist, twist_hbm, small_sem.at[1]),
        pltpu.make_async_copy(normal, normal_hbm, small_sem.at[2]),
    ]
    for copy in results:
        copy.start()
    for p, slot in enumerate(slots):
        copy = pltpu.make_async_copy(gots[0].at[0], out_ref.at[p], copy_sem.at[p])
        pl.when(slot >= 0)(copy.wait)
    for copy in results:
        copy.wait()


def finish(table, gots, held, shares, doms, tps):
    per_dev = held.shape[0]
    count = len(gots)
    vmem = pl.BlockSpec(memory_space=pltpu.VMEM)
    hbm = pl.BlockSpec(memory_space=pl.ANY)
    return pl.pallas_call(
        functools.partial(finish_kernel, doms, tps),
        out_shape=[
            jax.ShapeDtypeStruct(held.shape, held.dtype),
            jax.ShapeDtypeStruct((2, per_dev), jnp.float32),
            jax.ShapeDtypeStruct((1, per_dev), jnp.float32),
        ],
        in_specs=[vmem] + [vmem] * count + [hbm, vmem],
        out_specs=[hbm, hbm, hbm],
        input_output_aliases={1 + count: 0},
        scratch_shapes=[
            pltpu.SMEM(table.shape, jnp.int32),
            pltpu.VMEM((doms, HEAD_DIM), jnp.float32),
            pltpu.VMEM((2, per_dev), jnp.float32),
            pltpu.VMEM((1, per_dev), jnp.float32),
            pltpu.SemaphoreType.DMA((per_dev,)),
            pltpu.SemaphoreType.DMA((3,)),
        ],
        compiler_params=pltpu.CompilerParams(vmem_limit_bytes=VMEM_BYTES),
        cost_estimate=pl.CostEstimate(
            flops=0, bytes_accessed=held.size, transcendentals=0
        ),
        name="finish",
    )(table, *gots, held, shares)


def local(
    queries,
    new_kv,
    gen_cache,
    prompt_kv,
    lengths,
    ancestors,
    tokens,
    twist_vector,
    twist_bias,
    prior_weights,
):
    doms, tps = lax.axis_size("dom"), lax.axis_size("tp")
    per_dev = gen_cache.shape[0]
    everyone = ("dom", "tp")

    *sends, table = pack(lengths, ancestors, new_kv, gen_cache, doms)
    arrivals = [
        lax.ppermute(send, everyone, swaps(doms, tps, *pairing))
        for send, pairing in zip(sends, ROUNDS)
    ]

    shares, resampled = attend(
        table,
        queries,
        prompt_kv,
        gen_cache,
        tokens,
        twist_bias,
        new_kv,
        twist_vector,
        prior_weights,
        doms * tps,
    )
    shares = lax.all_to_all(shares, everyone, 0, 0, tiled=True)
    resampled, twist, normalized = finish(table, arrivals, resampled, shares, doms, tps)
    return (twist, normalized.reshape(per_dev), resampled, table[:per_dev])


def solution(mesh):
    in_specs = (
        P(None, "dom", "tp"),
        P(None, "dom", "tp"),
        P("dom", None, "tp"),
        P(None, "tp"),
        P(),
        P(),
        P(None, "dom"),
        P("tp"),
        P(),
        P("dom"),
    )
    out_specs = (P(None, "dom"), P("dom"), P("dom", None, "tp"), P("dom"))
    return jax.shard_map(local, mesh=mesh, in_specs=in_specs, out_specs=out_specs, check_vma=False)
```

```python
import functools
import math

import jax
import jax.numpy as jnp
from jax import lax
from jax.experimental import pallas as pl
from jax.experimental.pallas import tpu as pltpu
from jax.sharding import PartitionSpec as P

HEAD_DIM = 128
SPAN = 2
PICKS = 2
TABLE_PARTS = 4
AHEAD = 2
NEG_FILL = -1e30
LOG2_E = math.log2(math.e)
KEY_CHUNK = 512
VMEM_BYTES = 44 * 1024 * 1024
ROW_TILE = 16
WINDOW = 2 * ROW_TILE

ROUNDS = ((2, 0), (1, 0), (2, 2), (1, 1))


def is_first(device, distance, offset):
    return (device + distance * 2 - offset) % (2 * distance) < distance


def pairs(doms, distance, offset):
    return [
        [d, (d + distance) % doms] for d in range(doms) if is_first(d, distance, offset)
    ]


def swaps(doms, tps, distance, offset):
    routes = []
    for first, second in pairs(doms, distance, offset):
        if second - first == distance:
            for t in range(tps):
                ends = (first * tps + t, second * tps + t)
                routes += [ends, ends[::-1]]
    return routes


def partner(me, doms, distance, offset):
    step = jnp.where(is_first(me, distance, offset), distance, doms - distance)
    return (me + step) % doms


def in_hbm(x):
    return pltpu.with_memory_space_constraint(x, pltpu.HBM)


def place_new_rows(cache, new_rows, length, slot, per_dev):
    rows, width = cache.shape
    first = pl.multiple_of(
        jnp.minimum(length // ROW_TILE * ROW_TILE, rows - WINDOW), ROW_TILE
    )
    row_ids = first + lax.broadcasted_iota(jnp.int32, (WINDOW, width), 0)
    old = cache[pl.ds(first, WINDOW), :].astype(jnp.float32)
    later = jnp.where(row_ids == length + 1, new_rows[pl.ds(per_dev + slot, 1), :], 0.0)
    later = jnp.where(row_ids == length, new_rows[pl.ds(slot, 1), :], later)
    cache[pl.ds(first, WINDOW), :] = jnp.where(row_ids < length, old, later).astype(
        jnp.bfloat16
    )

    def clear(tile, carry):
        start = pl.multiple_of(tile * ROW_TILE, ROW_TILE)
        cache[pl.ds(start, ROW_TILE), :] = jnp.zeros((ROW_TILE, width), jnp.bfloat16)
        return carry

    lax.fori_loop(first // ROW_TILE + WINDOW // ROW_TILE, rows // ROW_TILE, clear, 0)


def named_range(anc_ref, first, owner, per_dev):
    low, high = jnp.int32(per_dev), jnp.int32(-1)
    for j in range(per_dev):
        local = anc_ref[first + j] - owner * per_dev
        named = jnp.logical_and(local >= 0, local < per_dev)
        low = jnp.minimum(low, jnp.where(named, local, per_dev))
        high = jnp.maximum(high, jnp.where(named, local, -1))
    return low, high


def pack_kernel(per_dev, doms, len_hbm, anc_hbm, new_hbm, gen_hbm, *refs):
    sends = refs[: len(ROUNDS)]
    table_hbm, table, len_ref, anc_ref, new_bf16, new_rows, list_sem, load_sem = refs[
        len(ROUNDS) :
    ]
    new_at, own_at, anc_at, slot_at = (k * per_dev for k in range(TABLE_PARTS))
    lists = [
        pltpu.make_async_copy(anc_hbm, anc_ref, list_sem.at[0]),
        pltpu.make_async_copy(len_hbm, len_ref, list_sem.at[1]),
        pltpu.make_async_copy(new_hbm, new_bf16, list_sem.at[2]),
    ]
    for copy in lists:
        copy.start()
    me = lax.axis_index("dom")
    lists[0].wait()
    picks = []
    loads = []
    for k, pairing in enumerate(ROUNDS):
        reader = partner(me, doms, *pairing)
        low, high = named_range(anc_ref, reader * per_dev, me, per_dev)
        for i, pick in enumerate((jnp.minimum(low, per_dev - 1), jnp.maximum(high, 0))):
            target = sends[k].at[i]
            load = pltpu.make_async_copy(gen_hbm.at[pick], target, load_sem.at[len(loads)])
            load.start()
            picks.append((pick, target))
            loads.append(load)
    lists[1].wait()
    for j in range(per_dev):
        table[anc_at + j] = anc_ref[me * per_dev + j]
        table[new_at + j] = len_ref[anc_ref[me * per_dev + j]] + 2
        table[own_at + j] = len_ref[me * per_dev + j]
        table[slot_at + j] = -PICKS
    for k, pairing in enumerate(ROUNDS):
        source = partner(me, doms, *pairing)
        low, _ = named_range(anc_ref, me * per_dev, source, per_dev)
        for j in range(per_dev):
            local = anc_ref[me * per_dev + j] - source * per_dev
            named = jnp.logical_and(local >= 0, local < per_dev)
            slot = k * PICKS + jnp.where(local == low, 0, PICKS - 1)
            table[slot_at + j] = jnp.where(named, slot, table[slot_at + j])
    table_copy = pltpu.make_async_copy(table, table_hbm, list_sem.at[3])
    table_copy.start()
    lists[2].wait()
    new_rows[...] = new_bf16[...].astype(jnp.float32).reshape(new_rows.shape)
    for load, (pick, target) in zip(loads, picks):
        load.wait()
        place_new_rows(target, new_rows, len_ref[me * per_dev + pick], pick, per_dev)
    table_copy.wait()


def pack(lengths, ancestors, new_kv, gen_cache, doms):
    per_dev, rows, width = gen_cache.shape
    count = len(ROUNDS)
    vmem = pl.BlockSpec(memory_space=pltpu.VMEM)
    hbm = pl.BlockSpec(memory_space=pltpu.HBM)
    block_bytes = PICKS * rows * width * 2
    return pl.pallas_call(
        functools.partial(pack_kernel, per_dev, doms),
        out_shape=[jax.ShapeDtypeStruct((PICKS, rows, width), jnp.bfloat16)] * count
        + [jax.ShapeDtypeStruct((TABLE_PARTS * per_dev,), jnp.int32)],
        in_specs=[hbm] * 4,
        out_specs=[vmem] * count + [hbm],
        scratch_shapes=[
            pltpu.SMEM((TABLE_PARTS * per_dev,), jnp.int32),
            pltpu.SMEM(lengths.shape, jnp.int32),
            pltpu.SMEM(ancestors.shape, jnp.int32),
            pltpu.VMEM(new_kv.shape, jnp.bfloat16),
            pltpu.VMEM((2 * per_dev, width), jnp.float32),
            pltpu.SemaphoreType.DMA((4,)),
            pltpu.SemaphoreType.DMA((count * PICKS,)),
        ],
        compiler_params=pltpu.CompilerParams(vmem_limit_bytes=VMEM_BYTES),
        cost_estimate=pl.CostEstimate(
            flops=0, bytes_accessed=2 * count * block_bytes, transcendentals=0
        ),
        name="pack_sends",
    )(*(in_hbm(x) for x in (lengths, ancestors, new_kv, gen_cache)))


def fold_lanes(block, combine, start):
    for first in range(0, block.shape[1], HEAD_DIM):
        start = combine(start, block[:, first : first + HEAD_DIM])
    return start


def attend_kernel(
    per_dev,
    group,
    kv_local,
    chunk,
    table_hbm,
    q_ref,
    prompt_hbm,
    gen_hbm,
    token_hbm,
    bias_hbm,
    new_ref,
    head_ref,
    prior_ref,
    share_ref,
    out_hbm,
    prompt,
    grown,
    new_rows,
    scores,
    tops,
    totals,
    mixed_ref,
    bias_rows,
    extra,
    table,
    token_ref,
    prompt_sem,
    gen_sem,
    out_sem,
    bias_sem,
    list_sem,
):
    me = lax.axis_index("dom")
    steps = q_ref.shape[0]
    rows, width = grown.shape[1:]
    chunks = prompt.shape[0] // chunk
    pair = 2 * HEAD_DIM
    scale = LOG2_E / math.sqrt(HEAD_DIM)
    base = steps * per_dev

    half = per_dev // 2
    per_chunk = per_dev // chunks

    def gen_load(p):
        return pltpu.make_async_copy(gen_hbm.at[p], grown.at[p], gen_sem.at[p])

    def prompt_load(j):
        part = pl.ds(pl.multiple_of(j * chunk, chunk), chunk)
        return pltpu.make_async_copy(prompt_hbm.at[part], prompt.at[part], prompt_sem.at[j])

    lists = [
        pltpu.make_async_copy(table_hbm, table, list_sem.at[0]),
        pltpu.make_async_copy(token_hbm, token_ref, list_sem.at[1]),
    ]
    for copy in lists:
        copy.start()
    def start_loads(j):
        prompt_load(j).start()
        for i in range(per_chunk):
            gen_load(j * per_chunk + i).start()

    for j in range(AHEAD):
        start_loads(j)

    for copy in lists:
        copy.wait()
    len_ref, anc_ref = (table.at[pl.ds(k * per_dev, per_dev)] for k in (1, 2))
    for i in range(base):
        row = token_ref[i // per_dev, i % per_dev] // HEAD_DIM
        pltpu.make_async_copy(bias_hbm.at[pl.ds(pl.multiple_of(row * HEAD_DIM, HEAD_DIM), HEAD_DIM)], bias_rows.at[i, 0], bias_sem.at[i]).start()

    new_rows[...] = new_ref[...].astype(jnp.float32).reshape(base, width)
    row_ids = lax.broadcasted_iota(jnp.int32, (rows, width), 0)

    def patch(p):
        gen_load(p).wait()
        behind = row_ids - len_ref[p]
        tail = jnp.where(behind == 1, new_rows[pl.ds(per_dev + p, 1), :], 0.0)
        tail = jnp.where(behind == 0, new_rows[pl.ds(p, 1), :], tail)
        grown[p] = jnp.where(behind < 0, grown[p].astype(jnp.float32), tail).astype(
            jnp.bfloat16
        )

    q2 = q_ref[...].reshape(base, q_ref.shape[-1])
    queries = [
        jnp.concatenate(
            [q2[:, h * HEAD_DIM : (h + 1) * HEAD_DIM] for h in range(c * group, (c + 1) * group)],
            axis=0,
        )
        for c in range(kv_local)
    ]

    def score(query_rows, keys):
        return lax.dot_general(
            query_rows, keys, (((1,), (1,)), ((), ())), preferred_element_type=jnp.float32
        )

    def mix(probs, values):
        return jnp.dot(probs, values, preferred_element_type=jnp.float32)

    tops[...] = jnp.full(tops.shape, NEG_FILL, jnp.float32)

    def score_chunk(j, carry):
        prompt_load(j).wait()
        pl.when(j + AHEAD < chunks)(functools.partial(start_loads, j + AHEAD))
        part = pl.ds(pl.multiple_of(j * chunk, chunk), chunk)
        for c in range(kv_local):
            block = score(queries[c], prompt[part, c * pair : c * pair + HEAD_DIM])
            scores[c, j] = block
            tops[c] = fold_lanes(block, jnp.maximum, tops[c])
        for i in range(per_chunk):
            patch(j * per_chunk + i)
        return carry

    lax.fori_loop(0, chunks, score_chunk, 0)

    homes = []
    for p in range(per_dev):
        local = anc_ref[p] - me * per_dev
        home = jnp.logical_and(local >= 0, local < per_dev)
        source = grown.at[jnp.clip(local, 0, per_dev - 1)]
        copy = pltpu.make_async_copy(source, out_hbm.at[p], out_sem.at[p])
        homes.append((home, copy))
        pl.when(home)(copy.start)

    row_ids = lax.broadcasted_iota(jnp.int32, (base, rows), 0)
    owner = row_ids % per_dev
    last = row_ids // per_dev
    for p in range(per_dev):
        last = last + jnp.where(owner == p, len_ref[p], 0)
    visible = lax.broadcasted_iota(jnp.int32, (base, rows), 1) <= last
    visible, lower, seat = (
        jnp.concatenate([part.astype(jnp.int32)] * group, axis=0)
        for part in (visible, owner < half, owner % half)
    )
    visible, lower = visible == 1, lower == 1

    def halves(block):
        block = block.astype(jnp.float32)
        parts = [jnp.where(lower, block, 0.0), jnp.where(lower, 0.0, block)]
        return jnp.concatenate(parts, axis=1).astype(jnp.bfloat16)

    def by_seat(blocks):
        chosen = blocks[:, :HEAD_DIM]
        for i in range(1, half):
            chosen = jnp.where(seat == i, blocks[:, i * HEAD_DIM : (i + 1) * HEAD_DIM], chosen)
        return chosen

    for c in range(kv_local):
        columns = slice(c * pair, c * pair + HEAD_DIM)
        keys = jnp.concatenate(
            [
                jnp.concatenate([grown[i, :, columns], grown[i + half, :, columns]], axis=1)
                for i in range(half)
            ],
            axis=0,
        )
        own = jnp.where(visible, by_seat(score(halves(queries[c]), keys)), NEG_FILL)
        top = jnp.max(jnp.maximum(tops[c], own), axis=1, keepdims=True)
        top = jnp.broadcast_to(top, own.shape)
        tops[c] = top
        exps = jnp.where(visible, jnp.exp2((own - top) * scale), 0.0)
        totals[c] = exps
        columns = slice(c * pair + HEAD_DIM, (c + 1) * pair)
        values = jnp.concatenate(
            [
                jnp.concatenate([grown[i, :, columns], grown[i + half, :, columns]], axis=0)
                for i in range(half)
            ],
            axis=1,
        )
        mixed_ref[c] = by_seat(mix(halves(exps), values))

    def mix_chunks(step, carry):
        for c in range(kv_local):
            top = jnp.concatenate([tops[c]] * (chunk // HEAD_DIM), axis=1)
            total, mixed = totals[c], mixed_ref[c]
            for i in range(AHEAD):
                j = step * AHEAD + i
                part = pl.ds(pl.multiple_of(j * chunk, chunk), chunk)
                exps = jnp.exp2((scores[c, j] - top) * scale)
                total = fold_lanes(exps, jnp.add, total)
                mixed = mixed + mix(
                    exps.astype(jnp.bfloat16), prompt[part, c * pair + HEAD_DIM : (c + 1) * pair]
                )
            totals[c] = total
            mixed_ref[c] = mixed
        return carry

    lax.fori_loop(0, chunks // AHEAD, mix_chunks, 0)
    weighted = jnp.zeros((base, HEAD_DIM), jnp.float32)
    for c in range(kv_local):
        mixed = mixed_ref[c] / jnp.sum(totals[c], axis=1, keepdims=True)
        for h in range(group):
            weighted = (
                weighted + mixed[h * base : (h + 1) * base] * head_ref[c * group + h][None, :]
            )
    row_ids = lax.broadcasted_iota(jnp.int32, (base, HEAD_DIM), 0)
    column = jnp.full((base, HEAD_DIM), -1, jnp.int32)
    for i in range(base):
        pltpu.make_async_copy(bias_hbm.at[pl.ds(0, HEAD_DIM)], bias_rows.at[i, 0], bias_sem.at[i]).wait()
        column = jnp.where(row_ids == i, token_ref[i // per_dev, i % per_dev] % HEAD_DIM, column)
    adds = lax.axis_index("tp") == 0
    lane_ids = lax.broadcasted_iota(jnp.int32, (base, HEAD_DIM), 1)
    bias = jnp.where(lane_ids == column, bias_rows[...].reshape(base, HEAD_DIM), 0.0)
    weighted = weighted + jnp.where(adds, bias, 0.0)
    extra[...] = jnp.zeros(extra.shape, jnp.float32)
    extra[:, base : base + per_dev] = jnp.where(adds, prior_ref[...], 0.0)
    padding = jnp.zeros((HEAD_DIM - base, HEAD_DIM), jnp.float32)
    square = jnp.concatenate([weighted, padding], axis=0)
    row = jnp.sum(square.T, axis=0, keepdims=True) + extra[...]
    share_ref[...] = jnp.broadcast_to(row[None], share_ref.shape)
    for home, copy in homes:
        pl.when(home)(copy.wait)


def attend(
    table,
    queries,
    prompt_kv,
    gen_cache,
    tokens,
    twist_bias,
    new_kv,
    twist_vector,
    prior_weights,
    devices,
):
    steps, per_dev, width = queries.shape
    keys, kv_width = prompt_kv.shape
    rows = gen_cache.shape[1]
    kv_local = kv_width // (2 * HEAD_DIM)
    group = width // (kv_local * HEAD_DIM)
    score_rows = steps * per_dev * group
    chunk = min(KEY_CHUNK, keys)
    head_weights = twist_vector.reshape(kv_local * group, HEAD_DIM)
    vmem = pl.BlockSpec(memory_space=pltpu.VMEM)
    hbm = pl.BlockSpec(memory_space=pltpu.HBM)
    score_count = score_rows * kv_local * (keys + rows)
    return pl.pallas_call(
        functools.partial(attend_kernel, per_dev, group, kv_local, chunk),
        out_shape=[
            jax.ShapeDtypeStruct((devices, 1, HEAD_DIM), jnp.float32),
            jax.ShapeDtypeStruct(gen_cache.shape, jnp.bfloat16),
        ],
        in_specs=[hbm, vmem, hbm, hbm, hbm, hbm, vmem, vmem, vmem],
        out_specs=[vmem, hbm],
        scratch_shapes=[
            pltpu.VMEM(prompt_kv.shape, jnp.bfloat16),
            pltpu.VMEM(gen_cache.shape, jnp.bfloat16),
            pltpu.VMEM((steps * per_dev, kv_width), jnp.float32),
            pltpu.VMEM((kv_local, keys // chunk, score_rows, chunk), jnp.float32),
            pltpu.VMEM((kv_local, score_rows, HEAD_DIM), jnp.float32),
            pltpu.VMEM((kv_local, score_rows, HEAD_DIM), jnp.float32),
            pltpu.VMEM((kv_local, score_rows, HEAD_DIM), jnp.float32),
            pltpu.VMEM((steps * per_dev, 1, HEAD_DIM), jnp.float32),
            pltpu.VMEM((1, HEAD_DIM), jnp.float32),
            pltpu.SMEM(table.shape, jnp.int32),
            pltpu.SMEM(tokens.shape, jnp.int32),
            pltpu.SemaphoreType.DMA((keys // chunk,)),
            pltpu.SemaphoreType.DMA((per_dev,)),
            pltpu.SemaphoreType.DMA((per_dev,)),
            pltpu.SemaphoreType.DMA((steps * per_dev,)),
            pltpu.SemaphoreType.DMA((2,)),
        ],
        compiler_params=pltpu.CompilerParams(vmem_limit_bytes=VMEM_BYTES),
        cost_estimate=pl.CostEstimate(
            flops=4 * score_count * HEAD_DIM,
            bytes_accessed=2 * (prompt_kv.size + 2 * gen_cache.size),
            transcendentals=score_count,
        ),
        name="attend",
    )(
        in_hbm(table),
        queries,
        in_hbm(prompt_kv),
        in_hbm(gen_cache),
        in_hbm(tokens),
        in_hbm(twist_bias),
        new_kv,
        head_weights,
        prior_weights[None],
    )


def finish_kernel(doms, tps, table_ref, *refs):
    gots = refs[: len(ROUNDS)]
    _, all_ref, out_ref, twist_hbm, normal_hbm = refs[len(gots) : len(gots) + 5]
    table, sums, twist, normal, copy_sem, small_sem = refs[len(gots) + 5 :]
    per_dev = out_ref.shape[0]
    table_copy = pltpu.make_async_copy(table_ref, table, small_sem.at[0])
    table_copy.start()
    table_copy.wait()
    slots = [table[(TABLE_PARTS - 1) * per_dev + p] for p in range(per_dev)]
    for p, slot in enumerate(slots):
        for k, got in enumerate(gots):
            copy = pltpu.make_async_copy(got.at[slot % PICKS], out_ref.at[p], copy_sem.at[p])
            pl.when(slot // PICKS == k)(copy.start)
    for d in range(doms):
        row = all_ref[d * tps]
        for t in range(1, tps):
            row = row + all_ref[d * tps + t]
        sums[d : d + 1, :] = row
    step_0, step_1, prior = (
        slice(k * per_dev, (k + 1) * per_dev) for k in range(3)
    )
    totals = sums[...]
    log_weights = totals[:, prior] + totals[:, step_1] - totals[:, step_0]
    largest = jnp.max(log_weights, keepdims=True)
    log_total = largest + jnp.log(jnp.sum(jnp.exp(log_weights - largest), keepdims=True))
    mine = sums[pl.ds(lax.axis_index("dom"), 1), :]
    own = mine[:, prior] + mine[:, step_1] - mine[:, step_0]
    twist[...] = jnp.concatenate([mine[:, step_0], mine[:, step_1]], axis=0)
    normal[...] = own - log_total
    results = [
        pltpu.make_async_copy(twist, twist_hbm, small_sem.at[1]),
        pltpu.make_async_copy(normal, normal_hbm, small_sem.at[2]),
    ]
    for copy in results:
        copy.start()
    for p, slot in enumerate(slots):
        copy = pltpu.make_async_copy(gots[0].at[0], out_ref.at[p], copy_sem.at[p])
        pl.when(slot >= 0)(copy.wait)
    for copy in results:
        copy.wait()


def finish(table, gots, held, shares, doms, tps):
    per_dev = held.shape[0]
    count = len(gots)
    vmem = pl.BlockSpec(memory_space=pltpu.VMEM)
    hbm = pl.BlockSpec(memory_space=pl.ANY)
    return pl.pallas_call(
        functools.partial(finish_kernel, doms, tps),
        out_shape=[
            jax.ShapeDtypeStruct(held.shape, held.dtype),
            jax.ShapeDtypeStruct((2, per_dev), jnp.float32),
            jax.ShapeDtypeStruct((1, per_dev), jnp.float32),
        ],
        in_specs=[vmem] + [vmem] * count + [hbm, vmem],
        out_specs=[hbm, hbm, hbm],
        input_output_aliases={1 + count: 0},
        scratch_shapes=[
            pltpu.SMEM(table.shape, jnp.int32),
            pltpu.VMEM((doms, HEAD_DIM), jnp.float32),
            pltpu.VMEM((2, per_dev), jnp.float32),
            pltpu.VMEM((1, per_dev), jnp.float32),
            pltpu.SemaphoreType.DMA((per_dev,)),
            pltpu.SemaphoreType.DMA((3,)),
        ],
        compiler_params=pltpu.CompilerParams(vmem_limit_bytes=VMEM_BYTES),
        cost_estimate=pl.CostEstimate(
            flops=0, bytes_accessed=held.size, transcendentals=0
        ),
        name="finish",
    )(table, *gots, held, shares)


def local(
    queries,
    new_kv,
    gen_cache,
    prompt_kv,
    lengths,
    ancestors,
    tokens,
    twist_vector,
    twist_bias,
    prior_weights,
):
    doms, tps = lax.axis_size("dom"), lax.axis_size("tp")
    per_dev = gen_cache.shape[0]
    everyone = ("dom", "tp")

    *sends, table = pack(lengths, ancestors, new_kv, gen_cache, doms)
    arrivals = [
        lax.ppermute(send, everyone, swaps(doms, tps, *pairing))
        for send, pairing in zip(sends, ROUNDS)
    ]

    shares, resampled = attend(
        table,
        queries,
        prompt_kv,
        gen_cache,
        tokens,
        twist_bias,
        new_kv,
        twist_vector,
        prior_weights,
        doms * tps,
    )
    shares = lax.all_to_all(shares, everyone, 0, 0, tiled=True)
    resampled, twist, normalized = finish(table, arrivals, resampled, shares, doms, tps)
    return (twist, normalized.reshape(per_dev), resampled, table[:per_dev])


def solution(mesh):
    in_specs = (
        P(None, "dom", "tp"),
        P(None, "dom", "tp"),
        P("dom", None, "tp"),
        P(None, "tp"),
        P(),
        P(),
        P(None, "dom"),
        P("tp"),
        P(),
        P("dom"),
    )
    out_specs = (P(None, "dom"), P("dom"), P("dom", None, "tp"), P("dom"))
    return jax.shard_map(local, mesh=mesh, in_specs=in_specs, out_specs=out_specs, check_vma=False)
```
